32 devices in a mesh: dp: 8 (over z, x), group: 4 (over y, core).
Axes of the slice: x: 2, y: 2, z: 4, core: 2. Of those that a mesh axis runs over, the one named last changes fastest.
Arguments:
- slow_in: bfloat16 [4, 64, 14, 14, 1024], P('group', 'dp'), may hold values from -6 to 6
- fast_in: bfloat16 [4, 256, 14, 14, 128], P('group', 'dp'), may hold values from -6 to 6
- slow_cotangent: bfloat16 [4, 64, 14, 14, 1024], P('group', 'dp'), may hold values from -6 to 6
- fast_cotangent: bfloat16 [4, 256, 14, 14, 128], P('group', 'dp'), may hold values from -6 to 6
- clip_start: int32 [4, 9], P('group'), may hold values from 0 to 64, as said below
- clip_end: int32 [4, 9], P('group'), may hold values from 4 to 64, as said below
- slow_reduce: float32 [3, 1024, 256], replicated, may hold values from -0.109375 to 0.109375
- slow_spatial: float32 [9, 256, 256], replicated, may hold values from -0.125 to 0.125
- slow_expand: float32 [256, 1024], replicated, may hold values from -0.375 to 0.375
- lateral: float32 [5, 128, 256], replicated, may hold values from -0.25 to 0.25
- fast_reduce: float32 [3, 128, 32], replicated, may hold values from -0.3125 to 0.3125
- fast_spatial: float32 [9, 32, 32], replicated, may hold values from -0.375 to 0.375
- fast_expand: float32 [32, 128], replicated, may hold values from -1 to 1
- slow_reduce_moment: float32 [3, 1024, 256], replicated, may hold values from -384 to 384
- slow_spatial_moment: float32 [9, 256, 256], replicated, may hold values from -384 to 384
- slow_expand_moment: float32 [256, 1024], replicated, may hold values from -384 to 384
- lateral_moment: float32 [5, 128, 256], replicated, may hold values from -384 to 384
- fast_reduce_moment: float32 [3, 128, 32], replicated, may hold values from -384 to 384
- fast_spatial_moment: float32 [9, 32, 32], replicated, may hold values from -384 to 384
- fast_expand_moment: float32 [32, 128], replicated, may hold values from -384 to 384
- norm_params: float32 [2, 1728], replicated, may hold values from -1.2 to 1.6, as said below
- norm_first: float32 [2, 1728], replicated, may hold values from -48 to 48
- norm_second: float32 [2, 1728], replicated, may hold values from 235.8272 to 953.344
Outputs:
- slow_out: bfloat16 [4, 64, 14, 14, 1024], P('group', 'dp')
- fast_out: bfloat16 [4, 256, 14, 14, 128], P('group', 'dp')
- slow_in_grad: float32 [4, 64, 14, 14, 1024], P('group', 'dp')
- fast_in_grad: float32 [4, 256, 14, 14, 128], P('group', 'dp')
- slow_reduce_new: float32 [3, 1024, 256], replicated
- slow_spatial_new: float32 [9, 256, 256], replicated
- slow_expand_new: float32 [256, 1024], replicated
- lateral_new: float32 [5, 128, 256], replicated
- fast_reduce_new: float32 [3, 128, 32], replicated
- fast_spatial_new: float32 [9, 32, 32], replicated
- fast_expand_new: float32 [32, 128], replicated
- slow_reduce_moment_new: float32 [3, 1024, 256], replicated
- slow_spatial_moment_new: float32 [9, 256, 256], replicated
- slow_expand_moment_new: float32 [256, 1024], replicated
- lateral_moment_new: float32 [5, 128, 256], replicated
- fast_reduce_moment_new: float32 [3, 128, 32], replicated
- fast_spatial_moment_new: float32 [9, 32, 32], replicated
- fast_expand_moment_new: float32 [32, 128], replicated
- norm_first_new: float32 [2, 1728], replicated
- norm_second_new: float32 [2, 1728], replicated
- norm_params_new: float32 [2, 1728], replicated
The draws below stay inside these ranges and needn't reach their ends.
Inputs may be any that keep to these rules, and one draw needn't show every extreme that they name: `clip_start`: row g holds the first frames of stream g's clips in rising order, the first being 0; unused slots hold 64. Every other start lies at 4 plus a multiple of 8. The clips of the last stream cover all its frames. clip_end[g,c] is where the clip that starts at clip_start[g,c] ends (exclusive): the next clip's start, or the end of the stream's clipped frames, which also lies at 4 plus a multiple of 8 or at 64; unused slots hold 64. Frames in no clip are padding. The first clip of stream 0 ends at 4. `norm_params`: row 0 the gains, row 1 the biases.
All inputs are finite; a program needn't handle non-finite values.
Results may differ from the reference program's by a relative error of at most 0.0095.
Values may be sent and summed in bfloat16 or wider, within the bound.
A program may use at most 256 MiB of HBM per device.

```python
import math
import jax
import jax.numpy as jnp
from jax import lax

CS = 1024
CM = 256
CF = 128
FM = 32
SIDE = 14
SF = 8
NS_STEPS = 5
STEP = 10
STREAMS = 4
TF = 64
NBN = 1728
VOXELS = 50176
N_DP = 8


def clip_layout(key):
    count = TF // SF
    streams = jnp.arange(STREAMS, dtype=jnp.int32)
    lower = jnp.maximum(1, streams * count // STREAMS)
    upper = jnp.maximum(lower + 1, (streams + 1) * count // STREAMS)
    chosen = jax.random.randint(jax.random.fold_in(key, 101), (STREAMS,), lower, upper)
    limit = jnp.where(streams == STREAMS - 1, TF, chosen * SF + SF // 2)
    flags = jax.random.randint(jax.random.fold_in(key, 102), (STREAMS, count), 0, 2)
    flags = flags.at[0, 0].set(1)
    places = SF // 2 + SF * jnp.arange(count, dtype=jnp.int32)
    kept = (flags == 1) & (places[None, :] < limit[:, None])
    raw = jnp.where(kept, places[None, :], TF)
    starts = jnp.sort(jnp.concatenate([jnp.zeros((STREAMS, 1), jnp.int32), raw.astype(jnp.int32)], axis=1), axis=1)
    following = jnp.concatenate([starts[:, 1:], jnp.full((STREAMS, 1), TF, jnp.int32)], axis=1)
    ends = jnp.where(starts < TF, jnp.minimum(following, limit[:, None]), TF)
    return (starts.astype(jnp.int32), ends.astype(jnp.int32))


def draw_clip_start(key, part):
    return clip_layout(key)[0]


def draw_clip_end(key, part):
    return clip_layout(key)[1]


def draw_norm_params(key, part):
    key = jax.random.fold_in(key, 7)
    gains = 1.0 + 0.15 * jnp.clip(jax.random.normal(jax.random.fold_in(key, 1), (NBN,), jnp.float32), -4.0, 4.0)
    biases = 0.3 * jnp.clip(jax.random.normal(jax.random.fold_in(key, 2), (NBN,), jnp.float32), -4.0, 4.0)
    return jnp.stack([gains, biases])


def steps_of(key, dims, shards, least, largest):
    level, own = 1.0, jax.random.fold_in(key, 6)
    for dim, parts in shards:
        draws = jnp.exp(jax.random.uniform(jax.random.fold_in(own, dim), (parts,), jnp.float32, least / len(shards), largest / len(shards)))
        level = level * jnp.repeat(draws, dims[dim] // parts).reshape([-1 if axis == dim else 1 for axis in range(len(dims))])
    return level


def centred(own_key, shape, deviation, bound, cuts=(), kind=jnp.bfloat16):
    level = steps_of(own_key, shape, cuts, -0.22, 0.18) if cuts else 1.0
    array = jax.random.normal(own_key, shape, jnp.float32) * deviation * level
    return jnp.minimum(jnp.maximum(array, -bound), bound).astype(kind)


def setup_inputs(seed: int = 0) -> dict:
    keys = jax.random.split(jax.random.key(seed), 24)
    slow_in = centred(keys[0], (STREAMS, TF, SIDE, SIDE, CS), 1.0, 6.0, ((0, 4), (1, 8)))
    fast_in = centred(keys[1], (STREAMS, 4 * TF, SIDE, SIDE, CF), 1.0, 6.0, ((0, 4), (1, 8)))
    slow_cotangent = centred(keys[2], (STREAMS, TF, SIDE, SIDE, CS), 1.0, 6.0, ((0, 4), (1, 8)))
    fast_cotangent = centred(keys[3], (STREAMS, 4 * TF, SIDE, SIDE, CF), 1.0, 6.0, ((0, 4), (1, 8)))
    clip_start = draw_clip_start(jax.random.fold_in(keys[23], 71), 0)
    clip_end = draw_clip_end(jax.random.fold_in(keys[23], 71), 0)
    slow_reduce = centred(keys[6], (3, CS, CM), (3 * CS) ** -0.5, 0.109375, (), jnp.float32)
    slow_spatial = centred(keys[7], (9, CM, CM), (9 * CM) ** -0.5, 0.125, (), jnp.float32)
    slow_expand = centred(keys[8], (CM, CS), CM ** -0.5, 0.375, (), jnp.float32)
    lateral = centred(keys[9], (5, CF, CM), (5 * CF) ** -0.5, 0.25, (), jnp.float32)
    fast_reduce = centred(keys[10], (3, CF, FM), (3 * CF) ** -0.5, 0.3125, (), jnp.float32)
    fast_spatial = centred(keys[11], (9, FM, FM), (9 * FM) ** -0.5, 0.375, (), jnp.float32)
    fast_expand = centred(keys[12], (FM, CF), FM ** -0.5, 1.0, (), jnp.float32)
    slow_reduce_moment = centred(keys[13], (3, CS, CM), (0.3 * VOXELS ** 0.5), 384.0, (), jnp.float32)
    slow_spatial_moment = centred(keys[14], (9, CM, CM), (0.3 * VOXELS ** 0.5), 384.0, (), jnp.float32)
    slow_expand_moment = centred(keys[15], (CM, CS), (0.3 * VOXELS ** 0.5), 384.0, (), jnp.float32)
    lateral_moment = centred(keys[16], (5, CF, CM), (0.3 * VOXELS ** 0.5), 384.0, (), jnp.float32)
    fast_reduce_moment = centred(keys[17], (3, CF, FM), (0.3 * VOXELS ** 0.5), 384.0, (), jnp.float32)
    fast_spatial_moment = centred(keys[18], (9, FM, FM), (0.3 * VOXELS ** 0.5), 384.0, (), jnp.float32)
    fast_expand_moment = centred(keys[19], (FM, CF), (0.3 * VOXELS ** 0.5), 384.0, (), jnp.float32)
    norm_params = draw_norm_params(jax.random.fold_in(keys[23], 71), 0)
    norm_first = centred(keys[21], (2, NBN), (0.033 * VOXELS ** 0.5), 48.0, (), jnp.float32)
    norm_second = jnp.clip(jnp.exp(jax.random.uniform(keys[22], (2, NBN), jnp.float32, math.log(235.8272), math.log(953.344))), 235.8272, 953.344)
    return dict(slow_in=slow_in, fast_in=fast_in, slow_cotangent=slow_cotangent, fast_cotangent=fast_cotangent, clip_start=clip_start, clip_end=clip_end, slow_reduce=slow_reduce, slow_spatial=slow_spatial, slow_expand=slow_expand, lateral=lateral, fast_reduce=fast_reduce, fast_spatial=fast_spatial, fast_expand=fast_expand, slow_reduce_moment=slow_reduce_moment, slow_spatial_moment=slow_spatial_moment, slow_expand_moment=slow_expand_moment, lateral_moment=lateral_moment, fast_reduce_moment=fast_reduce_moment, fast_spatial_moment=fast_spatial_moment, fast_expand_moment=fast_expand_moment, norm_params=norm_params, norm_first=norm_first, norm_second=norm_second)


EPS = 1e-05
MU = 0.95
LR = 0.3
BETA_ONE = 0.9
BETA_TWO = 0.95
LR_NORM = 0.2
ADAM_EPS = 1e-08
NS_A = 3.4445
NS_B = -4.775
NS_C = 2.0315
HIGH = lax.Precision.HIGHEST

@jax.custom_vjp
def low(v):
    return lax.optimization_barrier(v.astype(jnp.bfloat16)).astype(jnp.float32)

@jax.custom_vjp
def low_back(v):
    return v

def low_keep(v):
    return (low(v), None)

def low_pass(kept, grad):
    return (grad,)

def back_keep(v):
    return (v, None)

def back_low(kept, grad):
    return (low(grad),)
low.defvjp(low_keep, low_pass)
low_back.defvjp(back_keep, back_low)

def neighbour(values, offset, fill):
    padded = jnp.pad(values, ((0, 0), (2, 2)), constant_values=fill)
    return padded[:, 2 + offset:2 + offset + values.shape[1]]

def linked(valid_one, segment_one, valid_two, segment_two):
    return (valid_one & valid_two & (segment_one == segment_two)).astype(jnp.float32)

def frame_masks(clip_start, clip_end):
    frames = jnp.arange(TF, dtype=jnp.int32)
    begun = clip_start[:, None, :] <= frames[None, :, None]
    inside = begun & (frames[None, :, None] < clip_end[:, None, :])
    return (jnp.any(inside, axis=2), lax.optimization_barrier(jnp.sum(begun.astype(jnp.int32), axis=2)))

def temporal_conv(values, weight, links):
    count = values.shape[1]
    padded = jnp.pad(values, ((0, 0), (1, 1), (0, 0), (0, 0), (0, 0)))
    total = jnp.zeros(values.shape[:4] + (weight.shape[2],), jnp.float32)
    for tap in range(3):
        product = jnp.einsum('sfhwc,cd->sfhwd', padded[:, tap:tap + count], weight[tap], precision=HIGH)
        total = total + links[tap][:, :, None, None, None] * product
    return total

def lateral_conv(fast_values, weight, links):
    padded = jnp.pad(fast_values, ((0, 0), (2, 2), (0, 0), (0, 0), (0, 0)))
    total = jnp.zeros((STREAMS, TF, SIDE, SIDE, weight.shape[2]), jnp.float32)
    for tap in range(5):
        product = jnp.einsum('sfhwc,cd->sfhwd', padded[:, tap:tap + 4 * TF:4], weight[tap], precision=HIGH)
        total = total + links[tap][:, :, None, None, None] * product
    return total

def spatial_conv(values, weight):
    padded = jnp.pad(values, ((0, 0), (0, 0), (1, 1), (1, 1), (0, 0)))
    total = jnp.zeros(values.shape[:4] + (weight.shape[2],), jnp.float32)
    for vertical in range(3):
        for horizontal in range(3):
            patch = padded[:, :, vertical:vertical + SIDE, horizontal:horizontal + SIDE]
            total = total + jnp.einsum('sfhwc,cd->sfhwd', patch, weight[3 * vertical + horizontal], precision=HIGH)
    return total

def batch_norm(values, valid, gain, bias):
    streams, count_frames = valid.shape
    window = count_frames // N_DP
    width = values.shape[-1]
    grid = values.reshape(streams, N_DP, window, SIDE, SIDE, width)
    weights = valid.astype(jnp.float32).reshape(streams, N_DP, window, 1, 1, 1)
    count = lax.optimization_barrier(jnp.sum(weights, axis=(0, 2, 3, 4, 5))) * (SIDE * SIDE)
    total = lax.optimization_barrier(jnp.sum(grid * weights, axis=(0, 2, 3, 4)))
    squares = lax.optimization_barrier(jnp.sum(grid * grid * weights, axis=(0, 2, 3, 4)))
    mean = total / count[:, None]
    variance = squares / count[:, None] - mean * mean
    inverse = lax.rsqrt(variance + EPS)
    scaled = (grid - mean[None, :, None, None, None, :]) * inverse[None, :, None, None, None, :]
    return (gain * scaled + bias).reshape(values.shape)

def orthogonal(matrix):
    current = matrix / (jnp.sqrt(jnp.sum(matrix * matrix)) + 1e-07)
    rows, cols = current.shape
    for repeat in range(NS_STEPS):
        if rows >= cols:
            gram_matrix = jnp.dot(current.T, current, precision=HIGH)
            polynomial = NS_B * gram_matrix + NS_C * jnp.dot(gram_matrix, gram_matrix, precision=HIGH)
            current = NS_A * current + jnp.dot(current, polynomial, precision=HIGH)
        else:
            gram_matrix = jnp.dot(current, current.T, precision=HIGH)
            polynomial = NS_B * gram_matrix + NS_C * jnp.dot(gram_matrix, gram_matrix, precision=HIGH)
            current = NS_A * current + jnp.dot(polynomial, current, precision=HIGH)
    return current

def muon_step(weight, moment, grad):
    moment_new = MU * moment + grad
    rows = math.prod(weight.shape[:-1])
    cols = weight.shape[-1]
    scale = math.sqrt(max(1.0, cols / rows))
    direction = orthogonal(moment_new.reshape(rows, cols)).reshape(weight.shape)
    return (weight - LR * scale * direction, moment_new)

def adam_step(params, first, second, grad):
    first_new = BETA_ONE * first + (1.0 - BETA_ONE) * grad
    second_new = BETA_TWO * second + (1.0 - BETA_TWO) * grad * grad
    corrected = first_new / (1.0 - BETA_ONE ** STEP)
    params_new = params - LR_NORM * corrected / (jnp.sqrt(second_new / (1.0 - BETA_TWO ** STEP)) + ADAM_EPS)
    return (params_new, first_new, second_new)

def reference(slow_in, fast_in, slow_cotangent, fast_cotangent, clip_start, clip_end, slow_reduce, slow_spatial, slow_expand, lateral, fast_reduce, fast_spatial, fast_expand, slow_reduce_moment, slow_spatial_moment, slow_expand_moment, lateral_moment, fast_reduce_moment, fast_spatial_moment, fast_expand_moment, norm_params, norm_first, norm_second):
    valid, segment = frame_masks(clip_start, clip_end)
    fast_valid = jnp.repeat(valid, 4, axis=1)
    fast_segment = jnp.repeat(segment, 4, axis=1)
    slow_links = [linked(valid, segment, neighbour(valid, offset, False), neighbour(segment, offset, -1)) for offset in (-1, 0, 1)]
    fast_links = [linked(fast_valid, fast_segment, neighbour(fast_valid, offset, False), neighbour(fast_segment, offset, -1)) for offset in (-1, 0, 1)]
    padded_valid = jnp.pad(fast_valid, ((0, 0), (2, 2)), constant_values=False)
    padded_segment = jnp.pad(fast_segment, ((0, 0), (2, 2)), constant_values=-1)
    lateral_links = [linked(valid, segment, padded_valid[:, tap:tap + 4 * TF:4], padded_segment[:, tap:tap + 4 * TF:4]) for tap in range(5)]
    slow_mask = valid.astype(jnp.float32)[:, :, None, None, None]
    fast_mask = fast_valid.astype(jnp.float32)[:, :, None, None, None]
    widths = (CM, CM, CS, FM, FM, CF)
    offsets = [sum(widths[:place]) for place in range(6)]

    def forward(slow_x, fast_x, w_sa, w_sb, w_sc, w_lat, w_fa, w_fb, w_fc, params):
        gains = [params[0, start:start + width] for start, width in zip(offsets, widths)]
        biases = [params[1, start:start + width] for start, width in zip(offsets, widths)]
        slow_one = temporal_conv(slow_x, low(w_sa), slow_links) + lateral_conv(fast_x, low(w_lat), lateral_links)
        slow_one = low_back(slow_one)
        hidden_sa = low(jax.nn.silu(batch_norm(slow_one, valid, gains[0], biases[0])))
        slow_two = low_back(spatial_conv(hidden_sa, low(w_sb)))
        hidden_sb = low(jax.nn.silu(batch_norm(slow_two, valid, gains[1], biases[1])))
        slow_three = low_back(jnp.einsum('sfhwc,cd->sfhwd', hidden_sb, low(w_sc), precision=HIGH))
        slow_total = batch_norm(slow_three, valid, gains[2], biases[2]) + slow_x
        fast_one = low_back(temporal_conv(fast_x, low(w_fa), fast_links))
        hidden_fa = low(jax.nn.silu(batch_norm(fast_one, fast_valid, gains[3], biases[3])))
        fast_two = low_back(spatial_conv(hidden_fa, low(w_fb)))
        hidden_fb = low(jax.nn.silu(batch_norm(fast_two, fast_valid, gains[4], biases[4])))
        fast_three = low_back(jnp.einsum('sfhwc,cd->sfhwd', hidden_fb, low(w_fc), precision=HIGH))
        fast_total = batch_norm(fast_three, fast_valid, gains[5], biases[5]) + fast_x
        return (jax.nn.silu(slow_total) * slow_mask, jax.nn.silu(fast_total) * fast_mask)
    outputs, pullback = jax.vjp(forward, slow_in.astype(jnp.float32), fast_in.astype(jnp.float32), slow_reduce, slow_spatial, slow_expand, lateral, fast_reduce, fast_spatial, fast_expand, norm_params)
    grads = pullback((slow_cotangent.astype(jnp.float32), fast_cotangent.astype(jnp.float32)))
    weights = (slow_reduce, slow_spatial, slow_expand, lateral, fast_reduce, fast_spatial, fast_expand)
    moments = (slow_reduce_moment, slow_spatial_moment, slow_expand_moment, lateral_moment, fast_reduce_moment, fast_spatial_moment, fast_expand_moment)
    new_weights = []
    new_moments = []
    for weight, moment, grad in zip(weights, moments, grads[2:9]):
        weight_new, moment_new = muon_step(weight, moment, grad)
        new_weights.append(weight_new)
        new_moments.append(moment_new)
    params_new, first_new, second_new = adam_step(norm_params, norm_first, norm_second, grads[9])
    return (outputs[0].astype(jnp.bfloat16), outputs[1].astype(jnp.bfloat16), grads[0], grads[1], new_weights[0], new_weights[1], new_weights[2], new_weights[3], new_weights[4], new_weights[5], new_weights[6], new_moments[0], new_moments[1], new_moments[2], new_moments[3], new_moments[4], new_moments[5], new_moments[6], first_new, second_new, params_new)
```

```python
from functools import partial
import math

import jax
import jax.numpy as jnp
from jax import lax
from jax.experimental import pallas as pl
from jax.experimental.pallas import tpu as pltpu
from jax.sharding import PartitionSpec as P

NS_STEPS = 5
STEP = 10


EPS = 1e-05
MU = 0.95
LR = 0.3
BETA_ONE = 0.9
BETA_TWO = 0.95
LR_NORM = 0.2
ADAM_EPS = 1e-08
NS_A = 3.4445
NS_B = -4.775
NS_C = 2.0315
HIGH = lax.Precision.HIGHEST
F32 = jnp.float32
BF = jnp.bfloat16
MESH = pl.DeviceIdType.MESH
ROWS = 7168
PIECES = 2
VMEM_LIMIT = 60 * 2**20
WHOLE = pl.BlockSpec(memory_space=pltpu.VMEM)


def padded_2(cells, sides, width):
    for axis, dim in sides:
        count = lax.axis_size(axis)
        ends = count - 1
        head = lax.slice_in_dim(cells, 0, width, axis=dim)
        tail = lax.slice_in_dim(cells, cells.shape[dim] - width, cells.shape[dim], axis=dim)
        cells = jnp.concatenate(
            [
                lax.ppermute(tail, axis, [(i, (i + 1) % count) for i in range(ends)]),
                cells,
                lax.ppermute(head, axis, [((i + 1) % count, i) for i in range(ends)]),
            ],
            axis=dim,
        )
    return cells


def slope(values):
    sigma = jax.nn.sigmoid(values)
    return sigma * (1.0 + values * (1.0 - sigma))


def pair_mask(valid_one, segment_one, valid_two, segment_two):
    return valid_one & valid_two & (segment_one == segment_two)


def frame_info(starts, ends, first, count):
    frames = first + jnp.arange(count, dtype=jnp.int32)
    begun = starts[None, :] <= frames[:, None]
    inside = begun & (frames[:, None] < ends[None, :])
    return (jnp.any(inside, axis=1), jnp.sum(begun.astype(jnp.int32), axis=1))


def contract_rows(left, right):
    return lax.dot_general(
        left, right, (((0,), (0,)), ((), ())), preferred_element_type=jnp.float32
    )


def contract_cols(left, right):
    return lax.dot_general(
        left, right, (((1,), (1,)), ((), ())), preferred_element_type=jnp.float32
    )


def frame_grid(values, side):
    return jnp.pad(
        values.reshape(-1, side, side, values.shape[-1]), ((0, 0), (1, 1), (1, 1), (0, 0))
    )


def spatial_forward(hidden, weight, side):
    padded = frame_grid(hidden, side)
    total = jnp.zeros((hidden.shape[0], weight.shape[2]), jnp.float32)
    for vertical in range(3):
        for horizontal in range(3):
            patch = padded[:, vertical : vertical + side, horizontal : horizontal + side].reshape(
                -1, hidden.shape[1]
            )
            total = total + jnp.dot(
                patch, weight[3 * vertical + horizontal], preferred_element_type=jnp.float32
            )
    return total


def spatial_backward(hidden, grad, weight, side):
    padded = frame_grid(hidden, side)
    grad_padded = frame_grid(grad, side)
    weight_grads = []
    back = jnp.zeros(hidden.shape, jnp.float32)
    for vertical in range(3):
        for horizontal in range(3):
            patch = padded[:, vertical : vertical + side, horizontal : horizontal + side].reshape(
                -1, hidden.shape[1]
            )
            weight_grads.append(contract_rows(patch, grad))
            moved = grad_padded[
                :, 2 - vertical : 2 - vertical + side, 2 - horizontal : 2 - horizontal + side
            ]
            back = back + contract_cols(
                moved.reshape(-1, grad.shape[1]), weight[3 * vertical + horizontal]
            )
    return (jnp.stack(weight_grads), back)


def moments(values, weights):
    return (
        jnp.sum(values * weights[:, None], axis=0),
        jnp.sum(values * values * weights[:, None], axis=0),
    )


def normalize(values, total, squares, count, gain, bias):
    mean = total / count
    variance = squares / count - mean * mean
    inverse = lax.rsqrt(variance + EPS)
    scaled = (values - mean) * inverse
    return (scaled, inverse, gain * scaled + bias)


def norm_back(grad, scaled, inverse, gain, total, cross, count, weights):
    return inverse * (gain * grad - weights[:, None] * gain * (total + scaled * cross) / count)


def forward_sums(parts):
    return lax.psum(parts, "group")


def backward_sums(parts):
    return lax.psum((parts[0], parts[1], parts[2], parts[3]), "group")


def adam_step(params, first, second, grad):
    first_new = BETA_ONE * first + (1.0 - BETA_ONE) * grad
    second_new = BETA_TWO * second + (1.0 - BETA_TWO) * grad * grad
    corrected = first_new / (1.0 - BETA_ONE**STEP)
    params_new = params - LR_NORM * corrected / (
        jnp.sqrt(second_new / (1.0 - BETA_TWO**STEP)) + ADAM_EPS
    )
    return (params_new, first_new, second_new)


def rows_total(devices):
    unit = 16 * devices
    return -(-ROWS // unit) * unit


def pieces_of(devices):
    unit = 16 * devices
    total = rows_total(devices) // unit
    parts = min(PIECES, total)
    cuts = [total * place // parts * unit for place in range(parts + 1)]
    return [(cuts[place], cuts[place + 1] - cuts[place]) for place in range(parts)]


def reduce_kernel(n_dp, n_group, pieces, *refs):
    grads, norms, out, norms_out = refs[:4]
    count = len(pieces)
    stage = [refs[4 + 6 * place : 10 + 6 * place] for place in range(count)]
    rest = refs[4 + 6 * count :]
    z_in = rest[:count]
    norm_in, send, recv, z_send, z_recv, n_send, n_recv = rest[count:]
    depth = n_dp // 2
    dp, group = lax.axis_index("dp"), lax.axis_index("group")
    core, side_y = group % 2, group // 2
    side_x, side_z = dp % 2, dp // 2
    pair = (dp, group + 1 - 2 * core)
    over_x = (dp + 1 - 2 * side_x, group)
    over_y = (dp, group + 2 - 4 * side_y)
    one = (
        jnp.where(core == 0, over_x[0], over_y[0]),
        jnp.where(core == 0, over_x[1], over_y[1]),
    )
    two = (
        jnp.where(core == 0, over_y[0], over_x[0]),
        jnp.where(core == 0, over_y[1], over_x[1]),
    )
    bit_one = jnp.where(core == 0, side_x, side_y)
    bit_two = jnp.where(core == 0, side_y, side_x)

    barrier = pltpu.get_barrier_semaphore()
    for other in (pair, over_y):
        pl.semaphore_signal(barrier, inc=1, device_id=other, device_id_type=MESH)
    for step in range(1, n_dp):
        pl.semaphore_signal(
            barrier, inc=1, device_id=(lax.rem(dp + step, n_dp), group), device_id_type=MESH
        )
    pl.semaphore_wait(barrier, n_dp + 1)

    def copy(source, target, place, number, device):
        return pltpu.make_async_remote_copy(
            src_ref=source,
            dst_ref=target,
            send_sem=send.at[place, number],
            recv_sem=recv.at[place, number],
            device_id=device,
            device_id_type=MESH,
        )

    def at(ref, start, size):
        return ref.at[pl.ds(pl.multiple_of(start, 16), size)]

    def add(target, kept, kept_start, come, size):
        chunk = math.gcd(size, 128)

        def step(number, carry):
            row = pl.multiple_of(number * chunk, 16)
            mine = kept[pl.ds(pl.multiple_of(kept_start + row, 16), chunk), :]
            total = mine.astype(F32) + come[pl.ds(row, chunk), :].astype(F32)
            target[pl.ds(row, chunk), :] = total.astype(BF)
            return carry

        lax.fori_loop(0, size // chunk, step, 0)

    norm_copies = []
    norm_in[dp] = norms[...]
    for step in range(1, n_dp):
        made = pltpu.make_async_remote_copy(
            src_ref=norms,
            dst_ref=norm_in.at[dp],
            send_sem=n_send.at[step],
            recv_sem=n_recv.at[step],
            device_id=(lax.rem(dp + step, n_dp), group),
            device_id_type=MESH,
        )
        norm_copies.append(made)

    live = {}

    def begin(place, number):
        start, size = pieces[place]
        sum_one, in_one, sum_two, in_two, sum_three, in_three = stage[place]
        half, quarter, eighth = size // 2, size // 4, size // 8
        small = eighth // depth
        base_one = start + core * half
        base_two = base_one + bit_one * quarter
        base_three = base_two + bit_two * eighth
        if number == 0:
            made = [copy(at(grads, start + (1 - core) * half, half), in_one, place, 0, pair)]
        elif number == 1:
            made = [copy(at(sum_one, (1 - bit_one) * quarter, quarter), in_two, place, 1, one)]
        elif number == 2:
            made = [copy(at(sum_two, (1 - bit_two) * eighth, eighth), in_three, place, 2, two)]
        elif number in (3, 4):
            made = []
            for step in range(1, depth):
                other = lax.rem(side_z + step, depth)
                if number == 3:
                    source, target = at(sum_three, other * small, small), z_in[place].at[step - 1]
                else:
                    source = target = at(out, base_three + side_z * small, small)
                made.append(
                    pltpu.make_async_remote_copy(
                        src_ref=source,
                        dst_ref=target,
                        send_sem=z_send.at[place, number - 3, step],
                        recv_sem=z_recv.at[place, number - 3, step],
                        device_id=(other * 2 + side_x, group),
                        device_id_type=MESH,
                    )
                )
        elif number == 5:
            rows = at(out, base_three, eighth)
            made = [copy(rows, rows, place, 3, two)]
        elif number == 6:
            rows = at(out, base_two, quarter)
            made = [copy(rows, rows, place, 4, one)]
        else:
            rows = at(out, base_one, half)
            made = [copy(rows, rows, place, 5, pair)]
        for each in made:
            each.start()
        live[place, number] = made

    def finish(place, number):
        start, size = pieces[place]
        sum_one, in_one, sum_two, in_two, sum_three, in_three = stage[place]
        half, quarter, eighth = size // 2, size // 4, size // 8
        small = eighth // depth
        for each in live[place, number]:
            each.wait_recv()
        if number == 0:
            add(sum_one, grads, start + core * half, in_one, half)
        elif number == 1:
            add(sum_two, sum_one, bit_one * quarter, in_two, quarter)
        elif number == 2:
            add(sum_three, sum_two, bit_two * eighth, in_three, eighth)
        elif number == 3:
            mine = pl.multiple_of(side_z * small, 16)
            total = sum_three[pl.ds(mine, small), :].astype(F32)
            for step in range(depth - 1):
                total = total + z_in[place][step].astype(F32)
            own = start + core * half + bit_one * quarter + bit_two * eighth + side_z * small
            out[pl.ds(pl.multiple_of(own, 16), small), :] = total.astype(BF)

    for tick in range(8 + count - 1):
        for place in range(count):
            number = tick - place
            if 0 <= number - 1 < 8:
                finish(place, number - 1)
            if 0 <= number < 8:
                begin(place, number)
        if tick == 0:
            for made in norm_copies:
                made.start()
    finish(count - 1, 7)
    for made in norm_copies:
        made.wait()
    total = norm_in[0]
    for step in range(1, n_dp):
        total = total + norm_in[step]
    norms_out[...] = total
    for made in live.values():
        for each in made:
            each.wait_send()


def reduce_all(mesh, grads, norms):
    n_dp, n_group = mesh.shape["dp"], mesh.shape["group"]
    pieces = pieces_of(n_dp * n_group)
    count, depth = len(pieces), n_dp // 2
    stages, firsts = [], []
    for _, size in pieces:
        for part in (size // 2, size // 2, size // 4, size // 4, size // 8, size // 8):
            stages.append(pltpu.VMEM((part, 256), BF))
        firsts.append(pltpu.VMEM((max(depth - 1, 1), size // 8 // depth, 256), BF))
    dma = pltpu.SemaphoreType.DMA
    return pl.pallas_call(
        partial(reduce_kernel, n_dp, n_group, pieces),
        out_shape=(
            jax.ShapeDtypeStruct(grads.shape, BF),
            jax.ShapeDtypeStruct(norms.shape, F32),
        ),
        in_specs=[WHOLE] * 2,
        out_specs=(WHOLE, WHOLE),
        scratch_shapes=stages
        + firsts
        + [
            pltpu.VMEM((n_dp,) + norms.shape, F32),
            dma((count, 6)),
            dma((count, 6)),
            dma((count, 2, depth)),
            dma((count, 2, depth)),
            dma((n_dp,)),
            dma((n_dp,)),
        ],
        compiler_params=pltpu.CompilerParams(
            collective_id=0, has_side_effects=True, vmem_limit_bytes=VMEM_LIMIT
        ),
        name="reduce_grads",
    )(grads, norms)


def dot(left, right):
    return jnp.dot(left, right, preferred_element_type=F32)


def dot_nt(left, right):
    return lax.dot_general(left, right, (((1,), (1,)), ((), ())), preferred_element_type=F32)


def dot_tn(left, right):
    return lax.dot_general(left, right, (((0,), (0,)), ((), ())), preferred_element_type=F32)


def split(value):
    high = value.astype(BF)
    return high, (value - high.astype(F32)).astype(BF)


def dot_split(left, right):
    return dot(
        jnp.concatenate([left[0], left[0], left[1]], axis=1),
        jnp.concatenate([right[0], right[1], right[0]], axis=0),
    )


def gram_tn(value):
    high, low = split(value)
    return dot_tn(high, high) + dot_tn(high, low) + dot_tn(low, high)


def gram_nt(value):
    high, low = split(value)
    return dot_nt(high, high) + dot_nt(high, low) + dot_nt(low, high)


def eye(size, kept=None):
    row = lax.broadcasted_iota(jnp.int32, (size, size), 0)
    col = lax.broadcasted_iota(jnp.int32, (size, size), 1)
    return jnp.where(row == col, 1.0, 0.0).astype(F32)


def muon_kernel(*refs):
    grads = refs[0]
    weight_in, moment_in = refs[1:8], refs[8:15]
    weight_out, moment_out = refs[15:22], refs[22:29]
    g_buf = refs[29]
    weight, moment = refs[30:37], refs[37:44]
    chain_a, chain_p, small_a, small_p, sem, g_sem, out_sem = refs[44:51]

    g_cuts = (0, 1024, 3328, 3456, 6528, ROWS)
    loads = [
        pltpu.make_async_copy(
            grads.at[pl.ds(low, high - low)], g_buf.at[pl.ds(low, high - low)], g_sem.at[place]
        )
        for place, (low, high) in enumerate(zip(g_cuts[:-1], g_cuts[1:]))
    ]
    loads_m = [pltpu.make_async_copy(moment_in[i], moment[i], sem.at[0, i]) for i in range(7)]
    loads_w = [pltpu.make_async_copy(weight_in[i], weight[i], sem.at[1, i]) for i in range(7)]
    order = (2, 1, 4, 5, 6, 0, 3)
    for i, place in zip((2, 1, 4, 0, 3), range(5)):
        loads[place].start()
        loads_m[i].start()
        if i == 4:
            loads_m[5].start()
            loads_m[6].start()
    for i in order:
        loads_w[i].start()
    stores = []

    def send(source, target, number, i):
        made = pltpu.make_async_copy(source, target, out_sem.at[number, i])
        made.start()
        stores.append(made)

    def norm_of(gram, size):
        trace = jnp.sum(gram * eye(size))
        return 1.0 / (jnp.sqrt(trace) + 1e-07)

    scales = []

    loads[0].wait()
    loads_m[2].wait()
    for block in range(4):
        cols = slice(256 * block, 256 * (block + 1))
        rows = g_buf[256 * block : 256 * (block + 1), :].astype(F32)
        moment[2][:, cols] = MU * moment[2][:, cols] + rows
    send(moment[2], moment_out[2], 0, 2)
    gram = gram_nt(moment[2][...])
    inverse = norm_of(gram, 256)
    scales.append(inverse)
    chain_a[0] = gram * (inverse * inverse)

    def tall(i, place, taps, size, base, number):
        loads[place].wait()
        loads_m[i].wait()
        chain_a[number] = jnp.zeros((256, 256), F32)

        def step(tap, carry):
            row = pl.multiple_of(base + tap * size, 16)
            new = MU * moment[i][tap] + g_buf[pl.ds(row, size), :].astype(F32)
            moment[i][tap] = new
            chain_a[number] += gram_tn(new)
            return carry

        lax.fori_loop(0, taps, step, 0)
        send(moment[i], moment_out[i], 0, i)
        gram = chain_a[number]
        inverse = norm_of(gram, 256)
        scales.append(inverse)
        chain_a[number] = gram * (inverse * inverse)

    tall(1, 1, 9, 256, 1024, 1)

    loads[2].wait()
    for i in (4, 5, 6):
        loads_m[i].wait()
    tiny = g_buf[3328:3456, :].astype(F32)
    reduce_new = []
    for tap in range(3):
        rows, cols = 32 * (tap // 2), 128 * (tap % 2)
        new = MU * moment[4][tap] + tiny[rows : rows + 32, cols : cols + 128]
        moment[4][tap] = new
        reduce_new.append(new)
    expand_new = MU * moment[6][...] + tiny[32:64, 128:256]
    moment[6][...] = expand_new
    spatial_new = []
    for tap in range(9):
        block = tiny[64 + 32 * (tap // 8) : 96 + 32 * (tap // 8), 128 * (tap % 8 // 4) :][:, :128]
        if tap % 4:
            block = pltpu.roll(block, 128 - 32 * (tap % 4), 1)
        new = MU * moment[5][tap] + block[:, :32]
        moment[5][tap] = new
        spatial_new.append(new)
    for i in (4, 5, 6):
        send(moment[i], moment_out[i], 0, i)
    grams = (
        sum(gram_tn(new) for new in spatial_new),
        sum(gram_nt(new) for new in reduce_new),
        gram_nt(expand_new),
    )
    tiny_scales = [norm_of(gram, 32) for gram in grams]
    blocks = []
    for place, (gram, inverse) in enumerate(zip(grams, tiny_scales)):
        wide = jnp.concatenate([gram * (inverse * inverse), jnp.zeros((32, 96), F32)], axis=1)
        blocks.append(pltpu.roll(wide, 32 * place, 1) if place else wide)
    blocks.append(jnp.zeros((32, 128), F32))
    small_a[...] = jnp.concatenate(blocks, axis=0)

    tall(0, 3, 3, 1024, 3456, 2)
    tall(3, 4, 5, 128, 6528, 3)

    chains = [(chain_a.at[n], chain_p.at[n], eye(256)) for n in range(4)]
    chains.append((small_a, small_p, eye(128)))
    for _, chain, unit in chains:
        chain[...] = unit

    def newton(step, carry):
        for a_ref, p_ref, unit in chains:
            a = a_ref[...]
            a_split = split(a)
            square = dot_split(a_split, a_split)
            poly = split(NS_A * unit + NS_B * a + NS_C * square)
            p_ref[...] = dot_split(split(p_ref[...]), poly)
            once = dot_split(a_split, poly)
            a_ref[...] = dot_split(split(once), poly)
        return carry

    lax.fori_loop(0, NS_STEPS, newton, 0)

    loads_w[2].wait()
    poly = chain_p[0].astype(BF)
    factor = LR * 2.0 * scales[0]
    for block in range(4):
        cols = slice(256 * block, 256 * (block + 1))
        weight[2][:, cols] = weight[2][:, cols] - factor * dot(poly, moment[2][:, cols].astype(BF))
    send(weight[2], weight_out[2], 1, 2)

    def apply(i, taps, number):
        loads_w[i].wait()
        poly = chain_p[number].astype(BF)
        factor = LR * scales[number]

        def step(tap, carry):
            weight[i][tap] = weight[i][tap] - factor * dot(moment[i][tap].astype(BF), poly)
            return carry

        lax.fori_loop(0, taps, step, 0)
        send(weight[i], weight_out[i], 1, i)

    apply(1, 9, 1)
    apply(0, 3, 2)
    apply(3, 5, 3)
    for i in (4, 5, 6):
        loads_w[i].wait()
    tiny_p = small_p[...].astype(BF)
    for tap in range(9):
        change = dot(moment[5][tap].astype(BF), tiny_p[:32, :32])
        weight[5][tap] = weight[5][tap] - LR * tiny_scales[0] * change
    none = jnp.zeros((32, 128), BF)
    for tap in range(3):
        stack = jnp.concatenate([none, moment[4][tap].astype(BF), none, none], axis=0)
        weight[4][tap] = weight[4][tap] - LR * tiny_scales[1] * dot(tiny_p[32:64, :], stack)
    stack = jnp.concatenate([none, none, moment[6][...].astype(BF), none], axis=0)
    weight[6][...] = weight[6][...] - LR * 2.0 * tiny_scales[2] * dot(tiny_p[64:96, :], stack)
    for i in (4, 5, 6):
        send(weight[i], weight_out[i], 1, i)
    for made in stores:
        made.wait()


def muon(grads, weights, moments_old):
    shapes = [jax.ShapeDtypeStruct(each.shape, F32) for each in weights]
    dma = pltpu.SemaphoreType.DMA
    anywhere = pl.BlockSpec(memory_space=pl.ANY)
    out = pl.pallas_call(
        muon_kernel,
        out_shape=shapes + shapes,
        in_specs=[anywhere] * 15,
        out_specs=[anywhere] * 14,
        scratch_shapes=[pltpu.VMEM(grads.shape, BF)]
        + [pltpu.VMEM(each.shape, F32) for each in weights] * 2
        + [
            pltpu.VMEM((4, 256, 256), F32),
            pltpu.VMEM((4, 256, 256), F32),
            pltpu.VMEM((128, 128), F32),
            pltpu.VMEM((128, 128), F32),
            dma((2, 7)),
            dma((5,)),
            dma((2, 7)),
        ],
        compiler_params=pltpu.CompilerParams(vmem_limit_bytes=VMEM_LIMIT),
        name="muon",
    )(grads, *weights, *moments_old)
    return out[:7], out[7:]


def body(
    mesh,
    slow_in,
    fast_in,
    slow_cotangent,
    fast_cotangent,
    clip_start,
    clip_end,
    slow_reduce,
    slow_spatial,
    slow_expand,
    lateral,
    fast_reduce,
    fast_spatial,
    fast_expand,
    slow_reduce_moment,
    slow_spatial_moment,
    slow_expand_moment,
    lateral_moment,
    fast_reduce_moment,
    fast_spatial_moment,
    fast_expand_moment,
    norm_params,
    norm_first,
    norm_second,
):
    frames = slow_in.shape[1]
    side = slow_in.shape[2]
    pixels = side * side
    fast_frames = fast_in.shape[1]
    slow_width = slow_in.shape[4]
    fast_width = fast_in.shape[4]
    mid_width = slow_reduce.shape[2]
    fast_mid = fast_reduce.shape[2]
    half = jnp.bfloat16
    first = lax.axis_index("dp") * frames - 1
    slow_valid, slow_segment = frame_info(clip_start[0], clip_end[0], first, frames + 2)
    fast_valid = jnp.repeat(slow_valid, 4)[2:]
    fast_segment = jnp.repeat(slow_segment, 4)[2:]
    slow_taps = [
        pair_mask(
            slow_valid[1 : frames + 1],
            slow_segment[1 : frames + 1],
            slow_valid[tap : tap + frames],
            slow_segment[tap : tap + frames],
        ).astype(half)
        for tap in range(3)
    ]
    fast_taps = [
        pair_mask(
            fast_valid[2 : 2 + fast_frames],
            fast_segment[2 : 2 + fast_frames],
            fast_valid[1 + tap : 1 + tap + fast_frames],
            fast_segment[1 + tap : 1 + tap + fast_frames],
        ).astype(half)
        for tap in range(3)
    ]
    lateral_taps = [
        pair_mask(
            slow_valid[1 : frames + 2],
            slow_segment[1 : frames + 2],
            fast_valid[tap : tap + 4 * (frames + 1) : 4],
            fast_segment[tap : tap + 4 * (frames + 1) : 4],
        ).astype(half)
        for tap in range(5)
    ]
    slow_mask = jnp.repeat(slow_valid[1 : frames + 1].astype(jnp.float32), pixels)
    fast_mask = jnp.repeat(fast_valid[2 : 2 + fast_frames].astype(jnp.float32), pixels)
    count_local = jnp.sum(slow_valid[1 : frames + 1].astype(jnp.float32)) * pixels
    widths = (mid_width, mid_width, slow_width, fast_mid, fast_mid, fast_width)
    offsets = [sum(widths[:place]) for place in range(6)]
    gains = [norm_params[0, start : start + width] for start, width in zip(offsets, widths)]
    biases = [norm_params[1, start : start + width] for start, width in zip(offsets, widths)]
    reduce_low = slow_reduce.astype(half)
    spatial_low = slow_spatial.astype(half)
    expand_low = slow_expand.astype(half)
    lateral_low = lateral.astype(half)
    fast_reduce_low = fast_reduce.astype(half)
    fast_spatial_low = fast_spatial.astype(half)
    fast_expand_low = fast_expand.astype(half)
    slow_x = slow_in[0].reshape(frames, pixels, slow_width)
    fast_x = fast_in[0].reshape(fast_frames, pixels, fast_width)
    slow_size = pixels * slow_width
    edges = jnp.concatenate(
        [
            jnp.stack([slow_x[0].reshape(-1), slow_x[frames - 1].reshape(-1)]),
            jnp.stack([fast_x[0:2].reshape(-1), fast_x[fast_frames - 2 :].reshape(-1)]),
        ],
        axis=1,
    )
    rims = padded_2(edges, (("dp", 0),), 1)
    slow_wide = jnp.concatenate(
        [
            rims[0, :slow_size].reshape(1, pixels, slow_width),
            slow_x,
            rims[3, :slow_size].reshape(1, pixels, slow_width),
        ]
    )
    fast_wide = jnp.concatenate(
        [
            rims[0, slow_size:].reshape(2, pixels, fast_width),
            fast_x,
            rims[3, slow_size:].reshape(2, pixels, fast_width),
        ]
    )
    slow_one = jnp.zeros((frames * pixels, mid_width), jnp.float32)
    reduce_rows = []
    for tap in range(3):
        rows = (slow_wide[tap : tap + frames] * slow_taps[tap][:, None, None]).reshape(
            -1, slow_width
        )
        reduce_rows.append(rows)
        slow_one = slow_one + jnp.dot(rows, reduce_low[tap], preferred_element_type=jnp.float32)
    lateral_rows = []
    for tap in range(5):
        rows = (
            fast_wide[tap : tap + 4 * frames : 4] * lateral_taps[tap][:frames, None, None]
        ).reshape(-1, fast_width)
        lateral_rows.append(rows)
        slow_one = slow_one + jnp.dot(rows, lateral_low[tap], preferred_element_type=jnp.float32)
    fast_one = jnp.zeros((fast_frames * pixels, fast_mid), jnp.float32)
    fast_rows = []
    for tap in range(3):
        rows = (fast_wide[1 + tap : 1 + tap + fast_frames] * fast_taps[tap][:, None, None]).reshape(
            -1, fast_width
        )
        fast_rows.append(rows)
        fast_one = fast_one + jnp.dot(
            rows, fast_reduce_low[tap], preferred_element_type=jnp.float32
        )
    slow_total, slow_squares = moments(slow_one, slow_mask)
    fast_total, fast_squares = moments(fast_one, fast_mask)
    count, slow_total, slow_squares, fast_total, fast_squares = forward_sums(
        (count_local, slow_total, slow_squares, fast_total, fast_squares)
    )
    fast_count = 4.0 * count
    scaled_sa, inverse_sa, norm_sa = normalize(
        slow_one, slow_total, slow_squares, count, gains[0], biases[0]
    )
    scaled_fa, inverse_fa, norm_fa = normalize(
        fast_one, fast_total, fast_squares, fast_count, gains[3], biases[3]
    )
    hidden_sa = jax.nn.silu(norm_sa).astype(half)
    hidden_fa = jax.nn.silu(norm_fa).astype(half)
    slow_two = spatial_forward(hidden_sa, spatial_low, side)
    fast_two = spatial_forward(hidden_fa, fast_spatial_low, side)
    slow_total, slow_squares = moments(slow_two, slow_mask)
    fast_total, fast_squares = moments(fast_two, fast_mask)
    slow_total, slow_squares, fast_total, fast_squares = forward_sums(
        (slow_total, slow_squares, fast_total, fast_squares)
    )
    scaled_sb, inverse_sb, norm_sb = normalize(
        slow_two, slow_total, slow_squares, count, gains[1], biases[1]
    )
    scaled_fb, inverse_fb, norm_fb = normalize(
        fast_two, fast_total, fast_squares, fast_count, gains[4], biases[4]
    )
    hidden_sb = jax.nn.silu(norm_sb).astype(half)
    hidden_fb = jax.nn.silu(norm_fb).astype(half)
    slow_three = jnp.dot(hidden_sb, expand_low, preferred_element_type=jnp.float32)
    fast_three = jnp.dot(hidden_fb, fast_expand_low, preferred_element_type=jnp.float32)
    slow_total, slow_squares = moments(slow_three, slow_mask)
    fast_total, fast_squares = moments(fast_three, fast_mask)
    slow_total, slow_squares, fast_total, fast_squares = forward_sums(
        (slow_total, slow_squares, fast_total, fast_squares)
    )
    scaled_sc, inverse_sc, norm_sc = normalize(
        slow_three, slow_total, slow_squares, count, gains[2], biases[2]
    )
    scaled_fc, inverse_fc, norm_fc = normalize(
        fast_three, fast_total, fast_squares, fast_count, gains[5], biases[5]
    )
    slow_sum = norm_sc + slow_x.reshape(-1, slow_width).astype(jnp.float32)
    fast_sum = norm_fc + fast_x.reshape(-1, fast_width).astype(jnp.float32)
    slow_out = (jax.nn.silu(slow_sum) * slow_mask[:, None]).astype(half)
    fast_out = (jax.nn.silu(fast_sum) * fast_mask[:, None]).astype(half)
    slow_grad = (
        slow_cotangent[0].reshape(-1, slow_width).astype(jnp.float32)
        * slow_mask[:, None]
        * slope(slow_sum)
    )
    fast_grad = (
        fast_cotangent[0].reshape(-1, fast_width).astype(jnp.float32)
        * fast_mask[:, None]
        * slope(fast_sum)
    )
    slow_input_grad = slow_grad
    fast_input_grad = fast_grad
    bias_grads = [None] * 6
    gain_grads = [None] * 6
    bias_grads[2] = jnp.sum(slow_grad, axis=0)
    gain_grads[2] = jnp.sum(slow_grad * scaled_sc, axis=0)
    bias_grads[5] = jnp.sum(fast_grad, axis=0)
    gain_grads[5] = jnp.sum(fast_grad * scaled_fc, axis=0)
    slow_sums, slow_cross, fast_sums, fast_cross = backward_sums(
        (bias_grads[2], gain_grads[2], bias_grads[5], gain_grads[5])
    )
    bias_grads[2], gain_grads[2], bias_grads[5], gain_grads[5] = (
        slow_sums,
        slow_cross,
        fast_sums,
        fast_cross,
    )
    slow_dz = norm_back(
        slow_grad, scaled_sc, inverse_sc, gains[2], slow_sums, slow_cross, count, slow_mask
    ).astype(half)
    fast_dz = norm_back(
        fast_grad, scaled_fc, inverse_fc, gains[5], fast_sums, fast_cross, fast_count, fast_mask
    ).astype(half)
    grad_sc = contract_rows(hidden_sb, slow_dz)
    grad_fc = contract_rows(hidden_fb, fast_dz)
    slow_grad = contract_cols(slow_dz, expand_low) * slope(norm_sb)
    fast_grad = contract_cols(fast_dz, fast_expand_low) * slope(norm_fb)
    bias_grads[1] = jnp.sum(slow_grad, axis=0)
    gain_grads[1] = jnp.sum(slow_grad * scaled_sb, axis=0)
    bias_grads[4] = jnp.sum(fast_grad, axis=0)
    gain_grads[4] = jnp.sum(fast_grad * scaled_fb, axis=0)
    slow_sums, slow_cross, fast_sums, fast_cross = backward_sums(
        (bias_grads[1], gain_grads[1], bias_grads[4], gain_grads[4])
    )
    bias_grads[1], gain_grads[1], bias_grads[4], gain_grads[4] = (
        slow_sums,
        slow_cross,
        fast_sums,
        fast_cross,
    )
    slow_dz = norm_back(
        slow_grad, scaled_sb, inverse_sb, gains[1], slow_sums, slow_cross, count, slow_mask
    ).astype(half)
    fast_dz = norm_back(
        fast_grad, scaled_fb, inverse_fb, gains[4], fast_sums, fast_cross, fast_count, fast_mask
    ).astype(half)
    grad_sb, slow_back = spatial_backward(hidden_sa, slow_dz, spatial_low, side)
    grad_fb, fast_back = spatial_backward(hidden_fa, fast_dz, fast_spatial_low, side)
    slow_grad = slow_back * slope(norm_sa)
    fast_grad = fast_back * slope(norm_fa)
    bias_grads[0] = jnp.sum(slow_grad, axis=0)
    gain_grads[0] = jnp.sum(slow_grad * scaled_sa, axis=0)
    bias_grads[3] = jnp.sum(fast_grad, axis=0)
    gain_grads[3] = jnp.sum(fast_grad * scaled_fa, axis=0)
    slow_sums, slow_cross, fast_sums, fast_cross = backward_sums(
        (bias_grads[0], gain_grads[0], bias_grads[3], gain_grads[3])
    )
    bias_grads[0], gain_grads[0], bias_grads[3], gain_grads[3] = (
        slow_sums,
        slow_cross,
        fast_sums,
        fast_cross,
    )
    slow_dz = norm_back(
        slow_grad, scaled_sa, inverse_sa, gains[0], slow_sums, slow_cross, count, slow_mask
    ).astype(half)
    fast_dz = norm_back(
        fast_grad, scaled_fa, inverse_fa, gains[3], fast_sums, fast_cross, fast_count, fast_mask
    ).astype(half)
    grad_sa = jnp.stack([contract_rows(rows, slow_dz) for rows in reduce_rows])
    grad_lat = jnp.stack([contract_rows(rows, slow_dz) for rows in lateral_rows])
    grad_fa = jnp.stack([contract_rows(rows, fast_dz) for rows in fast_rows])
    slow_frames_dz = slow_dz.reshape(frames, pixels, mid_width)
    fast_frames_dz = fast_dz.reshape(fast_frames, pixels, fast_mid)
    slow_dz_size = pixels * mid_width
    back_edges = jnp.concatenate(
        [
            jnp.stack([slow_frames_dz[0].reshape(-1), slow_frames_dz[frames - 1].reshape(-1)]),
            jnp.stack([fast_frames_dz[0].reshape(-1), fast_frames_dz[fast_frames - 1].reshape(-1)]),
        ],
        axis=1,
    )
    back_rims = padded_2(back_edges, (("dp", 0),), 1)
    slow_dz_wide = jnp.concatenate(
        [
            back_rims[0, :slow_dz_size].reshape(1, pixels, mid_width),
            slow_frames_dz,
            back_rims[3, :slow_dz_size].reshape(1, pixels, mid_width),
        ]
    )
    fast_dz_wide = jnp.concatenate(
        [
            back_rims[0, slow_dz_size:].reshape(1, pixels, fast_mid),
            fast_frames_dz,
            back_rims[3, slow_dz_size:].reshape(1, pixels, fast_mid),
        ]
    )
    for tap in range(3):
        rows = (
            slow_dz_wide[2 - tap : 2 - tap + frames] * slow_taps[2 - tap][:, None, None]
        ).reshape(-1, mid_width)
        slow_input_grad = slow_input_grad + contract_cols(rows, reduce_low[tap])
        rows = (
            fast_dz_wide[2 - tap : 2 - tap + fast_frames] * fast_taps[2 - tap][:, None, None]
        ).reshape(-1, fast_mid)
        fast_input_grad = fast_input_grad + contract_cols(rows, fast_reduce_low[tap])
    slow_dz_next = slow_dz_wide[1 : frames + 2]
    lateral_pieces = []
    for tap in range(5):
        rows = (slow_dz_next * lateral_taps[tap][:, None, None]).reshape(-1, mid_width)
        lateral_pieces.append(
            contract_cols(rows, lateral_low[tap]).reshape(frames + 1, pixels, fast_width)
        )
    lateral_grid = jnp.stack(lateral_pieces[:4], axis=1)
    lateral_grid = lateral_grid.at[1:, 0].add(lateral_pieces[4][:frames])
    lateral_back = lateral_grid.reshape(4 * (frames + 1), pixels, fast_width)[2 : 2 + fast_frames]
    fast_input_grad = fast_input_grad + lateral_back.reshape(-1, fast_width)
    norm_grad = jnp.stack([jnp.concatenate(gain_grads), jnp.concatenate(bias_grads)])
    weights = (
        slow_reduce,
        slow_spatial,
        slow_expand,
        lateral,
        fast_reduce,
        fast_spatial,
        fast_expand,
    )
    moments_old = (
        slow_reduce_moment,
        slow_spatial_moment,
        slow_expand_moment,
        lateral_moment,
        fast_reduce_moment,
        fast_spatial_moment,
        fast_expand_moment,
    )
    zero = jnp.zeros((32, 224), F32)
    turned = jnp.swapaxes(grad_fa, 1, 2)
    packed = jnp.concatenate(
        [grad_sc[:, 256 * block : 256 * (block + 1)] for block in range(4)]
        + [grad_sb.reshape(-1, 256)]
        + [jnp.concatenate([turned[0], turned[1]], axis=1)]
        + [jnp.concatenate([turned[2], grad_fc], axis=1)]
        + [jnp.concatenate([grad_fb[tap] for tap in range(8)], axis=1)]
        + [jnp.concatenate([grad_fb[8], zero], axis=1)]
        + [grad_sa.reshape(-1, 256), grad_lat.reshape(-1, 256)]
    ).astype(half)
    total_rows = rows_total(mesh.shape["dp"] * mesh.shape["group"])
    packed = jnp.pad(packed, ((0, total_rows - ROWS), (0, 0)))
    width = norm_grad.shape[1]
    norm_wide = jnp.pad(norm_grad, ((0, 0), (0, 2048 - width))).reshape(16, 256)
    packed, norm_wide = reduce_all(mesh, packed, norm_wide)
    norm_grad = norm_wide.reshape(2, 2048)[:, :width]
    weights_new, moments_new = muon(
        packed,
        weights[:4] + (jnp.swapaxes(fast_reduce, 1, 2),) + weights[5:],
        moments_old[:4] + (jnp.swapaxes(fast_reduce_moment, 1, 2),) + moments_old[5:],
    )
    weights_new, moments_new = list(weights_new), list(moments_new)
    weights_new[4] = jnp.swapaxes(weights_new[4], 1, 2)
    moments_new[4] = jnp.swapaxes(moments_new[4], 1, 2)
    params_new, first_new, second_new = adam_step(norm_params, norm_first, norm_second, norm_grad)
    return (
        slow_out.reshape(1, frames, side, side, slow_width),
        fast_out.reshape(1, fast_frames, side, side, fast_width),
        slow_input_grad.reshape(1, frames, side, side, slow_width),
        fast_input_grad.reshape(1, fast_frames, side, side, fast_width),
        weights_new[0],
        weights_new[1],
        weights_new[2],
        weights_new[3],
        weights_new[4],
        weights_new[5],
        weights_new[6],
        moments_new[0],
        moments_new[1],
        moments_new[2],
        moments_new[3],
        moments_new[4],
        moments_new[5],
        moments_new[6],
        first_new,
        second_new,
        params_new,
    )


def solution(mesh):
    return jax.shard_map(
        partial(body, mesh),
        mesh=mesh,
        in_specs=(
            P("group", "dp", None, None, None),
            P("group", "dp", None, None, None),
            P("group", "dp", None, None, None),
            P("group", "dp", None, None, None),
            P("group", None),
            P("group", None),
            P(),
            P(),
            P(),
            P(),
            P(),
            P(),
            P(),
            P(),
            P(),
            P(),
            P(),
            P(),
            P(),
            P(),
            P(),
            P(),
            P(),
        ),
        out_specs=(
            P("group", "dp", None, None, None),
            P("group", "dp", None, None, None),
            P("group", "dp", None, None, None),
            P("group", "dp", None, None, None),
            P(),
            P(),
            P(),
            P(),
            P(),
            P(),
            P(),
            P(),
            P(),
            P(),
            P(),
            P(),
            P(),
            P(),
            P(),
            P(),
            P(),
        ),
        check_vma=False,
    )
```

```python
from functools import partial
import math

import jax
import jax.numpy as jnp
from jax import lax
from jax.experimental import pallas as pl
from jax.experimental.pallas import tpu as pltpu
from jax.sharding import PartitionSpec as P

NS_STEPS = 5
STEP = 10


EPS = 1e-05
MU = 0.95
LR = 0.3
BETA_ONE = 0.9
BETA_TWO = 0.95
LR_NORM = 0.2
ADAM_EPS = 1e-08
NS_A = 3.4445
NS_B = -4.775
NS_C = 2.0315
F32 = jnp.float32
BF = jnp.bfloat16
MESH = pl.DeviceIdType.MESH
TINY = 3328
REDUCE = 3456
LATERAL = 6528
ROWS = 7168
PIECES = 2
VMEM_LIMIT = 62 * 2**20
WHOLE = pl.BlockSpec(memory_space=pltpu.VMEM)
ANYWHERE = pl.BlockSpec(memory_space=pl.ANY)
SCALARS = pl.BlockSpec(memory_space=pltpu.SMEM)


def adam_step(params, first, second, grad):
    first_new = BETA_ONE * first + (1.0 - BETA_ONE) * grad
    second_new = BETA_TWO * second + (1.0 - BETA_TWO) * grad * grad
    corrected = first_new / (1.0 - BETA_ONE**STEP)
    params_new = params - LR_NORM * corrected / (
        jnp.sqrt(second_new / (1.0 - BETA_TWO**STEP)) + ADAM_EPS
    )
    return (params_new, first_new, second_new)


def rows_total(devices):
    unit = 16 * devices
    return -(-ROWS // unit) * unit


def pieces_of(devices):
    unit = 16 * devices
    total = rows_total(devices) // unit
    parts = min(PIECES, total)
    cuts = [total * place // parts * unit for place in range(parts + 1)]
    return [(cuts[place], cuts[place + 1] - cuts[place]) for place in range(parts)]


def reduce_kernel(n_dp, n_group, pieces, *refs):
    grads, norms, out, norms_out = refs[:4]
    count = len(pieces)
    stage = [refs[4 + 6 * place : 10 + 6 * place] for place in range(count)]
    rest = refs[4 + 6 * count :]
    z_in = rest[:count]
    norm_in, send, recv, z_send, z_recv, n_send, n_recv = rest[count:]
    depth = n_dp // 2
    dp, group = lax.axis_index("dp"), lax.axis_index("group")
    core, side_y = group % 2, group // 2
    side_x, side_z = dp % 2, dp // 2
    pair = (dp, group + 1 - 2 * core)
    over_x = (dp + 1 - 2 * side_x, group)
    over_y = (dp, group + 2 - 4 * side_y)
    one = (
        jnp.where(core == 0, over_x[0], over_y[0]),
        jnp.where(core == 0, over_x[1], over_y[1]),
    )
    two = (
        jnp.where(core == 0, over_y[0], over_x[0]),
        jnp.where(core == 0, over_y[1], over_x[1]),
    )
    bit_one = jnp.where(core == 0, side_x, side_y)
    bit_two = jnp.where(core == 0, side_y, side_x)

    barrier = pltpu.get_barrier_semaphore()
    for other in (pair, over_y):
        pl.semaphore_signal(barrier, inc=1, device_id=other, device_id_type=MESH)
    for step in range(1, n_dp):
        pl.semaphore_signal(
            barrier, inc=1, device_id=(lax.rem(dp + step, n_dp), group), device_id_type=MESH
        )
    pl.semaphore_wait(barrier, n_dp + 1)

    def copy(source, target, place, number, device):
        return pltpu.make_async_remote_copy(
            src_ref=source,
            dst_ref=target,
            send_sem=send.at[place, number],
            recv_sem=recv.at[place, number],
            device_id=device,
            device_id_type=MESH,
        )

    def at(ref, start, size):
        return ref.at[pl.ds(pl.multiple_of(start, 16), size)]

    def add(target, kept, kept_start, come, size):
        chunk = math.gcd(size, 128)

        def step(number, carry):
            row = pl.multiple_of(number * chunk, 16)
            mine = kept[pl.ds(pl.multiple_of(kept_start + row, 16), chunk), :]
            total = mine.astype(F32) + come[pl.ds(row, chunk), :].astype(F32)
            target[pl.ds(row, chunk), :] = total.astype(BF)
            return carry

        lax.fori_loop(0, size // chunk, step, 0)

    norm_copies = []
    norm_in[dp] = norms[...]
    for step in range(1, n_dp):
        made = pltpu.make_async_remote_copy(
            src_ref=norms,
            dst_ref=norm_in.at[dp],
            send_sem=n_send.at[step],
            recv_sem=n_recv.at[step],
            device_id=(lax.rem(dp + step, n_dp), group),
            device_id_type=MESH,
        )
        norm_copies.append(made)

    live = {}

    def begin(place, number):
        start, size = pieces[place]
        sum_one, in_one, sum_two, in_two, sum_three, in_three = stage[place]
        half, quarter, eighth = size // 2, size // 4, size // 8
        small = eighth // depth
        base_one = start + core * half
        base_two = base_one + bit_one * quarter
        base_three = base_two + bit_two * eighth
        if number == 0:
            made = [copy(at(grads, start + (1 - core) * half, half), in_one, place, 0, pair)]
        elif number == 1:
            made = [copy(at(sum_one, (1 - bit_one) * quarter, quarter), in_two, place, 1, one)]
        elif number == 2:
            made = [copy(at(sum_two, (1 - bit_two) * eighth, eighth), in_three, place, 2, two)]
        elif number in (3, 4):
            made = []
            for step in range(1, depth):
                other = lax.rem(side_z + step, depth)
                if number == 3:
                    source, target = at(sum_three, other * small, small), z_in[place].at[step - 1]
                else:
                    source = target = at(out, base_three + side_z * small, small)
                made.append(
                    pltpu.make_async_remote_copy(
                        src_ref=source,
                        dst_ref=target,
                        send_sem=z_send.at[place, number - 3, step],
                        recv_sem=z_recv.at[place, number - 3, step],
                        device_id=(other * 2 + side_x, group),
                        device_id_type=MESH,
                    )
                )
        elif number == 5:
            rows = at(out, base_three, eighth)
            made = [copy(rows, rows, place, 3, two)]
        elif number == 6:
            rows = at(out, base_two, quarter)
            made = [copy(rows, rows, place, 4, one)]
        else:
            rows = at(out, base_one, half)
            made = [copy(rows, rows, place, 5, pair)]
        for each in made:
            each.start()
        live[place, number] = made

    def finish(place, number):
        start, size = pieces[place]
        sum_one, in_one, sum_two, in_two, sum_three, in_three = stage[place]
        half, quarter, eighth = size // 2, size // 4, size // 8
        small = eighth // depth
        for each in live[place, number]:
            each.wait_recv()
        if number == 0:
            add(sum_one, grads, start + core * half, in_one, half)
        elif number == 1:
            add(sum_two, sum_one, bit_one * quarter, in_two, quarter)
        elif number == 2:
            add(sum_three, sum_two, bit_two * eighth, in_three, eighth)
        elif number == 3:
            mine = pl.multiple_of(side_z * small, 16)
            total = sum_three[pl.ds(mine, small), :].astype(F32)
            for step in range(depth - 1):
                total = total + z_in[place][step].astype(F32)
            own = start + core * half + bit_one * quarter + bit_two * eighth + side_z * small
            out[pl.ds(pl.multiple_of(own, 16), small), :] = total.astype(BF)

    for tick in range(8 + count - 1):
        for place in range(count):
            number = tick - place
            if 0 <= number - 1 < 8:
                finish(place, number - 1)
            if 0 <= number < 8:
                begin(place, number)
        if tick == 0:
            for made in norm_copies:
                made.start()
    finish(count - 1, 7)
    for made in norm_copies:
        made.wait()
    total = norm_in[0]
    for step in range(1, n_dp):
        total = total + norm_in[step]
    norms_out[...] = total
    for made in live.values():
        for each in made:
            each.wait_send()


def reduce_all(mesh, grads, norms):
    n_dp, n_group = mesh.shape["dp"], mesh.shape["group"]
    pieces = pieces_of(n_dp * n_group)
    count, depth = len(pieces), n_dp // 2
    stages, firsts = [], []
    for _, size in pieces:
        for part in (size // 2, size // 2, size // 4, size // 4, size // 8, size // 8):
            stages.append(pltpu.VMEM((part, 256), BF))
        firsts.append(pltpu.VMEM((max(depth - 1, 1), size // 8 // depth, 256), BF))
    dma = pltpu.SemaphoreType.DMA
    return pl.pallas_call(
        partial(reduce_kernel, n_dp, n_group, pieces),
        out_shape=(
            jax.ShapeDtypeStruct(grads.shape, BF),
            jax.ShapeDtypeStruct(norms.shape, F32),
        ),
        in_specs=[WHOLE] * 2,
        out_specs=(WHOLE, WHOLE),
        scratch_shapes=stages
        + firsts
        + [
            pltpu.VMEM((n_dp,) + norms.shape, F32),
            dma((count, 6)),
            dma((count, 6)),
            dma((count, 2, depth)),
            dma((count, 2, depth)),
            dma((n_dp,)),
            dma((n_dp,)),
        ],
        compiler_params=pltpu.CompilerParams(
            collective_id=0, has_side_effects=True, vmem_limit_bytes=VMEM_LIMIT
        ),
        name="reduce_grads",
    )(grads, norms)


def dot(left, right):
    return jnp.dot(left, right, preferred_element_type=F32)


def dot_nt(left, right):
    return lax.dot_general(left, right, (((1,), (1,)), ((), ())), preferred_element_type=F32)


def dot_tn(left, right):
    return lax.dot_general(left, right, (((0,), (0,)), ((), ())), preferred_element_type=F32)


def split(value):
    high = value.astype(BF)
    return high, (value - high.astype(F32)).astype(BF)


def dot_split(left, right):
    return dot(
        jnp.concatenate([left[0], left[0], left[1]], axis=1),
        jnp.concatenate([right[0], right[1], right[0]], axis=0),
    )


def gram_tn(value):
    high, low = split(value)
    return dot_tn(high, high) + dot_tn(high, low) + dot_tn(low, high)


def gram_nt(value):
    high, low = split(value)
    return dot_nt(high, high) + dot_nt(high, low) + dot_nt(low, high)


def eye(size, kept=None):
    row = lax.broadcasted_iota(jnp.int32, (size, size), 0)
    col = lax.broadcasted_iota(jnp.int32, (size, size), 1)
    return jnp.where(row == col, 1.0, 0.0).astype(F32)


def muon_kernel(*refs):
    grads = refs[0]
    weight_in, moment_in = refs[1:8], refs[8:15]
    weight_out, moment_out = refs[15:22], refs[22:29]
    g_buf = refs[29]
    weight, moment = refs[30:37], refs[37:44]
    chain_a, chain_p, small_a, small_p, sem, g_sem, out_sem = refs[44:51]

    g_cuts = (0, 1024, 3328, 3456, 6528, ROWS)
    loads = [
        pltpu.make_async_copy(
            grads.at[pl.ds(low, high - low)], g_buf.at[pl.ds(low, high - low)], g_sem.at[place]
        )
        for place, (low, high) in enumerate(zip(g_cuts[:-1], g_cuts[1:]))
    ]
    loads_m = [pltpu.make_async_copy(moment_in[i], moment[i], sem.at[0, i]) for i in range(7)]
    loads_w = [pltpu.make_async_copy(weight_in[i], weight[i], sem.at[1, i]) for i in range(7)]
    order = (2, 1, 4, 5, 6, 0, 3)
    for i, place in zip((2, 1, 4, 0, 3), range(5)):
        loads[place].start()
        loads_m[i].start()
        if i == 4:
            loads_m[5].start()
            loads_m[6].start()
    for i in order:
        loads_w[i].start()
    stores = []

    def send(source, target, number, i):
        made = pltpu.make_async_copy(source, target, out_sem.at[number, i])
        made.start()
        stores.append(made)

    def norm_of(gram, size):
        trace = jnp.sum(gram * eye(size))
        return 1.0 / (jnp.sqrt(trace) + 1e-07)

    scales = []

    loads[0].wait()
    loads_m[2].wait()
    for block in range(4):
        cols = slice(256 * block, 256 * (block + 1))
        rows = g_buf[256 * block : 256 * (block + 1), :].astype(F32)
        moment[2][:, cols] = MU * moment[2][:, cols] + rows
    send(moment[2], moment_out[2], 0, 2)
    gram = gram_nt(moment[2][...])
    inverse = norm_of(gram, 256)
    scales.append(inverse)
    chain_a[0] = gram * (inverse * inverse)

    def tall(i, place, taps, size, base, number):
        loads[place].wait()
        loads_m[i].wait()
        chain_a[number] = jnp.zeros((256, 256), F32)

        def step(tap, carry):
            row = pl.multiple_of(base + tap * size, 16)
            new = MU * moment[i][tap] + g_buf[pl.ds(row, size), :].astype(F32)
            moment[i][tap] = new
            chain_a[number] += gram_tn(new)
            return carry

        lax.fori_loop(0, taps, step, 0)
        send(moment[i], moment_out[i], 0, i)
        gram = chain_a[number]
        inverse = norm_of(gram, 256)
        scales.append(inverse)
        chain_a[number] = gram * (inverse * inverse)

    tall(1, 1, 9, 256, 1024, 1)

    loads[2].wait()
    for i in (4, 5, 6):
        loads_m[i].wait()
    tiny = g_buf[3328:3456, :].astype(F32)
    reduce_new = []
    for tap in range(3):
        rows, cols = 32 * (tap // 2), 128 * (tap % 2)
        new = MU * moment[4][tap] + tiny[rows : rows + 32, cols : cols + 128]
        moment[4][tap] = new
        reduce_new.append(new)
    expand_new = MU * moment[6][...] + tiny[32:64, 128:256]
    moment[6][...] = expand_new
    spatial_new = []
    for tap in range(9):
        block = tiny[64 + 32 * (tap // 8) : 96 + 32 * (tap // 8), 128 * (tap % 8 // 4) :][:, :128]
        if tap % 4:
            block = pltpu.roll(block, 128 - 32 * (tap % 4), 1)
        new = MU * moment[5][tap] + block[:, :32]
        moment[5][tap] = new
        spatial_new.append(new)
    for i in (4, 5, 6):
        send(moment[i], moment_out[i], 0, i)
    grams = (
        sum(gram_tn(new) for new in spatial_new),
        sum(gram_nt(new) for new in reduce_new),
        gram_nt(expand_new),
    )
    tiny_scales = [norm_of(gram, 32) for gram in grams]
    blocks = []
    for place, (gram, inverse) in enumerate(zip(grams, tiny_scales)):
        wide = jnp.concatenate([gram * (inverse * inverse), jnp.zeros((32, 96), F32)], axis=1)
        blocks.append(pltpu.roll(wide, 32 * place, 1) if place else wide)
    blocks.append(jnp.zeros((32, 128), F32))
    small_a[...] = jnp.concatenate(blocks, axis=0)

    tall(0, 3, 3, 1024, 3456, 2)
    tall(3, 4, 5, 128, 6528, 3)

    chains = [(chain_a.at[n], chain_p.at[n], eye(256)) for n in range(4)]
    chains.append((small_a, small_p, eye(128)))
    for _, chain, unit in chains:
        chain[...] = unit

    def newton(step, carry):
        for a_ref, p_ref, unit in chains:
            a = a_ref[...]
            a_split = split(a)
            square = dot_split(a_split, a_split)
            poly = split(NS_A * unit + NS_B * a + NS_C * square)
            p_ref[...] = dot_split(split(p_ref[...]), poly)
            once = dot_split(a_split, poly)
            a_ref[...] = dot_split(split(once), poly)
        return carry

    lax.fori_loop(0, NS_STEPS, newton, 0)

    loads_w[2].wait()
    poly = chain_p[0].astype(BF)
    factor = LR * 2.0 * scales[0]
    for block in range(4):
        cols = slice(256 * block, 256 * (block + 1))
        weight[2][:, cols] = weight[2][:, cols] - factor * dot(poly, moment[2][:, cols].astype(BF))
    send(weight[2], weight_out[2], 1, 2)

    def apply(i, taps, number):
        loads_w[i].wait()
        poly = chain_p[number].astype(BF)
        factor = LR * scales[number]

        def step(tap, carry):
            weight[i][tap] = weight[i][tap] - factor * dot(moment[i][tap].astype(BF), poly)
            return carry

        lax.fori_loop(0, taps, step, 0)
        send(weight[i], weight_out[i], 1, i)

    apply(1, 9, 1)
    apply(0, 3, 2)
    apply(3, 5, 3)
    for i in (4, 5, 6):
        loads_w[i].wait()
    tiny_p = small_p[...].astype(BF)
    for tap in range(9):
        change = dot(moment[5][tap].astype(BF), tiny_p[:32, :32])
        weight[5][tap] = weight[5][tap] - LR * tiny_scales[0] * change
    none = jnp.zeros((32, 128), BF)
    for tap in range(3):
        stack = jnp.concatenate([none, moment[4][tap].astype(BF), none, none], axis=0)
        weight[4][tap] = weight[4][tap] - LR * tiny_scales[1] * dot(tiny_p[32:64, :], stack)
    stack = jnp.concatenate([none, none, moment[6][...].astype(BF), none], axis=0)
    weight[6][...] = weight[6][...] - LR * 2.0 * tiny_scales[2] * dot(tiny_p[64:96, :], stack)
    for i in (4, 5, 6):
        send(weight[i], weight_out[i], 1, i)
    for made in stores:
        made.wait()


def muon(grads, weights, moments_old):
    shapes = [jax.ShapeDtypeStruct(each.shape, F32) for each in weights]
    dma = pltpu.SemaphoreType.DMA
    out = pl.pallas_call(
        muon_kernel,
        out_shape=shapes + shapes,
        in_specs=[ANYWHERE] * 15,
        out_specs=[ANYWHERE] * 14,
        scratch_shapes=[pltpu.VMEM(grads.shape, BF)]
        + [pltpu.VMEM(each.shape, F32) for each in weights] * 2
        + [
            pltpu.VMEM((4, 256, 256), F32),
            pltpu.VMEM((4, 256, 256), F32),
            pltpu.VMEM((128, 128), F32),
            pltpu.VMEM((128, 128), F32),
            dma((2, 7)),
            dma((5,)),
            dma((2, 7)),
        ],
        compiler_params=pltpu.CompilerParams(vmem_limit_bytes=VMEM_LIMIT),
        name="muon",
    )(grads, *weights, *moments_old)
    return out[:7], out[7:]


def sigmoid(value):
    return 0.5 * jnp.tanh(0.5 * value) + 0.5


def spread(row):
    return jnp.broadcast_to(row, (8, row.shape[1]))


def tiled(value):
    value = value + pltpu.roll(value, 64, 1)
    return value + pltpu.roll(value, 32, 1)


def block_kernel(n_dp, n_group, frames, side, *refs):
    slow_in, fast_in, slow_cot, fast_cot, starts, ends = refs[:6]
    w_reduce, w_spatial, w_expand, w_lateral, f_reduce, f_spatial, f_expand, params = refs[6:14]
    slow_out, fast_out, slow_grad, fast_grad, g_out, norm_out = refs[14:20]
    (
        xs, cs, xn, cf, fp, zf, df, ds, zc, za, zb, b1, b2, sa, fa, hsb, hfb, zfa, zfb, fx, fy,
        dzf, h_t, wr, ws, we, wl, bt, fs, fe, gbuf, masks, hs, hr, st_a, st_c, st_f,
        load, store, h_send, h_recv, a_send, a_recv, c_send, c_recv, f_send, f_recv,
    ) = refs[20:]
    pixels = side * side
    n_rows = pixels * frames
    line = side * frames
    dp, group = lax.axis_index("dp"), lax.axis_index("group")
    after = (lax.rem(dp + 1, n_dp), group)
    before = (lax.rem(dp + n_dp - 1, n_dp), group)
    peers = [(dp, lax.rem(group + step, n_group)) for step in range(1, n_group)]

    barrier = pltpu.get_barrier_semaphore()
    for other in peers + [after, before]:
        pl.semaphore_signal(barrier, inc=1, device_id=other, device_id_type=MESH)

    loads = {}

    def fetch(name, source, target):
        loads[name] = pltpu.make_async_copy(source, target, load.at[len(loads)])
        loads[name].start()

    def ready(*names):
        for name in names:
            loads[name].wait()

    half = n_rows // 2
    fetch("xn", fast_in, xn)
    for tap in range(5):
        fetch(("wl", tap), w_lateral.at[tap], lateral_stage(ds, tap))
    fetch("wr0", w_reduce.at[0], ds.at[0:1024, 0:256])
    fetch("xs", slow_in, xs)
    fetch("wr2", w_reduce.at[2], ds.at[0:1024, 512:768])
    fetch("wr1", w_reduce.at[1], ds.at[0:1024, 256:512])
    for tap in range(9):
        fetch(("ws", tap), w_spatial.at[tap], spatial_stage(ds, tap))
    for block in range(4):
        fetch(
            ("we", block),
            w_expand.at[:, 256 * block : 256 * (block + 1)],
            zb.at[256 * block : 256 * (block + 1)],
        )
    fetch("cs", slow_cot, cs)
    fetch("cf", fast_cot, cf)

    first = dp * frames
    row_id = lax.broadcasted_iota(jnp.int32, (frames, 128), 0)
    lane = lax.broadcasted_iota(jnp.int32, (8, 128), 1)

    def info(offset, rows):
        frame = first + offset + rows
        inside = jnp.zeros(rows.shape, jnp.int32)
        begun = jnp.zeros(rows.shape, jnp.int32)
        for slot in range(starts.shape[1]):
            open_ = frame >= starts[0, slot]
            begun = begun + jnp.where(open_, 1, 0)
            inside = jnp.where(open_ & (frame < ends[0, slot]), 1, inside)
        return inside, begun

    own, own_segment = info(0, row_id)
    valid = own.astype(F32)
    for offset, place in ((-1, 1), (1, 2)):
        near, near_segment = info(offset, row_id)
        both = jnp.where((own * near == 1) & (own_segment == near_segment), 1.0, 0.0)
        masks[8 * place : 8 * place + 8, 0:128] = both.astype(F32)
        masks[8 * place : 8 * place + 8, 128:256] = both.astype(F32)
    for block in range(8):
        masks[0:8, 128 * block : 128 * (block + 1)] = valid
    fast_id = lax.broadcasted_iota(jnp.int32, (4 * frames, 128), 0)
    fast_valid = info(0, fast_id >> 2)[0].astype(F32)
    masks[24:56, 0:128] = fast_valid
    count_local = jnp.sum(valid, axis=0, keepdims=True) * float(pixels)
    count_block = jnp.concatenate([spread(count_local)] * 2, axis=1)

    def chunk(number, size):
        return pl.ds(pl.multiple_of(number * size, 16), size)

    def three(value):
        return value.reshape(-1, 8, value.shape[-1])

    def fold(value):
        return jnp.sum(three(value), axis=0)

    def pair(ref, rows):
        return jnp.concatenate([ref[0, rows, :], ref[1, rows, :]], axis=1)

    def set_pair(ref, rows, value):
        ref[0, rows, :] = value[:, :128]
        ref[1, rows, :] = value[:, 128:]

    def loop(count, body, carry=0):
        return lax.fori_loop(0, count, body, carry)

    def zeros(*shape):
        return jnp.zeros(shape, F32)

    row8 = lax.broadcasted_iota(jnp.int32, (8, 1), 0)

    def share(store_ref, sends, recvs, place, sums, squares, extra=None):
        top = jnp.sum(sums, axis=0, keepdims=True)
        second = jnp.sum(squares, axis=0, keepdims=True)
        block = jnp.where(row8 == 0, top, jnp.where(row8 == 1, second, 0.0))
        if extra is not None:
            block = jnp.where(row8 == 2, extra, block)
        store_ref[place, group] = block
        made = []
        for step, peer in enumerate(peers):
            made.append(
                pltpu.make_async_remote_copy(
                    src_ref=store_ref.at[place, group],
                    dst_ref=store_ref.at[place, group],
                    send_sem=sends.at[place, step],
                    recv_sem=recvs.at[place, step],
                    device_id=peer,
                    device_id_type=MESH,
                )
            )
            made[-1].start()

        def receive():
            for each in made:
                each.wait()
            total = store_ref[place, 0]
            for slot in range(1, n_group):
                total = total + store_ref[place, slot]
            return [spread(total[i : i + 1, :]) for i in range(3)]

        return receive

    def share_a(place, sums, squares, extra=None):
        return share(st_a, a_send, a_recv, place, sums, squares, extra)

    def share_c(place, sums, squares):
        return share(st_c, c_send, c_recv, place, sums, squares)

    def share_f(place, sums, squares):
        return share(st_f, f_send, f_recv, place, sums, squares)

    def coefs(total, squares, count, gain, bias):
        mean = total / count
        inverse = lax.rsqrt(squares / count - mean * mean + EPS)
        slope_a = gain * inverse
        return mean, inverse, slope_a, bias - mean * slope_a

    def back_coefs(total, cross, count, mean, inverse, slope_a):
        c3 = slope_a * inverse * cross / count
        return slope_a * total / count - mean * c3, c3

    def param(kind, place):
        top = 8 * kind
        if place < 2:
            return spread(params[top + place : top + place + 1, :])
        if place == 2:
            return spread(
                jnp.concatenate([params[top + 2 + i : top + 3 + i, :] for i in range(4)], axis=1)
            )
        low = spread(params[top + 6 : top + 7, 0:128])
        high = spread(params[top + 6 : top + 7, 128:256])
        if place == 3:
            return tiled(jnp.where(lane < 32, low, 0.0))
        if place == 4:
            return tiled(jnp.where((lane >= 32) & (lane < 64), low, 0.0))
        return jnp.where(lane < 64, pltpu.roll(low, 64, 1), pltpu.roll(high, 64, 1))

    bt[...] = jnp.zeros(bt.shape, BF)
    for tap in range(3):
        low = f_reduce[tap].astype(BF)
        for q in range(4):
            other = q + tap - 1
            if 0 <= other < 4:
                bt[32 * q : 32 * q + 32, 128 * other : 128 * other + 128] = low
    bt[128:160, 384:512] = f_reduce[0].astype(BF)
    bt[224:256, 0:128] = f_reduce[2].astype(BF)
    fe[...] = jnp.zeros(fe.shape, BF)
    for q in range(4):
        fe[32 * q : 32 * q + 32, 128 * q : 128 * q + 128] = f_expand[...].astype(BF)
    for tap in range(9):
        wide = jnp.concatenate([f_spatial[tap], zeros(32, 96)], axis=1)
        for q in range(4):
            fs[tap, 32 * q : 32 * q + 32, :] = (
                pltpu.roll(wide, 32 * q, 1) if q else wide
            ).astype(BF)

    ready("xn")

    def widen(number, carry):
        rows = chunk(number, 4 * 2 * line)
        zf[rows, :] = xn[rows, :].astype(F32)
        return carry

    loop(side // 2, widen)

    def pack(source, target):
        def step(number, carry):
            size = 2 * line
            start = pl.multiple_of(number * 4 * size, 16)
            for q in range(4):
                target[chunk(number, size), 128 * q : 128 * q + 128] = source[
                    pl.ds(start + q, size, stride=4), :
                ].astype(BF)
            return carry

        loop(side // 2, step)

    pack(zf, fp)

    for tap in range(5):
        ready(("wl", tap))
        wl[128 * tap : 128 * tap + 128, :] = lateral_stage(ds, tap)[...].astype(BF)

    def lower_reduce(tap):
        ready("wr%d" % tap)

        def step(number, carry):
            rows = chunk(number, 128)
            wr[tap, rows, :] = ds[rows, 256 * tap : 256 * tap + 256].astype(BF)
            return carry

        loop(8, step)

    lower_reduce(0)
    lower_reduce(2)
    ready("xs")

    def edges(number, carry):
        rows = chunk(number, half)
        set_pair(b1, rows, dot(xs[rows, :], wr[0]) + dot(fp[rows, 256:512], wl[0:256, :]))
        set_pair(b2, rows, dot(xs[rows, :], wr[2]))
        return carry

    def fast_first(number, carry):
        rows = chunk(number, half)
        both = dot_nt(fp[rows, :], bt[...])
        zfa[rows, :] = (three(both[:, :128]) * masks[0:8, 0:128]).reshape(half, 128)
        fx[rows, :] = both[:, 128:]
        return carry

    loop(2, fast_first)
    loop(2, edges)

    def send_halo(place, last, zero, last_fast, zero_fast):
        ends_ = pl.ds(frames - 1, pixels, stride=frames)
        heads = pl.ds(0, pixels, stride=frames)
        for part in range(2):
            hs[place, part, 0:pixels, :] = last[part, ends_, :].astype(BF)
            hs[place + 1, part, 0:pixels, :] = zero[part, heads, :].astype(BF)
        hs[place, 2, 0:pixels, :] = last_fast[ends_, :].astype(BF)
        hs[place + 1, 2, 0:pixels, :] = zero_fast[heads, :].astype(BF)
        made = []
        for way, other in enumerate((after, before)):
            made.append(
                pltpu.make_async_remote_copy(
                    src_ref=hs.at[place + way],
                    dst_ref=hr.at[place + way],
                    send_sem=h_send.at[place + way],
                    recv_sem=h_recv.at[place + way],
                    device_id=other,
                    device_id_type=MESH,
                )
            )
            made[-1].start()
        return made

    def take_halo(made, place, last, zero, cross):
        for each in made:
            each.wait()
        ends_ = pl.ds(frames - 1, pixels, stride=frames)
        heads = pl.ds(0, pixels, stride=frames)
        for part in range(2):
            last[part, ends_, :] = hr[place, part, 0:pixels, :].astype(F32)
            zero[part, heads, :] = hr[place + 1, part, 0:pixels, :].astype(F32)
        low = lax.broadcasted_iota(jnp.int32, (pixels, 128), 1) < 64
        return low, hr[place, 2, 0:pixels, :].astype(F32), hr[place + 1, 2, 0:pixels, :].astype(F32)

    hs[...] = jnp.zeros(hs.shape, BF)
    pl.semaphore_wait(barrier, n_group + 1)
    halo = send_halo(0, b1, b2, fx, fx)

    lower_reduce(1)

    def middle(number, carry):
        rows = chunk(number, half)
        total = dot(xs[rows, :], wr[1]) + dot(fp[rows, 0:384], wl[256:640, :])
        za[rows, :] = (three(total) * masks[0:8, 0:256]).reshape(half, 256)
        return carry

    loop(2, middle)
    for tap in range(9):
        ready(("ws", tap))
        ws[256 * tap : 256 * tap + 256, :] = spatial_stage(ds, tap)[...].astype(BF)
    for block in range(4):
        ready(("we", block))
        we[:, 256 * block : 256 * block + 256] = zb[256 * block : 256 * block + 256, :].astype(BF)
    sa[0] = jnp.zeros((line, 768), BF)
    sa[side + 1] = jnp.zeros((line, 768), BF)
    fa[0] = jnp.zeros((line, 384), BF)
    fa[side + 1] = jnp.zeros((line, 384), BF)

    low, from_before, from_after = take_halo(halo, 0, b1, b2, fx)
    ends_ = pl.ds(frames - 1, pixels, stride=frames)
    heads = pl.ds(0, pixels, stride=frames)
    fx[ends_, :] = jnp.where(low, from_before, fx[ends_, :])
    fx[heads, :] = jnp.where(low, fx[heads, :], from_after)

    def join(number, carry):
        rows = chunk(number, line)
        total = three(za[rows, :])
        total = total + masks[8:16, 0:256] * pltpu.roll(three(pair(b1, rows)), 1, 1)
        total = total + masks[16:24, 0:256] * pltpu.roll(three(pair(b2, rows)), frames - 1, 1)
        za[rows, :] = total.reshape(line, 256)
        return carry[0] + jnp.sum(total, axis=0), carry[1] + jnp.sum(total * total, axis=0)

    sums = loop(side, join, (zeros(8, 256), zeros(8, 256)))
    got_sa = share_a(0, *sums, extra=count_block)

    def join_fast(number, carry):
        rows = chunk(number, line)
        cross = three(fx[rows, :])
        moved = jnp.where(
            lane < 64,
            masks[8:16, 0:128] * pltpu.roll(cross, 1, 1),
            masks[16:24, 0:128] * pltpu.roll(cross, frames - 1, 1),
        )
        total = three(zfa[rows, :]) + moved
        zfa[rows, :] = total.reshape(line, 128)
        return carry[0] + jnp.sum(total, axis=0), carry[1] + jnp.sum(total * total, axis=0)

    sums = loop(side, join_fast, (zeros(8, 128), zeros(8, 128)))
    got_fa = share_f(0, *sums)

    def silu_of(value, slope_a, shift):
        norm = value * slope_a + shift
        return norm * sigmoid(norm)

    def shifted(ref, y, value, flip):
        width = value.shape[1]
        edge = zeros(frames, width)
        back = jnp.concatenate([edge, value[: line - frames]], axis=0).astype(BF)
        ahead = jnp.concatenate([value[frames:], edge], axis=0).astype(BF)
        ref[y + 1, :, 0:width] = ahead if flip else back
        ref[y + 1, :, width : 2 * width] = value.astype(BF)
        ref[y + 1, :, 2 * width : 3 * width] = back if flip else ahead

    def spatial(z_ref, pad_ref, weight, width, slope_a, shift, out_ref):
        def hide(y, carry):
            value = silu_of(three(z_ref[chunk(y, line), :]), slope_a, shift)
            value = value * masks[0:8, 0:width]
            shifted(pad_ref, y, value.reshape(line, width), False)
            return carry

        loop(side, hide)
        tall = side // 2

        def step(number, carry):
            total = zeros(half, width)
            for a in range(3):
                patch = pad_ref[pl.ds(number * tall + a, tall)].reshape(half, 3 * width)
                total = total + dot(patch, weight(a))
            out_ref[chunk(number, half), :] = total
            return carry[0] + fold(total), carry[1] + fold(total * total)

        return loop(2, step, (zeros(8, width), zeros(8, width)))

    sums, squares, count = got_sa()
    count = count[:, 0:128]
    fast_count = 4.0 * count
    counts = jnp.concatenate([count] * 8, axis=1)
    mean_sa, inv_sa, m_sa, s_sa = coefs(sums, squares, counts[:, :256], param(0, 0), param(1, 0))
    sums = spatial(za, sa, lambda a: ws[768 * a : 768 * a + 768, :], 256, m_sa, s_sa, zb)
    got_sb = share_a(1, *sums)

    sums, squares, _ = got_fa()
    mean_fa, inv_fa, m_fa, s_fa = coefs(
        tiled(sums), tiled(squares), fast_count, param(0, 3), param(1, 3)
    )
    sums = spatial(
        zfa, fa, lambda a: fs[3 * a : 3 * a + 3].reshape(384, 128), 128, m_fa, s_fa, zfb
    )
    got_fb = share_f(1, *sums)

    def hide_to(z_ref, target, width, slope_a, shift):
        def hide(y, carry):
            rows = chunk(y, line)
            value = silu_of(three(z_ref[rows, :]), slope_a, shift) * masks[0:8, 0:width]
            target[rows, :] = value.reshape(line, width).astype(BF)
            return carry

        loop(side, hide)

    sums, squares, _ = got_sb()
    mean_sb, inv_sb, m_sb, s_sb = coefs(sums, squares, counts[:, :256], param(0, 1), param(1, 1))
    hide_to(zb, hsb, 256, m_sb, s_sb)

    def expand(number, carry):
        rows = chunk(number, 2 * line)
        total = dot(hsb[rows, :], we[...])
        zc[rows, :] = total
        return carry[0] + fold(total), carry[1] + fold(total * total)

    sums = loop(side // 2, expand, (zeros(8, 1024), zeros(8, 1024)))
    got_sc = share_c(0, *sums)

    sums, squares, _ = got_fb()
    mean_fb, inv_fb, m_fb, s_fb = coefs(
        tiled(sums), tiled(squares), fast_count, param(0, 4), param(1, 4)
    )
    hide_to(zfb, hfb, 128, m_fb, s_fb)

    def unpacked(ref, number, size, value, add):
        start = pl.multiple_of(number * 4 * size, 16)
        for q in range(4):
            place = pl.ds(start + q, size, stride=4)
            piece = value[:, 128 * q : 128 * q + 128]
            ref[place, :] = ref[place, :] + piece if add else piece

    def four(value):
        return value[:, 0:128] + value[:, 128:256] + value[:, 256:384] + value[:, 384:512]

    def expand_fast(number, carry):
        size = 2 * line
        total = dot(hfb[chunk(number, size), :], fe[...])
        unpacked(zf, number, size, total, False)
        return carry[0] + four(fold(total)), carry[1] + four(fold(total * total))

    sums = loop(side // 2, expand_fast, (zeros(8, 128), zeros(8, 128)))
    got_fc = share_f(2, *sums)

    sums, squares, _ = got_sc()
    mean_sc, inv_sc, m_sc, s_sc = coefs(sums, squares, counts, param(0, 2), param(1, 2))
    offset_sc = mean_sc * inv_sc
    ready("cs")

    def finish_slow(y, carry):
        rows = chunk(y, line)
        z = three(zc[rows, :])
        norm = z * m_sc + s_sc + three(xs[rows, :].astype(F32))
        gate = sigmoid(norm)
        act = norm * gate
        mask = masks[0:8, :]
        grad = three(cs[rows, :].astype(F32)) * mask * (gate + act * (1.0 - gate))
        cs[rows, :] = (act * mask).reshape(line, 1024).astype(BF)
        ds[rows, :] = grad.reshape(line, 1024)
        cross = grad * (z * inv_sc - offset_sc)
        return carry[0] + jnp.sum(grad, axis=0), carry[1] + jnp.sum(cross, axis=0)

    sums = loop(side, finish_slow, (zeros(8, 1024), zeros(8, 1024)))
    back_sc = share_c(1, *sums)
    save_slow = pltpu.make_async_copy(cs, slow_out, store.at[0])
    save_slow.start()

    sums, squares, _ = got_fc()
    mean_fc, inv_fc, m_fc, s_fc = coefs(sums, squares, fast_count, param(0, 5), param(1, 5))
    offset_fc = mean_fc * inv_fc
    ready("cf")
    fast_line = 4 * line

    def quad(value):
        return value.reshape(-1, 4, 8, 128)

    def fold_quad(value):
        return jnp.sum(value.reshape(-1, 8, 128), axis=0)

    def finish_fast(y, carry):
        rows = chunk(y, fast_line)
        mask = masks[24:56, 0:128].reshape(4, 8, 128)
        z = quad(zf[rows, :])
        norm = z * m_fc + s_fc + quad(xn[rows, :].astype(F32))
        gate = sigmoid(norm)
        act = norm * gate
        grad = quad(cf[rows, :].astype(F32)) * mask * (gate + act * (1.0 - gate))
        cf[rows, :] = (act * mask).reshape(fast_line, 128).astype(BF)
        df[rows, :] = grad.reshape(fast_line, 128)
        cross = grad * (z * inv_fc - offset_fc)
        return carry[0] + fold_quad(grad), carry[1] + fold_quad(cross)

    sums = loop(side, finish_fast, (zeros(8, 128), zeros(8, 128)))
    back_fc = share_f(3, *sums)
    save_fast = pltpu.make_async_copy(cf, fast_out, store.at[1])
    save_fast.start()

    norm_out[...] = zeros(16, 256)
    total, cross, _ = back_sc()
    for block in range(4):
        cols = slice(256 * block, 256 * (block + 1))
        norm_out[2 + block : 3 + block, :] = cross[0:1, cols]
        norm_out[10 + block : 11 + block, :] = total[0:1, cols]
    c2, c3 = back_coefs(total, cross, counts, mean_sc, inv_sc, m_sc)
    save_slow.wait()

    def back_expand(y, carry, c2=c2, c3=c3):
        rows = chunk(y, line)
        grad = m_sc * three(ds[rows, :]) - masks[0:8, :] * (c2 + c3 * three(zc[rows, :]))
        cs[rows, :] = grad.reshape(line, 1024).astype(BF)
        return carry

    loop(side, back_expand)

    def slope_of(norm):
        gate = sigmoid(norm)
        return gate + norm * gate * (1.0 - gate)

    def through(z_ref, rows, back, slope_a, shift, inverse, offset):
        z = three(z_ref[rows, :])
        grad = three(back) * slope_of(z * slope_a + shift)
        cross = grad * (z * inverse - offset)
        return grad, jnp.sum(grad, axis=0), jnp.sum(cross, axis=0)

    def back_hidden(number, carry):
        rows = chunk(number, half)
        back = dot_nt(cs[rows, :], we[...])
        grad, one, two = through(zb, rows, back, m_sb, s_sb, inv_sb, mean_sb * inv_sb)
        set_pair(b1, rows, grad.reshape(half, 256))
        return carry[0] + one, carry[1] + two

    sums = loop(2, back_hidden, (zeros(8, 256), zeros(8, 256)))
    back_sb = share_a(2, *sums)
    h_t[...] = hsb[...].T
    for block in range(4):
        cols = slice(256 * block, 256 * (block + 1))
        gbuf[cols, :] = dot(h_t[...], cs[:, cols]).astype(BF)

    total_fc, cross_fc, _ = back_fc()
    c2, c3 = back_coefs(total_fc, cross_fc, fast_count, mean_fc, inv_fc, m_fc)

    def back_fast(y, carry, c2=c2, c3=c3):
        rows = chunk(y, fast_line)
        mask = masks[24:56, 0:128].reshape(4, 8, 128)
        grad = m_fc * quad(df[rows, :]) - mask * (c2 + c3 * quad(zf[rows, :]))
        zf[rows, :] = grad.reshape(fast_line, 128)
        return carry

    loop(side, back_fast)
    pack(zf, dzf)

    def back_hidden_fast(number, carry):
        rows = chunk(number, half)
        back = dot_nt(dzf[rows, :], fe[...])
        grad, one, two = through(zfb, rows, back, m_fb, s_fb, inv_fb, mean_fb * inv_fb)
        fx[rows, :] = grad.reshape(half, 128)
        return carry[0] + one, carry[1] + two

    sums = loop(2, back_hidden_fast, (zeros(8, 128), zeros(8, 128)))
    back_fb = share_f(4, *sums)
    wide = dot_tn(hfb[...], dzf[...])
    grad_fc = sum(wide[32 * q : 32 * q + 32, 128 * q : 128 * q + 128] for q in range(4))
    gbuf[TINY + 32 : TINY + 64, 128:256] = grad_fc.astype(BF)

    def back_spatial(dy, z_ref, pad_ref, width, slope_a, c2, c3):
        def step(y, carry):
            rows = chunk(y, line)
            grad = slope_a * three(dy(rows)) - masks[0:8, 0:width] * (c2 + c3 * three(z_ref[rows, :]))
            shifted(pad_ref, y, grad.reshape(line, width), True)
            return carry

        loop(side, step)

    def back_taps(pad_ref, weight, width, number):
        tall = side // 2
        total = zeros(half, width)
        for a in range(3):
            for b in range(3):
                patch = pad_ref[pl.ds(number * tall + 2 - a, tall), :, width * b : width * (b + 1)]
                total = total + dot_nt(patch.reshape(half, width), weight(3 * a + b))
        return total

    total, cross, _ = back_sb()
    norm_out[1:2, :] = cross[0:1, :]
    norm_out[9:10, :] = total[0:1, :]
    c2, c3 = back_coefs(total, cross, counts[:, :256], mean_sb, inv_sb, m_sb)
    h_t[...] = sa[1 : side + 1, :, 256:512].reshape(n_rows, 256).T
    back_spatial(lambda rows: pair(b1, rows), zb, sa, 256, m_sb, c2, c3)

    def back_first(number, carry):
        rows = chunk(number, half)
        back = back_taps(sa, lambda tap: ws[256 * tap : 256 * tap + 256, :], 256, number)
        grad, one, two = through(za, rows, back, m_sa, s_sa, inv_sa, mean_sa * inv_sa)
        set_pair(b1, rows, grad.reshape(half, 256))
        return carry[0] + one, carry[1] + two

    sums = loop(2, back_first, (zeros(8, 256), zeros(8, 256)))
    back_sa = share_a(3, *sums)

    def spatial_grad(tap, carry):
        for b in range(3):
            patch = sa[pl.ds(2 - tap, side), :, 256 * b : 256 * (b + 1)].reshape(n_rows, 256)
            place = pl.multiple_of(1024 + 768 * tap + 256 * b, 16)
            gbuf[pl.ds(place, 256), :] = dot(h_t[...], patch).astype(BF)
        return carry

    loop(3, spatial_grad)

    total_fb, cross_fb, _ = back_fb()
    total_fb, cross_fb = tiled(total_fb), tiled(cross_fb)
    c2, c3 = back_coefs(total_fb, cross_fb, fast_count, mean_fb, inv_fb, m_fb)
    hidden = fa[1 : side + 1, :, 128:256].reshape(n_rows, 128).T
    h_t[0:128, :] = hidden
    back_spatial(lambda rows: fx[rows, :], zfb, fa, 128, m_fb, c2, c3)

    def back_first_fast(number, carry):
        rows = chunk(number, half)
        back = back_taps(fa, lambda tap: fs[tap], 128, number)
        grad, one, two = through(zfa, rows, back, m_fa, s_fa, inv_fa, mean_fa * inv_fa)
        fx[rows, :] = grad.reshape(half, 128)
        return carry[0] + one, carry[1] + two

    sums = loop(2, back_first_fast, (zeros(8, 128), zeros(8, 128)))
    back_fa = share_f(5, *sums)
    lanes = lax.broadcasted_iota(jnp.int32, (32, 128), 1)
    tiles = [zeros(32, 128) for _ in range(3)]
    for a in range(3):
        patch = fa[2 - a : 2 - a + side].reshape(n_rows, 384)
        wide = dot(h_t[0:128, :], patch)
        for b in range(3):
            tap = 3 * a + b
            for q in range(4):
                piece = wide[32 * q : 32 * q + 32, 128 * b : 128 * b + 128]
                turn = (32 * (tap % 4) - 32 * q) % 128
                piece = pltpu.roll(piece, turn, 1) if turn else piece
                inside = (lanes >= 32 * (tap % 4)) & (lanes < 32 * (tap % 4) + 32)
                tiles[tap // 4] = tiles[tap // 4] + jnp.where(inside, piece, 0.0)
    gbuf[TINY + 64 : TINY + 96, 0:128] = tiles[0].astype(BF)
    gbuf[TINY + 64 : TINY + 96, 128:256] = tiles[1].astype(BF)
    gbuf[TINY + 96 : TINY + 128, 0:128] = tiles[2].astype(BF)
    gbuf[TINY + 96 : TINY + 128, 128:256] = jnp.zeros((32, 128), BF)

    total, cross, _ = back_sa()
    norm_out[0:1, :] = cross[0:1, :]
    norm_out[8:9, :] = total[0:1, :]
    c2, c3 = back_coefs(total, cross, counts[:, :256], mean_sa, inv_sa, m_sa)

    def back_one(y, carry, c2=c2, c3=c3):
        rows = chunk(y, line)
        grad = m_sa * three(pair(b1, rows)) - masks[0:8, 0:256] * (c2 + c3 * three(za[rows, :]))
        grad = grad.reshape(line, 256)
        set_pair(b1, rows, grad)
        set_pair(b2, rows, grad)
        cs[rows, 512:768] = grad.astype(BF)
        return carry

    loop(side, back_one)

    total_fa, cross_fa, _ = back_fa()
    total_fa, cross_fa = tiled(total_fa), tiled(cross_fa)
    c2, c3 = back_coefs(total_fa, cross_fa, fast_count, mean_fa, inv_fa, m_fa)
    for top, values in ((6, (cross_fa, cross_fb, cross_fc)), (14, (total_fa, total_fb, total_fc))):
        turned = pltpu.roll(values[2], 64, 1)
        left = jnp.where(lane < 32, values[0], jnp.where(lane < 64, values[1], turned))
        norm_out[top : top + 1, 0:128] = left[0:1]
        norm_out[top : top + 1, 128:256] = jnp.where(lane < 64, turned, 0.0)[0:1]

    def back_one_fast(y, carry, c2=c2, c3=c3):
        rows = chunk(y, line)
        grad = m_fa * three(fx[rows, :]) - masks[0:8, 0:128] * (c2 + c3 * three(zfa[rows, :]))
        grad = grad.reshape(line, 128)
        fy[rows, :] = grad
        dzf[rows, 0:128] = grad.astype(BF)
        return carry

    loop(side, back_one_fast)
    halo = send_halo(2, b2, b1, fy, fy)

    def reduce_grad_mid(number, carry):
        cols = pl.ds(pl.multiple_of(256 * number, 256), 256)
        place = pl.multiple_of(REDUCE + 1024 + 256 * number, 16)
        gbuf[pl.ds(place, 256), :] = dot_tn(xs[:, cols], cs[:, 512:768]).astype(BF)
        return carry

    loop(4, reduce_grad_mid)
    gbuf[LATERAL + 256 : LATERAL + 640, :] = dot_tn(fp[:, 0:384], cs[:, 512:768]).astype(BF)

    low, from_before, from_after = take_halo(halo, 2, b2, b1, fy)
    fy[ends_, :] = jnp.where(low, fy[ends_, :], from_before)
    fy[heads, :] = jnp.where(low, from_after, fy[heads, :])

    def neighbours(y, carry):
        rows = chunk(y, line)
        up = masks[16:24, 0:256] * pltpu.roll(three(pair(b1, rows)), frames - 1, 1)
        down = masks[8:16, 0:256] * pltpu.roll(three(pair(b2, rows)), 1, 1)
        cs[rows, 0:256] = up.reshape(line, 256).astype(BF)
        cs[rows, 256:512] = down.reshape(line, 256).astype(BF)
        cross = three(fy[rows, :])
        moved = jnp.where(
            lane < 64,
            masks[16:24, 0:128] * pltpu.roll(cross, frames - 1, 1),
            masks[8:16, 0:128] * pltpu.roll(cross, 1, 1),
        )
        moved = jnp.where((lane < 32) | (lane >= 96), moved, 0.0)
        dzf[rows, 128:256] = moved.reshape(line, 128).astype(BF)
        return carry

    loop(side, neighbours)

    def reduce_grad(number, carry):
        cols = pl.ds(pl.multiple_of(256 * number, 256), 256)
        both = dot_tn(xs[:, cols], cs[:, 0:512]).astype(BF)
        place = pl.multiple_of(REDUCE + 256 * number, 16)
        gbuf[pl.ds(place, 256), :] = both[:, 0:256]
        gbuf[pl.ds(place + 2048, 256), :] = both[:, 256:512]
        return carry

    loop(4, reduce_grad)
    gbuf[LATERAL : LATERAL + 256, :] = dot_tn(fp[:, 256:512], cs[:, 0:256]).astype(BF)
    wide = dot_tn(dzf[:, 0:256], fp[...])
    parts = [zeros(32, 128) for _ in range(3)]
    for tap in range(3):
        for q in range(4):
            other = q + tap - 1
            if 0 <= other < 4:
                parts[tap] = parts[tap] + wide[
                    32 * q : 32 * q + 32, 128 * other : 128 * other + 128
                ]
    parts[0] = parts[0] + wide[128:160, 384:512]
    parts[2] = parts[2] + wide[224:256, 0:128]
    gbuf[TINY : TINY + 32, 0:128] = parts[0].astype(BF)
    gbuf[TINY : TINY + 32, 128:256] = parts[1].astype(BF)
    gbuf[TINY + 32 : TINY + 64, 0:128] = parts[2].astype(BF)
    if gbuf.shape[0] > ROWS:
        gbuf[ROWS:, :] = jnp.zeros((gbuf.shape[0] - ROWS, 256), BF)
    save_g = pltpu.make_async_copy(gbuf, g_out, store.at[2])
    save_g.start()

    def input_grad(number, carry):
        rows = chunk(number, 2 * line)
        total = dot_nt(cs[rows, 0:256], wr[0])
        total = total + dot_nt(cs[rows, 512:768], wr[1])
        total = total + dot_nt(cs[rows, 256:512], wr[2])
        ds[rows, :] = ds[rows, :] + total
        return carry

    def input_grad_fast(number, carry):
        size = 2 * line
        rows = chunk(number, size)
        total = dot(dzf[rows, 0:256], bt[...])
        mid = dot_nt(cs[rows, 512:768], wl[256:640, :])
        up = dot_nt(cs[rows, 0:256], wl[0:256, :])
        total = total + jnp.concatenate([mid, zeros(size, 128)], axis=1)
        total = total + jnp.concatenate([zeros(size, 256), up], axis=1)
        unpacked(df, number, size, total, True)
        return carry

    loop(side // 2, input_grad_fast)
    save_df = pltpu.make_async_copy(df, fast_grad, store.at[3])
    save_df.start()
    loop(side // 2, input_grad)
    save_ds = pltpu.make_async_copy(ds, slow_grad, store.at[4])
    save_ds.start()
    save_fast.wait()
    save_g.wait()
    save_df.wait()
    save_ds.wait()


def spatial_stage(ref, tap):
    if tap == 8:
        return ref.at[0:256, 768:1024]
    top = 1024 + 256 * (tap // 4)
    return ref.at[top : top + 256, 256 * (tap % 4) : 256 * (tap % 4) + 256]


def lateral_stage(ref, tap):
    return ref.at[256 + 128 * tap : 384 + 128 * tap, 768:1024]


def block_call(mesh, frames, side, rows, operands):
    n_dp, n_group = mesh.shape["dp"], mesh.shape["group"]
    pixels = side * side
    n = pixels * frames
    line = side * frames
    dma = pltpu.SemaphoreType.DMA
    vmem = pltpu.VMEM
    shape = jax.ShapeDtypeStruct
    peers = n_group - 1
    return pl.pallas_call(
        partial(block_kernel, n_dp, n_group, frames, side),
        out_shape=(
            shape((n, 1024), BF),
            shape((4 * n, 128), BF),
            shape((n, 1024), F32),
            shape((4 * n, 128), F32),
            shape((rows, 256), BF),
            shape((16, 256), F32),
        ),
        in_specs=[ANYWHERE] * 4 + [SCALARS] * 2 + [ANYWHERE] * 4 + [WHOLE] * 4,
        out_specs=(ANYWHERE,) * 5 + (WHOLE,),
        scratch_shapes=[
            vmem((n, 1024), BF),
            vmem((n, 1024), BF),
            vmem((4 * n, 128), BF),
            vmem((4 * n, 128), BF),
            vmem((n, 512), BF),
            vmem((4 * n, 128), F32),
            vmem((4 * n, 128), F32),
            vmem((n, 1024), F32),
            vmem((n, 1024), F32),
            vmem((n, 256), F32),
            vmem((n, 256), F32),
            vmem((2, n, 128), F32),
            vmem((2, n, 128), F32),
            vmem((side + 2, line, 768), BF),
            vmem((side + 2, line, 384), BF),
            vmem((n, 256), BF),
            vmem((n, 128), BF),
            vmem((n, 128), F32),
            vmem((n, 128), F32),
            vmem((n, 128), F32),
            vmem((n, 128), F32),
            vmem((n, 512), BF),
            vmem((256, n), BF),
            vmem((3, 1024, 256), BF),
            vmem((9 * 256, 256), BF),
            vmem((256, 1024), BF),
            vmem((640, 256), BF),
            vmem((256, 512), BF),
            vmem((9, 128, 128), BF),
            vmem((128, 512), BF),
            vmem((rows, 256), BF),
            vmem((56, 1024), F32),
            vmem((4, 3, -(-pixels // 16) * 16, 128), BF),
            vmem((4, 3, -(-pixels // 16) * 16, 128), BF),
            vmem((4, n_group, 8, 256), F32),
            vmem((2, n_group, 8, 1024), F32),
            vmem((6, n_group, 8, 128), F32),
            dma((32,)),
            dma((5,)),
            dma((4,)),
            dma((4,)),
            dma((4, peers)),
            dma((4, peers)),
            dma((2, peers)),
            dma((2, peers)),
            dma((6, peers)),
            dma((6, peers)),
        ],
        compiler_params=pltpu.CompilerParams(
            collective_id=1, has_side_effects=True, vmem_limit_bytes=VMEM_LIMIT
        ),
        name="bottleneck",
    )(*operands)


def body(mesh, slow_in, fast_in, slow_cotangent, fast_cotangent, clip_start, clip_end, *rest):
    weights, moments_old, norms = rest[:7], rest[7:14], rest[14:]
    frames, side, slow_width = slow_in.shape[1], slow_in.shape[2], slow_in.shape[4]
    fast_frames, fast_width = fast_in.shape[1], fast_in.shape[4]
    rows = rows_total(mesh.shape["dp"] * mesh.shape["group"])

    def flat(array):
        return jnp.transpose(array[0], (1, 2, 0, 3)).reshape(-1, array.shape[4])

    def unflat(array, count):
        grid = array.reshape(side, side, count, array.shape[1])
        return jnp.transpose(grid, (2, 0, 1, 3))[None]

    def turn(arrays):
        return arrays[:4] + (jnp.swapaxes(arrays[4], 1, 2),) + arrays[5:]

    def wide(array):
        return jnp.pad(array, ((0, 0), (0, 2048 - array.shape[1]))).reshape(16, 256)

    turned = turn(weights)
    slow_out, fast_out, slow_grad, fast_grad, grads, norm_grad = block_call(
        mesh,
        frames,
        side,
        rows,
        (
            flat(slow_in),
            flat(fast_in),
            flat(slow_cotangent),
            flat(fast_cotangent),
            clip_start,
            clip_end,
            *turned,
            wide(norms[0]),
        ),
    )
    grads, norm_grad = reduce_all(mesh, grads, norm_grad)
    norm_grad = norm_grad.reshape(2, 2048)[:, : norms[0].shape[1]]
    weights_new, moments_new = muon(grads, turned, turn(moments_old))
    weights_new, moments_new = turn(tuple(weights_new)), turn(tuple(moments_new))
    params_new, first_new, second_new = adam_step(*norms, norm_grad)
    return (
        unflat(slow_out, frames),
        unflat(fast_out, fast_frames),
        unflat(slow_grad, frames),
        unflat(fast_grad, fast_frames),
        *weights_new,
        *moments_new,
        first_new,
        second_new,
        params_new,
    )


def solution(mesh):
    sharded = P("group", "dp", None, None, None)
    return jax.shard_map(
        partial(body, mesh),
        mesh=mesh,
        in_specs=(sharded,) * 4 + (P("group", None),) * 2 + (P(),) * 17,
        out_specs=(sharded,) * 4 + (P(),) * 17,
        check_vma=False,
    )
```

```python
from functools import partial
import math

import jax
import jax.numpy as jnp
from jax import lax
from jax.experimental import pallas as pl
from jax.experimental.pallas import tpu as pltpu
from jax.sharding import PartitionSpec as P

NS_STEPS = 5
STEP = 10


EPS = 1e-05
MU = 0.95
LR = 0.3
BETA_ONE = 0.9
BETA_TWO = 0.95
LR_NORM = 0.2
ADAM_EPS = 1e-08
NS_A = 3.4445
NS_B = -4.775
NS_C = 2.0315
F32 = jnp.float32
BF = jnp.bfloat16
MESH = pl.DeviceIdType.MESH
REDUCE_1 = 3328
LATERAL_2 = 4352
TINY = 4736
REDUCE_0 = 4864
LATERAL_0 = 5888
REDUCE_2 = 6144
ROWS = 7168
CUTS = (1024, 3072, 4096, 6144)
LOADS = 25
VMEM_LIMIT = 62 * 2**20
WHOLE = pl.BlockSpec(memory_space=pltpu.VMEM)
ANYWHERE = pl.BlockSpec(memory_space=pl.ANY)
SCALARS = pl.BlockSpec(memory_space=pltpu.SMEM)


def adam_step(params, first, second, grad):
    first_new = BETA_ONE * first + (1.0 - BETA_ONE) * grad
    second_new = BETA_TWO * second + (1.0 - BETA_TWO) * grad * grad
    corrected = first_new / (1.0 - BETA_ONE**STEP)
    params_new = params - LR_NORM * corrected / (
        jnp.sqrt(second_new / (1.0 - BETA_TWO**STEP)) + ADAM_EPS
    )
    return (params_new, first_new, second_new)


def rows_total(n_dp):
    unit = 256 * (n_dp // 2)
    return -(-ROWS // unit) * unit


def pieces_of(n_dp):
    unit = 256 * (n_dp // 2)
    cuts = [0] + [cut // unit * unit for cut in CUTS] + [rows_total(n_dp)]
    cuts = sorted(set(cuts))
    return [(low, high - low) for low, high in zip(cuts[:-1], cuts[1:])]


def orders_of(place):
    return (("x", "y", "z"), ("y", "x", "z"))


def stage_sizes(place, size, depth):
    rows, result = size // 4, []
    for axis in orders_of(place)[0]:
        rows = rows // depth if axis == "z" else rows // 2
        result.append((rows, depth - 1 if axis == "z" else 1))
    return result


def dot(left, right):
    return jnp.dot(left, right, preferred_element_type=F32)


def dot_nt(left, right):
    return lax.dot_general(left, right, (((1,), (1,)), ((), ())), preferred_element_type=F32)


def dot_tn(left, right):
    return lax.dot_general(left, right, (((0,), (0,)), ((), ())), preferred_element_type=F32)


def split(value):
    high = value.astype(BF)
    return high, (value - high.astype(F32)).astype(BF)


def dot_split(left, right):
    return dot(
        jnp.concatenate([left[0], left[0], left[1]], axis=1),
        jnp.concatenate([right[0], right[1], right[0]], axis=0),
    )


def gram_tn(value):
    low = value.astype(BF)
    return dot_tn(low, low)


def gram_nt(value):
    low = value.astype(BF)
    return dot_nt(low, low)


def eye(size, kept=None):
    row = lax.broadcasted_iota(jnp.int32, (size, size), 0)
    col = lax.broadcasted_iota(jnp.int32, (size, size), 1)
    return jnp.where(row == col, 1.0, 0.0).astype(F32)


def square_split(value):
    high, low = value
    cross = dot(high, low)
    return dot(high, high) + cross + cross.T


def newton_poly(a, square):
    return NS_A * eye(a.shape[0]) + NS_B * a + NS_C * square


def newton_first(chains):
    newton_middle(chains, True)


def newton_middle(chains, first=False):
    values = [a_ref[...] for a_ref, _ in chains]
    splits = [split(a) for a in values]
    squares = [square_split(each) for each in splits]
    polys = [newton_poly(a, square) for a, square in zip(values, squares)]
    fine = [a.shape[0] < 256 for a in values]
    polys = [split(poly) if each else poly.astype(BF) for poly, each in zip(polys, fine)]
    if first:
        products = [
            poly[0].astype(F32) + poly[1].astype(F32) if each else poly.astype(F32)
            for poly, each in zip(polys, fine)
        ]
    else:
        products = [
            dot(p_ref[...].astype(BF), poly[0] if each else poly)
            for (_, p_ref), poly, each in zip(chains, polys, fine)
        ]
    once = [
        dot_split(a, poly) if each else dot(a[0], poly) + dot(a[1], poly)
        for a, poly, each in zip(splits, polys, fine)
    ]
    once = [split(each) for each in once]
    twice = [
        dot_split(a, poly) if each else dot(poly, a[0]) + dot(poly, a[1])
        for a, poly, each in zip(once, polys, fine)
    ]
    for (a_ref, p_ref), a, product in zip(chains, twice, products):
        a_ref[...] = a
        p_ref[...] = product


def newton_last(chains):
    values = [a_ref[...] for a_ref, _ in chains]
    lows = [a.astype(BF) for a in values]
    squares = [dot(low, low) for low in lows]
    polys = [
        (NS_A * eye(a.shape[0]) + NS_B * a + NS_C * square).astype(BF)
        for a, square in zip(values, squares)
    ]
    products = [dot(p_ref[...].astype(BF), poly) for (_, p_ref), poly in zip(chains, polys)]
    for (_, p_ref), product in zip(chains, products):
        p_ref[...] = product


def newton_steps():
    return [newton_first] + [newton_middle] * (NS_STEPS - 2) + [newton_last]


def norm_of(gram, size):
    trace = jnp.sum(gram * eye(size))
    return 1.0 / (jnp.sqrt(trace) + 1e-07)


def muon_kernel(*refs):
    grads = refs[0]
    weight_in, moment_in, kept = refs[1:8], refs[8:15], refs[15:19]
    weight_out, moment_out, kept_out = refs[19:26], refs[26:33], refs[33:37]
    g_buf = refs[37]
    weight, moment, keep = refs[38:45], refs[45:52], refs[52:56]
    chain_a, chain_p, small_a, small_p, both_sum, wide_keep = refs[56:62]
    sem, g_sem, tap_sem, out_sem, keep_in, keep_out = refs[62:68]

    g_cuts = (0, 1024, REDUCE_1, LATERAL_2, TINY, REDUCE_0, LATERAL_0, REDUCE_2, ROWS)
    loads = {}
    for place, (low, high) in enumerate(zip(g_cuts[:-1], g_cuts[1:])):
        span = pl.ds(low, high - low)
        loads[low] = pltpu.make_async_copy(grads.at[span], g_buf.at[span], g_sem.at[place])
    loads_m = [None] + [
        pltpu.make_async_copy(moment_in[i], moment[i], sem.at[0, i]) for i in range(1, 7)
    ]
    loads_w = [pltpu.make_async_copy(weight_in[i], weight[i], sem.at[1, i]) for i in range(7)]
    taps_m = [
        pltpu.make_async_copy(moment_in[0].at[tap], moment[0].at[tap], tap_sem.at[tap])
        for tap in range(3)
    ]
    loads[0].start()
    loads_m[2].start()
    for tap, low in ((1, REDUCE_1), (0, REDUCE_0), (2, REDUCE_2)):
        loads[low].start()
        taps_m[tap].start()
    stores, moving = [], []
    for place, (source, target) in enumerate(zip(kept, keep)):
        rows = source.shape[0] // 2
        for part in range(2):
            span = pl.ds(rows * part, rows)
            made = pltpu.make_async_copy(
                source.at[span], target.at[span], keep_in.at[place, part]
            )
            moving.append((place, part, span, made))
    later = [loads[1024], loads_m[1], loads_m[3]]
    later += [loads[low] for low in (LATERAL_2, LATERAL_0, TINY)] + loads_m[4:7]
    later += [each[3] for each in moving] + [loads_w[i] for i in (2, 0, 1, 3, 4, 5, 6)]

    def start_next(count):
        for _ in range(min(count, len(later))):
            later.pop(0).start()

    def move(count):
        for _ in range(min(count, len(moving))):
            place, part, span, made = moving.pop(0)
            made.wait()
            source = keep[place]
            if source.dtype != kept_out[place].dtype:
                source = wide_keep
                size = keep[place].shape[0] // 14

                def widen(number, carry, place=place):
                    rows = pl.ds(pl.multiple_of(number * size, 16), size)
                    wide_keep[rows, :] = keep[place][rows, :].astype(F32)
                    return carry

                lax.fori_loop(7 * part, 7 * part + 7, widen, 0)
            stores.append(
                pltpu.make_async_copy(
                    source.at[span], kept_out[place].at[span], keep_out.at[place, part]
                )
            )
            stores[-1].start()

    def send(source, target, number, i):
        made = pltpu.make_async_copy(source, target, out_sem.at[number, i])
        made.start()
        stores.append(made)

    scales = []

    def close(i, number):
        send(moment[i], moment_out[i], 0, i)
        gram = both_sum[...]
        inverse = norm_of(gram, 256)
        scales.append(inverse)
        chain_a[number] = gram * (inverse * inverse)

    loads[0].wait()
    loads_m[2].wait()
    both = jnp.zeros((256, 256), F32)
    for block in range(4):
        cols = slice(256 * block, 256 * (block + 1))
        new = MU * moment[2][:, cols] + g_buf[256 * block : 256 * (block + 1), :].astype(F32)
        moment[2][:, cols] = new
        both = both + gram_nt(new)
    both_sum[...] = both
    close(2, 0)
    start_next(9)

    both_sum[...] = jnp.zeros((256, 256), F32)
    for tap, low in ((1, REDUCE_1), (0, REDUCE_0), (2, REDUCE_2)):
        loads[low].wait()
        taps_m[tap].wait()
        if tap == 0:
            start_next(4)
        if tap == 2:
            start_next(len(later))

        def step(part, carry, tap=tap, low=low):
            rows = pl.ds(pl.multiple_of(256 * part, 16), 256)
            span = pl.ds(pl.multiple_of(low + 256 * part, 16), 256)
            new = MU * moment[0][tap, rows, :] + g_buf[span, :].T.astype(F32)
            moment[0][tap, rows, :] = new
            both_sum[...] += gram_tn(new)
            return carry

        lax.fori_loop(0, 4, step, 0)
    close(0, 1)
    move(1)

    loads[1024].wait()
    loads_m[1].wait()
    both_sum[...] = jnp.zeros((256, 256), F32)

    def renew_spatial(tap, carry):
        span = pl.ds(pl.multiple_of(1024 + 256 * tap, 16), 256)
        new = MU * moment[1][tap] + g_buf[span, :].astype(F32)
        moment[1][tap] = new
        both_sum[...] += gram_tn(new)
        return carry

    lax.fori_loop(0, 9, renew_spatial, 0)
    close(1, 2)
    move(1)

    loads_m[3].wait()
    loads[LATERAL_2].wait()
    loads[LATERAL_0].wait()
    first = g_buf[LATERAL_0 : LATERAL_0 + 256, :].T
    second = g_buf[LATERAL_2 : LATERAL_2 + 256, :].T
    third = g_buf[LATERAL_2 + 256 : LATERAL_2 + 384, :]
    third = jnp.concatenate([third[:, :128], third[:, 128:]], axis=0).T
    turned = (first[:128], first[128:], second[:128], second[128:], third)
    both = jnp.zeros((256, 256), F32)
    for tap in range(5):
        new = MU * moment[3][tap] + turned[tap].astype(F32)
        moment[3][tap] = new
        both = both + gram_tn(new)
    both_sum[...] = both
    close(3, 3)
    move(1)

    loads[TINY].wait()
    for i in (4, 5, 6):
        loads_m[i].wait()
    tiny = g_buf[TINY : TINY + 128, :].astype(F32)
    reduce_new = []
    for tap in range(3):
        rows, cols = 32 * (tap // 2), 128 * (tap % 2)
        new = MU * moment[4][tap] + tiny[rows : rows + 32, cols : cols + 128]
        moment[4][tap] = new
        reduce_new.append(new)
    expand_new = MU * moment[6][...] + tiny[32:64, 128:256]
    moment[6][...] = expand_new
    spatial_new = []
    for tap in range(9):
        block = tiny[64 + 32 * (tap // 8) : 96 + 32 * (tap // 8), 128 * (tap % 8 // 4) :][:, :128]
        if tap % 4:
            block = pltpu.roll(block, 128 - 32 * (tap % 4), 1)
        new = MU * moment[5][tap] + block[:, :32]
        moment[5][tap] = new
        spatial_new.append(new)
    for i in (4, 5, 6):
        send(moment[i], moment_out[i], 0, i)
    grams = (
        sum(gram_tn(new) for new in spatial_new),
        sum(gram_nt(new) for new in reduce_new),
        gram_nt(expand_new),
    )
    tiny_scales = [norm_of(gram, 32) for gram in grams]
    blocks = []
    for place, (gram, inverse) in enumerate(zip(grams, tiny_scales)):
        wide = jnp.concatenate([gram * (inverse * inverse), jnp.zeros((32, 96), F32)], axis=1)
        blocks.append(pltpu.roll(wide, 32 * place, 1) if place else wide)
    blocks.append(jnp.zeros((32, 128), F32))
    small_a[...] = jnp.concatenate(blocks, axis=0)
    move(1)

    chains = [(chain_a.at[n], chain_p.at[n]) for n in range(4)] + [(small_a, small_p)]
    for step in newton_steps():
        step(chains)
        move(1)

    loads_w[2].wait()
    poly = (chain_p[0] * (2.0 * LR * scales[0])).astype(BF)
    for block in range(4):
        cols = slice(256 * block, 256 * (block + 1))
        change = dot(poly, moment[2][:, cols].astype(BF))
        weight[2][:, cols] = weight[2][:, cols] - change
    send(weight[2], weight_out[2], 1, 2)

    def apply(i, taps, number):
        loads_w[i].wait()
        poly = (chain_p[number] * (LR * scales[number])).astype(BF)

        each = 3 if taps == 9 else 1
        shape = (each,) + weight[i].shape[1:]

        def step(number, carry):
            span = pl.ds(number * each, each)
            rows = moment[i][span].reshape(-1, 256).astype(BF)
            weight[i][span] = weight[i][span] - dot(rows, poly).reshape(shape)
            return carry

        lax.fori_loop(0, taps // each, step, 0)
        send(weight[i], weight_out[i], 1, i)

    apply(0, 3, 1)
    apply(1, 9, 2)
    apply(3, 5, 3)
    for i in (4, 5, 6):
        loads_w[i].wait()
    tiny_p = small_p[...].astype(BF)
    for tap in range(9):
        change = dot(moment[5][tap].astype(BF), tiny_p[:32, :32])
        weight[5][tap] = weight[5][tap] - LR * tiny_scales[0] * change
    none = jnp.zeros((32, 128), BF)
    for tap in range(3):
        stack = jnp.concatenate([none, moment[4][tap].astype(BF), none, none], axis=0)
        weight[4][tap] = weight[4][tap] - LR * tiny_scales[1] * dot(tiny_p[32:64, :], stack)
    stack = jnp.concatenate([none, none, moment[6][...].astype(BF), none], axis=0)
    weight[6][...] = weight[6][...] - LR * 2.0 * tiny_scales[2] * dot(tiny_p[64:96, :], stack)
    for i in (4, 5, 6):
        send(weight[i], weight_out[i], 1, i)
    move(len(moving))
    for made in stores:
        made.wait()


def muon(grads, weights, moments_old, kept):
    shapes = [jax.ShapeDtypeStruct(each.shape, F32) for each in weights]
    types = (BF, BF, F32, F32)
    same = [jax.ShapeDtypeStruct(each.shape, kind) for each, kind in zip(kept, types)]
    dma = pltpu.SemaphoreType.DMA
    out = pl.pallas_call(
        muon_kernel,
        out_shape=shapes + shapes + same,
        in_specs=[ANYWHERE] * 19,
        out_specs=[ANYWHERE] * 18,
        scratch_shapes=[pltpu.VMEM(grads.shape, BF)]
        + [pltpu.VMEM(each.shape, F32) for each in weights] * 2
        + [pltpu.VMEM(each.shape, each.dtype) for each in kept]
        + [
            pltpu.VMEM((4, 256, 256), F32),
            pltpu.VMEM((4, 256, 256), F32),
            pltpu.VMEM((128, 128), F32),
            pltpu.VMEM((128, 128), F32),
            pltpu.VMEM((256, 256), F32),
            pltpu.VMEM(kept[2].shape, F32),
            dma((2, 7)),
            dma((8,)),
            dma((3,)),
            dma((2, 7)),
            dma((4, 2)),
            dma((4, 2)),
        ],
        compiler_params=pltpu.CompilerParams(vmem_limit_bytes=VMEM_LIMIT),
        name="muon",
    )(grads, *weights, *moments_old, *kept)
    return out[:7], out[7:14], out[14:]


def sigmoid(value):
    return 0.5 * jnp.tanh(0.5 * value) + 0.5


def spread(row):
    return jnp.broadcast_to(row, (8, row.shape[1]))


def tiled(value):
    value = value + pltpu.roll(value, 64, 1)
    return value + pltpu.roll(value, 32, 1)


def block_kernel(n_dp, n_group, frames, side, pieces, *refs):
    slow_in, fast_in, slow_cot, fast_cot, starts, ends = refs[:6]
    w_reduce, w_spatial, w_expand, w_lateral, f_reduce, f_spatial, f_expand, params = refs[6:14]
    slow_out, fast_out, slow_grad, fast_grad, g_out, norm_out = refs[14:20]
    (
        xs, cs, xn, cf, fp, zf, df, ds, zc, za, zb, b1, b2, sa, fa, hsb, hfb, zfa, zfb, fx,
        dzf, h_t, wr, ws, we, wl, bt, fs, fst, fe, gbuf, masks, links, fast_mask, hs, hr, fhs, fhr, st_a, st_c, st_f,
        load, store, h_send, h_recv, s_send, a_recv, c_recv, f_send, f_recv, summed, norm_loc, n_in, n_send, n_recv,
        g_save, *sums_refs,
    ) = refs[20:]
    pixels = side * side
    n_rows = pixels * frames
    line = side * frames
    dp, group = lax.axis_index("dp"), lax.axis_index("group")
    after = (lax.rem(dp + 1, n_dp), group)
    before = (lax.rem(dp + n_dp - 1, n_dp), group)
    peers = [(dp, lax.rem(group + step, n_group)) for step in range(1, n_group)]

    dp_peers = [(lax.rem(dp + step, n_dp), group) for step in range(1, n_dp)]
    barrier = pltpu.get_barrier_semaphore()
    for other in peers + dp_peers:
        pl.semaphore_signal(barrier, inc=1, device_id=other, device_id_type=MESH)

    loads = {}

    def fetch(name, source, target):
        loads[name] = pltpu.make_async_copy(source, target, load.at[len(loads) % LOADS])
        loads[name].start()

    def ready(*names):
        for name in names:
            loads[name].wait()

    half = n_rows // 2
    fetch("xn", fast_in, xn)
    for tap in range(5):
        fetch(("wl", tap), w_lateral.at[tap], lateral_stage(zc, tap))
    fetch("wr0", w_reduce.at[0], zc.at[0:1024, 0:256])
    fetch("xs", slow_in, xs)
    fetch("wr2", w_reduce.at[2], zc.at[0:1024, 512:768])
    fetch("wr1", w_reduce.at[1], zc.at[0:1024, 256:512])
    for tap in range(9):
        fetch(("ws", tap), w_spatial.at[tap], spatial_stage(zc, tap))
    for block in range(4):
        fetch(
            ("we", block),
            w_expand.at[:, 256 * block : 256 * (block + 1)],
            zb.at[256 * block : 256 * (block + 1)],
        )
    fetch("cs", slow_cot, cs)
    fetch("cf", fast_cot, cf)

    first = dp * frames
    row_id = lax.broadcasted_iota(jnp.int32, (frames, 128), 0)
    lane = lax.broadcasted_iota(jnp.int32, (8, 128), 1)

    def info(offset, rows):
        frame = first + offset + rows
        inside = jnp.zeros(rows.shape, jnp.int32)
        begun = jnp.zeros(rows.shape, jnp.int32)
        for slot in range(starts.shape[1]):
            open_ = frame >= starts[0, slot]
            begun = begun + jnp.where(open_, 1, 0)
            inside = jnp.where(open_ & (frame < ends[0, slot]), 1, inside)
        return inside, begun

    own, own_segment = info(0, row_id)
    valid = own.astype(F32)
    for offset, place in ((-1, 0), (1, 1)):
        near, near_segment = info(offset, row_id)
        both = jnp.where((own * near == 1) & (own_segment == near_segment), 1.0, 0.0)
        links[8 * place : 8 * place + 8, 0:128] = both.astype(F32)
        links[8 * place : 8 * place + 8, 128:256] = both.astype(F32)
    for block in range(8):
        masks[0:8, 128 * block : 128 * (block + 1)] = valid
    fast_id = lax.broadcasted_iota(jnp.int32, (4 * frames, 128), 0)
    fast_valid = info(0, fast_id >> 2)[0].astype(F32)
    fast_mask[...] = fast_valid
    count_local = jnp.sum(valid, axis=0, keepdims=True) * float(pixels)
    count_block = spread(count_local)

    def chunk(number, size):
        return pl.ds(pl.multiple_of(number * size, 16), size)

    def three(value):
        return value.reshape(-1, 8, value.shape[-1])

    def fold(value):
        return jnp.sum(three(value), axis=0)

    def pair(ref, rows):
        return jnp.concatenate([ref[0, rows, :], ref[1, rows, :]], axis=1)

    def set_pair(ref, rows, value):
        ref[0, rows, :] = value[:, :128]
        ref[1, rows, :] = value[:, 128:]

    def loop(count, body, carry=0):
        return lax.fori_loop(0, count, body, carry)

    def zeros(*shape):
        return jnp.zeros(shape, F32)

    depth = n_dp // 2
    core, side_y = lax.rem(group, 2), group // 2
    side_x, side_z = lax.rem(dp, 2), dp // 2
    pair_core = (dp, group + 1 - 2 * core)
    sides = {"x": side_x, "y": side_y}
    over = {"x": (dp + 1 - 2 * side_x, group), "y": (dp, group + 2 - 4 * side_y)}
    live = {}

    def at(ref, start, size):
        return ref.at[pl.ds(pl.multiple_of(start, 16), size)]

    def regions(place):
        start, size = pieces[place]
        base = start + core * (size // 2)
        sizes = stage_sizes(place, size, depth)
        result = []
        for way, axes in enumerate(orders_of(place)):
            offset = base + way * (size // 4)
            offsets = [offset]
            for axis, (rows, _) in zip(axes, sizes):
                offset = offset + (side_z if axis == "z" else sides[axis]) * rows
                offsets.append(offset)
            result.append(offsets)
        return base, sizes, result

    def begin(place):
        number = live[place][0]
        start, size = pieces[place]
        send, recv = sums_refs[5 * place + 3 : 5 * place + 5]
        base, sizes, offsets = regions(place)
        counts = [1] + [2 * count for _, count in sizes]
        counts = counts + counts[:0:-1] + [1]
        slot = sum(counts[:number])
        made = []

        def add_copy(source, target, device):
            made.append(
                pltpu.make_async_remote_copy(
                    src_ref=source,
                    dst_ref=target,
                    send_sem=send.at[len(made)],
                    recv_sem=recv.at[slot + len(made)],
                    device_id=device,
                    device_id_type=MESH,
                )
            )

        if number == 0:
            other = start + (1 - core) * (size // 2)
            add_copy(at(gbuf, other, size // 2), at(summed, other, size // 2), pair_core)
        elif number == 7:
            add_copy(at(summed, base, size // 2), at(summed, base, size // 2), pair_core)
        else:
            stage = number - 1 if number < 4 else 6 - number
            rows, _ = sizes[stage]
            into = sums_refs[5 * place + stage]
            for way, axes in enumerate(orders_of(place)):
                axis, before_ = axes[stage], offsets[way][stage]
                mine = at(summed, offsets[way][stage + 1], rows)
                if axis == "z":
                    for step in range(1, depth):
                        other = lax.rem(side_z + step, depth)
                        device = (other * 2 + side_x, group)
                        if number < 4:
                            source = at(gbuf, before_ + other * rows, rows)
                            add_copy(source, into.at[way, step - 1], device)
                        else:
                            add_copy(mine, mine, device)
                elif number < 4:
                    source = at(gbuf, before_ + (1 - sides[axis]) * rows, rows)
                    add_copy(source, into.at[way, 0], over[axis])
                else:
                    add_copy(mine, mine, over[axis])
        for each in made:
            each.start()
        live[place] = (number, made)

    def add_rows(start, size, target, sources):
        step_rows = math.gcd(size, 64)

        def step(number, carry):
            row = pl.multiple_of(number * step_rows, 16)
            rows = pl.ds(pl.multiple_of(start + row, 16), step_rows)
            total = gbuf[rows, :].astype(F32)
            for source in sources(row, step_rows, rows):
                total = total + source.astype(F32)
            target[rows, :] = total.astype(BF)
            return carry

        lax.fori_loop(0, size // step_rows, step, 0)

    def finish(place):
        number, made = live[place]
        start, size = pieces[place]
        base, sizes, offsets = regions(place)
        for each in made:
            each.wait()
        if number == 0:
            add_rows(base, size // 2, gbuf, lambda row, count, rows: [summed[rows, :]])
        elif number < 4:
            rows_, messages = sizes[number - 1]
            into = sums_refs[5 * place + number - 1]
            for way in range(2):
                add_rows(
                    offsets[way][number],
                    rows_,
                    summed if number == 3 else gbuf,
                    lambda row, count, rows, way=way: [
                        into[way, message, pl.ds(row, count), :] for message in range(messages)
                    ],
                )
        elif number == 7:
            save = pltpu.make_async_copy(
                summed.at[start : start + size], g_out.at[start : start + size], g_save.at[place]
            )
            save.start()
            saves.append(save)
        live[place] = (number + 1, None) if number < 7 else None

    saves, norm_made = [], []

    def share_norms():
        n_in[dp] = norm_loc[...]
        for step, peer in enumerate(dp_peers):
            norm_made.append(
                pltpu.make_async_remote_copy(
                    src_ref=n_in.at[dp],
                    dst_ref=n_in.at[dp],
                    send_sem=n_send.at[step],
                    recv_sem=n_recv.at[step],
                    device_id=peer,
                    device_id_type=MESH,
                )
            )
            norm_made[-1].start()

    def launch(ready_rows):
        for place, (start, size) in enumerate(pieces):
            if place not in live and start + size <= ready_rows:
                live[place] = (0, None)
                begin(place)

    def pump(*places):
        for place in places:
            if live.get(place):
                finish(place)
                if live[place]:
                    begin(place)


    row8 = lax.broadcasted_iota(jnp.int32, (8, 1), 0)

    def share(store_ref, sends, recvs, place, sums, squares, extra=None):
        top = jnp.sum(sums, axis=0, keepdims=True)
        second = jnp.sum(squares, axis=0, keepdims=True)
        block = jnp.where(row8 == 0, top, jnp.where(row8 == 1, second, 0.0))
        if extra is not None:
            block = jnp.where(row8 == 2, extra, block)
        store_ref[place, group] = block
        made = []
        for step, peer in enumerate(peers):
            made.append(
                pltpu.make_async_remote_copy(
                    src_ref=store_ref.at[place, group],
                    dst_ref=store_ref.at[place, group],
                    send_sem=sends.at[step],
                    recv_sem=recvs.at[place, step],
                    device_id=peer,
                    device_id_type=MESH,
                )
            )
            made[-1].start()

        def receive():
            for each in made:
                each.wait()
            total = store_ref[place, 0]
            for slot in range(1, n_group):
                total = total + store_ref[place, slot]
            return [spread(total[i : i + 1, :]) for i in range(3)]

        return receive

    def share_a(place, sums, squares):
        return share(st_a, s_send, a_recv, place, sums, squares)

    def share_c(place, sums, squares):
        return share(st_c, s_send, c_recv, place, sums, squares)

    def share_f(place, sums, squares, extra=None):
        return share(st_f, f_send, f_recv, place, sums, squares, extra)

    def coefs(total, squares, count, gain, bias):
        mean = total / count
        inverse = lax.rsqrt(squares / count - mean * mean + EPS)
        slope_a = gain * inverse
        return mean, inverse, slope_a, bias - mean * slope_a

    def back_coefs(total, cross, count, mean, inverse, slope_a):
        c3 = slope_a * inverse * cross / count
        return slope_a * total / count - mean * c3, c3

    def param(kind, place):
        top = 8 * kind
        if place < 2:
            return spread(params[top + place : top + place + 1, :])
        if place == 2:
            return spread(
                jnp.concatenate([params[top + 2 + i : top + 3 + i, :] for i in range(4)], axis=1)
            )
        low = spread(params[top + 6 : top + 7, 0:128])
        high = spread(params[top + 6 : top + 7, 128:256])
        if place == 3:
            return tiled(jnp.where(lane < 32, low, 0.0))
        if place == 4:
            return tiled(jnp.where((lane >= 32) & (lane < 64), low, 0.0))
        return jnp.where(lane < 64, pltpu.roll(low, 64, 1), pltpu.roll(high, 64, 1))

    bt[...] = jnp.zeros(bt.shape, BF)
    for tap in range(3):
        low = f_reduce[tap].astype(BF)
        for q in range(4):
            other = q + tap - 1
            if 0 <= other < 4:
                bt[32 * q : 32 * q + 32, 128 * other : 128 * other + 128] = low
    bt[128:160, 384:512] = f_reduce[0].astype(BF)
    bt[224:256, 0:128] = f_reduce[2].astype(BF)
    fe[...] = jnp.zeros(fe.shape, BF)
    for q in range(4):
        fe[32 * q : 32 * q + 32, 128 * q : 128 * q + 128] = f_expand[...].astype(BF)
    for tap in range(9):
        wide = jnp.concatenate([f_spatial[tap], zeros(32, 96)], axis=1)
        for q in range(4):
            fs[tap, 32 * q : 32 * q + 32, :] = (
                pltpu.roll(wide, 32 * q, 1) if q else wide
            ).astype(BF)
        side_b = 128 * (tap % 3)
        fst[tap // 3, side_b : side_b + 128, :] = fs[tap].T

    if gbuf.shape[0] > ROWS:
        gbuf[ROWS:, :] = jnp.zeros((gbuf.shape[0] - ROWS, 256), BF)

    ready("xn")

    def widen(number, carry):
        rows = chunk(number, 4 * 2 * line)
        zf[rows, :] = xn[rows, :].astype(F32)
        return carry

    loop(side // 2, widen)

    def pack(source, target):
        def step(number, carry):
            size = 2 * line
            start = pl.multiple_of(number * 4 * size, 16)
            for q in range(4):
                target[chunk(number, size), 128 * q : 128 * q + 128] = source[
                    pl.ds(start + q, size, stride=4), :
                ].astype(BF)
            return carry

        loop(side // 2, step)

    pack(zf, fp)

    for tap in range(5):
        ready(("wl", tap))
        wl[128 * tap : 128 * tap + 128, :] = lateral_stage(zc, tap)[...].astype(BF)

    def lower_reduce(tap):
        ready("wr%d" % tap)

        def step(number, carry):
            rows = chunk(number, 128)
            wr[tap, rows, :] = zc[rows, 256 * tap : 256 * tap + 256].astype(BF)
            return carry

        loop(8, step)

    def edges(number, carry):
        rows = chunk(number, half)
        set_pair(b1, rows, dot(xs[rows, :], wr[0]) + dot(fp[rows, 256:512], wl[0:256, :]))
        set_pair(b2, rows, dot(xs[rows, :], wr[2]))
        return carry

    def fast_first(number, carry):
        rows = chunk(number, half)
        both = dot_nt(fp[rows, :], bt[...])
        zfa[rows, :] = (three(both[:, :128]) * masks[0:8, 0:128]).reshape(half, 128)
        fx[rows, :] = both[:, 128:]
        return carry

    ends_ = pl.ds(frames - 1, pixels, stride=frames)
    heads = pl.ds(0, pixels, stride=frames)

    def halo_copy(ref, place, way, sems):
        made = pltpu.make_async_remote_copy(
            src_ref=ref[0].at[place + way],
            dst_ref=ref[1].at[place + way],
            send_sem=h_send.at[sems, place + way],
            recv_sem=h_recv.at[sems, place + way],
            device_id=(after, before)[way],
            device_id_type=MESH,
        )
        pl.when((dp < n_dp - 1, dp > 0)[way])(made.start)
        return made

    def halo_wait(made):
        @pl.when(dp < n_dp - 1)
        def _():
            made[0].wait_send()
            made[1].wait_recv()

        @pl.when(dp > 0)
        def _():
            made[1].wait_send()
            made[0].wait_recv()

    for way, edge in enumerate((0, n_dp - 1)):

        @pl.when(dp == edge)
        def _(way=way):
            for place in (way, 2 + way):
                hr[place] = jnp.zeros(hr.shape[1:], BF)
                fhr[place] = jnp.zeros(fhr.shape[1:], BF)

    def send_halo(place, last, zero):
        for part in range(2):
            hs[place, part, 0:pixels, :] = last[part, ends_, :].astype(BF)
            hs[place + 1, part, 0:pixels, :] = zero[part, heads, :].astype(BF)
        return [halo_copy((hs, hr), place, way, 0) for way in range(2)]

    def take_halo(made, place, last, zero):
        halo_wait(made)
        for part in range(2):
            last[part, ends_, :] = hr[place, part, 0:pixels, :].astype(F32)
            zero[part, heads, :] = hr[place + 1, part, 0:pixels, :].astype(F32)

    block_rows = -(-pixels // 64) * 16
    lanes_ = lax.broadcasted_iota(jnp.int32, (block_rows, 128), 1)
    fill = zeros(4 * block_rows - pixels, 128)

    def send_fast_halo(place, ref, first_lanes):
        for way, (rows, first_lane) in enumerate(zip((ends_, heads), first_lanes)):
            value = jnp.concatenate([ref[rows, :], fill], axis=0)
            total = zeros(block_rows, 128)
            for q in range(4):
                piece = value[block_rows * q : block_rows * (q + 1)]
                turn = (32 * q - first_lane) % 128
                piece = pltpu.roll(piece, turn, 1) if turn else piece
                total = jnp.where((lanes_ >= 32 * q) & (lanes_ < 32 * q + 32), piece, total)
            fhs[place + way] = total.astype(BF)
        return [halo_copy((fhs, fhr), place, way, 1) for way in range(2)]

    def take_fast_halo(made, place, first_lanes):
        halo_wait(made)
        result = []
        for way, first_lane in enumerate(first_lanes):
            value = fhr[place + way].astype(F32)
            pieces_ = []
            for q in range(4):
                turn = (first_lane - 32 * q) % 128
                piece = pltpu.roll(value, turn, 1) if turn else value
                keep = (lanes_ >= first_lane) & (lanes_ < first_lane + 32)
                pieces_.append(jnp.where(keep, piece, 0.0))
            result.append(jnp.concatenate(pieces_, axis=0)[:pixels])
        return result

    low = lax.broadcasted_iota(jnp.int32, (pixels, 128), 1) < 64

    def silu_of(value, slope_a, shift):
        norm = value * slope_a + shift
        return norm * sigmoid(norm)

    def slope_of(norm):
        gate = sigmoid(norm)
        return gate + norm * gate * (1.0 - gate)

    def shifted(ref, y, value, flip):
        width = value.shape[1]
        edge = zeros(frames, width)
        back = jnp.concatenate([edge, value[: line - frames]], axis=0).astype(BF)
        ahead = jnp.concatenate([value[frames:], edge], axis=0).astype(BF)
        ref[y + 1, :, 0:width] = ahead if flip else back
        ref[y + 1, :, width : 2 * width] = value.astype(BF)
        ref[y + 1, :, 2 * width : 3 * width] = back if flip else ahead

    def spatial(z_ref, pad_ref, weight, width, slope_a, shift, out_ref):
        def hide(y, carry):
            value = silu_of(three(z_ref[chunk(y, line), :]), slope_a, shift)
            value = value * masks[0:8, 0:width]
            shifted(pad_ref, y, value.reshape(line, width), False)
            return carry

        loop(side, hide)
        tall = side // 2

        def step(number, carry):
            total = zeros(half, width)
            for a in range(3):
                patch = pad_ref[pl.ds(number * tall + a, tall)].reshape(half, 3 * width)
                total = total + dot(patch, weight(a))
            out_ref[chunk(number, half), :] = total
            return carry[0] + fold(total), carry[1] + fold(total * total)

        return loop(2, step, (zeros(8, width), zeros(8, width)))

    def hide_to(z_ref, target, width, slope_a, shift):
        def hide(y, carry):
            rows = chunk(y, line)
            value = silu_of(three(z_ref[rows, :]), slope_a, shift) * masks[0:8, 0:width]
            target[rows, :] = value.reshape(line, width).astype(BF)
            return carry

        loop(side, hide)

    def unpacked(ref, number, size, value, add):
        start = pl.multiple_of(number * 4 * size, 16)
        for q in range(4):
            place = pl.ds(start + q, size, stride=4)
            piece = value[:, 128 * q : 128 * q + 128]
            ref[place, :] = ref[place, :] + piece if add else piece

    def four(value):
        return value[:, 0:128] + value[:, 128:256] + value[:, 256:384] + value[:, 384:512]

    fast_line = 4 * line

    def quad(value):
        return value.reshape(-1, 4, 8, 128)

    def fold_quad(value):
        return jnp.sum(value.reshape(-1, 8, 128), axis=0)

    def through(z_ref, rows, back, slope_a, shift):
        z = three(z_ref[rows, :])
        grad = three(back) * slope_of(z * slope_a + shift)
        return grad, jnp.sum(grad, axis=0), jnp.sum(grad * z, axis=0)

    def scaled_sums(sums, mean, inverse):
        return sums[0], inverse * (sums[1] - mean * sums[0])

    def back_spatial(dy, z_ref, pad_ref, width, slope_a, c2, c3):
        def step(y, carry):
            rows = chunk(y, line)
            grad = slope_a * three(dy(rows)) - masks[0:8, 0:width] * (c2 + c3 * three(z_ref[rows, :]))
            shifted(pad_ref, y, grad.reshape(line, width), True)
            return carry

        loop(side, step)

    loop(2, fast_first)
    hs[...] = jnp.zeros(hs.shape, BF)
    pl.semaphore_wait(barrier, n_group + n_dp - 2)
    fast_halo = send_fast_halo(0, fx, (0, 96))

    lower_reduce(0)
    lower_reduce(2)
    ready("xs")
    loop(2, edges)
    halo = send_halo(0, b1, b2)

    def middle(number, carry):
        rows = chunk(number, 2 * line)
        total = dot(xs[rows, :], wr[1]) + dot(fp[rows, 0:384], wl[256:640, :])
        za[rows, :] = (three(total) * masks[0:8, 0:256]).reshape(2 * line, 256)
        return carry

    middle_parts = side // 2
    from_before, from_after = take_fast_halo(fast_halo, 0, (0, 96))
    fx[ends_, :] = jnp.where(low, from_before, fx[ends_, :])
    fx[heads, :] = jnp.where(low, fx[heads, :], from_after)

    def join_fast(number, carry):
        rows = chunk(number, line)
        cross = three(fx[rows, :])
        moved = jnp.where(
            lane < 64,
            links[0:8, 0:128] * pltpu.roll(cross, 1, 1),
            links[8:16, 0:128] * pltpu.roll(cross, frames - 1, 1),
        )
        total = three(zfa[rows, :]) + moved
        zfa[rows, :] = total.reshape(line, 128)
        return carry[0] + jnp.sum(total, axis=0), carry[1] + jnp.sum(total * total, axis=0)

    sums = loop(side, join_fast, (zeros(8, 128), zeros(8, 128)))
    got_fa = share_f(0, *sums, extra=count_block)
    lower_reduce(1)
    lax.fori_loop(0, middle_parts // 2, middle, 0)

    for tap in range(9):
        ready(("ws", tap))
        ws[256 * tap : 256 * tap + 256, :] = spatial_stage(zc, tap)[...].astype(BF)
    for block in range(4):
        ready(("we", block))
        we[:, 256 * block : 256 * block + 256] = zb[256 * block : 256 * block + 256, :].astype(BF)
    sa[0] = jnp.zeros((line, 768), BF)
    sa[side + 1] = jnp.zeros((line, 768), BF)
    fa[0] = jnp.zeros((line, 384), BF)
    fa[side + 1] = jnp.zeros((line, 384), BF)

    sums, squares, count = got_fa()
    fast_count = 4.0 * count
    counts = jnp.concatenate([count] * 8, axis=1)
    mean_fa, inv_fa, m_fa, s_fa = coefs(
        tiled(sums), tiled(squares), fast_count, param(0, 3), param(1, 3)
    )
    sums = spatial(
        zfa, fa, lambda a: fs[3 * a : 3 * a + 3].reshape(384, 128), 128, m_fa, s_fa, zfb
    )
    got_fb = share_f(1, *sums)

    lax.fori_loop(middle_parts // 2, middle_parts, middle, 0)
    take_halo(halo, 0, b1, b2)

    def join(number, carry):
        rows = chunk(number, line)
        total = three(za[rows, :])
        total = total + links[0:8, 0:256] * pltpu.roll(three(pair(b1, rows)), 1, 1)
        total = total + links[8:16, 0:256] * pltpu.roll(three(pair(b2, rows)), frames - 1, 1)
        za[rows, :] = total.reshape(line, 256)
        return carry[0] + jnp.sum(total, axis=0), carry[1] + jnp.sum(total * total, axis=0)

    sums = loop(side, join, (zeros(8, 256), zeros(8, 256)))
    got_sa = share_a(0, *sums)

    sums, squares, _ = got_fb()
    mean_fb, inv_fb, m_fb, s_fb = coefs(
        tiled(sums), tiled(squares), fast_count, param(0, 4), param(1, 4)
    )
    hide_to(zfb, hfb, 128, m_fb, s_fb)

    def expand_fast(number, carry):
        size = 2 * line
        total = dot(hfb[chunk(number, size), :], fe[...])
        unpacked(zf, number, size, total, False)
        return carry[0] + four(fold(total)), carry[1] + four(fold(total * total))

    sums = loop(side // 2, expand_fast, (zeros(8, 128), zeros(8, 128)))
    got_fc = share_f(2, *sums)

    sums, squares, _ = got_sa()
    mean_sa, inv_sa, m_sa, s_sa = coefs(sums, squares, counts[:, :256], param(0, 0), param(1, 0))
    sums = spatial(za, sa, lambda a: ws[768 * a : 768 * a + 768, :], 256, m_sa, s_sa, zb)
    got_sb = share_a(1, *sums)

    sums, squares, _ = got_fc()
    mean_fc, inv_fc, m_fc, s_fc = coefs(sums, squares, fast_count, param(0, 5), param(1, 5))
    ready("cf")

    def finish_fast(y, carry):
        rows = chunk(y, fast_line)
        z = quad(zf[rows, :])
        norm = z * m_fc + s_fc + quad(xn[rows, :].astype(F32))
        gate = sigmoid(norm)
        kept = gate * fast_mask[...].reshape(4, 8, 128)
        act = norm * kept
        grad = quad(cf[rows, :].astype(F32)) * (kept + act * (1.0 - gate))
        cf[rows, :] = act.reshape(fast_line, 128).astype(BF)
        df[rows, :] = grad.reshape(fast_line, 128)
        return carry[0] + fold_quad(grad), carry[1] + fold_quad(grad * z)

    sums = loop(side, finish_fast, (zeros(8, 128), zeros(8, 128)))
    back_fc = share_f(3, *scaled_sums(sums, mean_fc, inv_fc))
    save_fast = pltpu.make_async_copy(cf, fast_out, store.at[1])
    save_fast.start()

    sums, squares, _ = got_sb()
    mean_sb, inv_sb, m_sb, s_sb = coefs(sums, squares, counts[:, :256], param(0, 1), param(1, 1))
    hide_to(zb, hsb, 256, m_sb, s_sb)

    def expand(number, carry):
        rows = chunk(number, 2 * line)
        total = dot(hsb[rows, :], we[...])
        zc[rows, :] = total
        return carry[0] + fold(total), carry[1] + fold(total * total)

    sums = loop(side // 2, expand, (zeros(8, 1024), zeros(8, 1024)))
    got_sc = share_c(0, *sums)

    norm_loc[...] = zeros(16, 256)
    total_fc, cross_fc, _ = back_fc()
    c2, c3 = back_coefs(total_fc, cross_fc, fast_count, mean_fc, inv_fc, m_fc)

    def back_fast(y, carry, c2=c2, c3=c3):
        rows = chunk(y, fast_line)
        mask = fast_mask[...].reshape(4, 8, 128)
        grad = m_fc * quad(df[rows, :]) - mask * (c2 + c3 * quad(zf[rows, :]))
        zf[rows, :] = grad.reshape(fast_line, 128)
        return carry

    loop(side, back_fast)
    pack(zf, dzf)

    def back_hidden_fast(number, carry):
        rows = chunk(number, half)
        back = dot_nt(dzf[rows, :], fe[...])
        grad, one, two = through(zfb, rows, back, m_fb, s_fb)
        fx[rows, :] = grad.reshape(half, 128)
        return carry[0] + one, carry[1] + two

    sums = loop(2, back_hidden_fast, (zeros(8, 128), zeros(8, 128)))
    back_fb = share_f(4, *scaled_sums(sums, mean_fb, inv_fb))

    sums, squares, _ = got_sc()
    mean_sc, inv_sc, m_sc, s_sc = coefs(sums, squares, counts, param(0, 2), param(1, 2))
    ready("cs")

    def finish_slow(y, carry):
        rows = chunk(y, line)
        z = three(zc[rows, :])
        norm = z * m_sc + s_sc + three(xs[rows, :].astype(F32))
        gate = sigmoid(norm)
        kept = gate * masks[0:8, :]
        act = norm * kept
        grad = three(cs[rows, :].astype(F32)) * (kept + act * (1.0 - gate))
        cs[rows, :] = act.reshape(line, 1024).astype(BF)
        ds[rows, :] = grad.reshape(line, 1024).astype(BF)
        return carry[0] + jnp.sum(grad, axis=0), carry[1] + jnp.sum(grad * z, axis=0)

    sums = loop(side, finish_slow, (zeros(8, 1024), zeros(8, 1024)))
    back_sc = share_c(1, *scaled_sums(sums, mean_sc, inv_sc))
    save_slow = pltpu.make_async_copy(cs, slow_out, store.at[0])
    save_slow.start()

    wide = dot_tn(hfb[...], dzf[...])
    grad_fc = sum(wide[32 * q : 32 * q + 32, 128 * q : 128 * q + 128] for q in range(4))
    gbuf[TINY + 32 : TINY + 64, 128:256] = grad_fc.astype(BF)

    total_fb, cross_fb, _ = back_fb()
    total_fb, cross_fb = tiled(total_fb), tiled(cross_fb)
    c2, c3 = back_coefs(total_fb, cross_fb, fast_count, mean_fb, inv_fb, m_fb)
    hfb[...] = fa[1 : side + 1, :, 128:256].reshape(n_rows, 128)
    back_spatial(lambda rows: fx[rows, :], zfb, fa, 128, m_fb, c2, c3)

    def back_first_fast(number, carry):
        rows = chunk(number, half)
        tall = side // 2
        back = zeros(half, 128)
        for a in range(3):
            patch = fa[pl.ds(number * tall + 2 - a, tall)].reshape(half, 384)
            back = back + dot(patch, fst[a])
        grad, one, two = through(zfa, rows, back, m_fa, s_fa)
        fx[rows, :] = grad.reshape(half, 128)
        return carry[0] + one, carry[1] + two

    sums = loop(2, back_first_fast, (zeros(8, 128), zeros(8, 128)))
    back_fa = share_f(5, *scaled_sums(sums, mean_fa, inv_fa))

    total, cross, _ = back_sc()
    for block in range(4):
        cols = slice(256 * block, 256 * (block + 1))
        norm_loc[2 + block : 3 + block, :] = cross[0:1, cols]
        norm_loc[10 + block : 11 + block, :] = total[0:1, cols]
    c2, c3 = back_coefs(total, cross, counts, mean_sc, inv_sc, m_sc)
    save_slow.wait()

    def back_expand(y, carry, c2=c2, c3=c3):
        rows = chunk(y, line)
        grad = m_sc * three(ds[rows, :].astype(F32)) - masks[0:8, :] * (c2 + c3 * three(zc[rows, :]))
        cs[rows, :] = grad.reshape(line, 1024).astype(BF)
        return carry

    loop(side, back_expand)

    def back_hidden(number, carry):
        rows = chunk(number, half)
        back = dot_nt(cs[rows, :], we[...])
        grad, one, two = through(zb, rows, back, m_sb, s_sb)
        set_pair(b1, rows, grad.reshape(half, 256))
        return carry[0] + one, carry[1] + two

    sums = loop(2, back_hidden, (zeros(8, 256), zeros(8, 256)))
    back_sb = share_a(2, *scaled_sums(sums, mean_sb, inv_sb))
    h_t[...] = hsb[...].T
    for block in range(4):
        cols = slice(256 * block, 256 * (block + 1))
        gbuf[cols, :] = dot(h_t[...], cs[:, cols]).astype(BF)
    launch(1024)

    total_fa, cross_fa, _ = back_fa()
    total_fa, cross_fa = tiled(total_fa), tiled(cross_fa)
    c2, c3 = back_coefs(total_fa, cross_fa, fast_count, mean_fa, inv_fa, m_fa)

    def back_one_fast(y, carry, c2=c2, c3=c3):
        rows = chunk(y, line)
        grad = m_fa * three(fx[rows, :]) - masks[0:8, 0:128] * (c2 + c3 * three(zfa[rows, :]))
        grad = grad.reshape(line, 128)
        zfb[rows, :] = grad
        dzf[rows, 0:128] = grad.astype(BF)
        return carry

    loop(side, back_one_fast)
    fast_halo = send_fast_halo(2, zfb, (96, 0))
    pump(0)

    total, cross, _ = back_sb()
    norm_loc[1:2, :] = cross[0:1, :]
    norm_loc[9:10, :] = total[0:1, :]
    c2, c3 = back_coefs(total, cross, counts[:, :256], mean_sb, inv_sb, m_sb)
    h_t[...] = sa[1 : side + 1, :, 256:512].reshape(n_rows, 256).T
    back_spatial(lambda rows: pair(b1, rows), zb, sa, 256, m_sb, c2, c3)

    def spatial_grad(tap, carry):
        for b in range(3):
            patch = sa[pl.ds(2 - tap, side), :, 256 * b : 256 * (b + 1)].reshape(n_rows, 256)
            place = pl.multiple_of(1024 + 768 * tap + 256 * b, 16)
            gbuf[pl.ds(place, 256), :] = dot(h_t[...], patch).astype(BF)
        return carry

    loop(3, spatial_grad)
    launch(REDUCE_1)
    pump(0)

    def back_first(number, carry):
        rows = chunk(number, half)
        tall = side // 2
        back = zeros(half, 256)
        for a in range(3):
            for b in range(3):
                tap = 3 * a + b
                patch = sa[pl.ds(number * tall + 2 - a, tall), :, 256 * b : 256 * (b + 1)]
                back = back + dot_nt(patch.reshape(half, 256), ws[256 * tap : 256 * tap + 256, :])
        grad, one, two = through(za, rows, back, m_sa, s_sa)
        set_pair(b1, rows, grad.reshape(half, 256))
        return carry[0] + one, carry[1] + two

    sums = loop(2, back_first, (zeros(8, 256), zeros(8, 256)))
    back_sa = share_a(3, *scaled_sums(sums, mean_sa, inv_sa))
    pump(1, 0)

    lanes = lax.broadcasted_iota(jnp.int32, (32, 128), 1)
    tiles = [zeros(32, 128) for _ in range(3)]
    for a in range(3):
        patch = fa[2 - a : 2 - a + side].reshape(n_rows, 384)
        wide = dot_tn(hfb[...], patch)
        for b in range(3):
            tap = 3 * a + b
            for q in range(4):
                piece = wide[32 * q : 32 * q + 32, 128 * b : 128 * b + 128]
                turn = (32 * (tap % 4) - 32 * q) % 128
                piece = pltpu.roll(piece, turn, 1) if turn else piece
                inside = (lanes >= 32 * (tap % 4)) & (lanes < 32 * (tap % 4) + 32)
                tiles[tap // 4] = tiles[tap // 4] + jnp.where(inside, piece, 0.0)
    gbuf[TINY + 64 : TINY + 96, 0:128] = tiles[0].astype(BF)
    gbuf[TINY + 64 : TINY + 96, 128:256] = tiles[1].astype(BF)
    gbuf[TINY + 96 : TINY + 128, 0:128] = tiles[2].astype(BF)
    gbuf[TINY + 96 : TINY + 128, 128:256] = jnp.zeros((32, 128), BF)


    total, cross, _ = back_sa()
    norm_loc[0:1, :] = cross[0:1, :]
    norm_loc[8:9, :] = total[0:1, :]
    c2, c3 = back_coefs(total, cross, counts[:, :256], mean_sa, inv_sa, m_sa)

    def back_one(y, carry, c2=c2, c3=c3):
        rows = chunk(y, line)
        grad = m_sa * three(pair(b1, rows)) - masks[0:8, 0:256] * (c2 + c3 * three(za[rows, :]))
        grad = grad.reshape(line, 256)
        set_pair(b1, rows, grad)
        set_pair(b2, rows, grad)
        cs[rows, 512:768] = grad.astype(BF)
        return carry

    loop(side, back_one)
    halo = send_halo(2, b2, b1)
    pump(0)
    for top, values in ((6, (cross_fa, cross_fb, cross_fc)), (14, (total_fa, total_fb, total_fc))):
        turned = pltpu.roll(values[2], 64, 1)
        left = jnp.where(lane < 32, values[0], jnp.where(lane < 64, values[1], turned))
        norm_loc[top : top + 1, 0:128] = left[0:1]
        norm_loc[top : top + 1, 128:256] = jnp.where(lane < 64, turned, 0.0)[0:1]
    share_norms()

    h_t[...] = cs[:, 512:768].T
    for block in range(4):
        cols = slice(256 * block, 256 * (block + 1))
        rows = slice(REDUCE_1 + 256 * block, REDUCE_1 + 256 * (block + 1))
        gbuf[rows, :] = dot(h_t[...], xs[:, cols]).astype(BF)
    wide = dot(h_t[...], fp[:, 0:384]).astype(BF)
    gbuf[LATERAL_2 : LATERAL_2 + 256, :] = wide[:, 0:256]
    gbuf[LATERAL_2 + 256 : LATERAL_2 + 384, 0:128] = wide[0:128, 256:384]
    gbuf[LATERAL_2 + 256 : LATERAL_2 + 384, 128:256] = wide[128:256, 256:384]
    launch(LATERAL_2 + 384)
    pump(1)

    def input_grad_mid(number, carry):
        rows = chunk(number, half)
        total = ds[rows, :].astype(F32) + dot_nt(cs[rows, 512:768], wr[1])
        ds[rows, :] = total.astype(BF)
        return carry

    loop(2, input_grad_mid)
    from_before, from_after = take_fast_halo(fast_halo, 2, (96, 0))
    zfb[ends_, :] = jnp.where(low, zfb[ends_, :], from_before)
    zfb[heads, :] = jnp.where(low, from_after, zfb[heads, :])

    def neighbours_fast(y, carry):
        rows = chunk(y, line)
        cross = three(zfb[rows, :])
        moved = jnp.where(
            lane < 64,
            links[8:16, 0:128] * pltpu.roll(cross, frames - 1, 1),
            links[0:8, 0:128] * pltpu.roll(cross, 1, 1),
        )
        moved = jnp.where((lane < 32) | (lane >= 96), moved, 0.0)
        dzf[rows, 128:256] = moved.reshape(line, 128).astype(BF)
        return carry

    loop(side, neighbours_fast)
    wide = dot_tn(dzf[:, 0:256], fp[...])
    parts = [zeros(32, 128) for _ in range(3)]
    for tap in range(3):
        for q in range(4):
            other = q + tap - 1
            if 0 <= other < 4:
                parts[tap] = parts[tap] + wide[
                    32 * q : 32 * q + 32, 128 * other : 128 * other + 128
                ]
    parts[0] = parts[0] + wide[128:160, 384:512]
    parts[2] = parts[2] + wide[224:256, 0:128]
    gbuf[TINY : TINY + 32, 0:128] = parts[0].astype(BF)
    gbuf[TINY : TINY + 32, 128:256] = parts[1].astype(BF)
    gbuf[TINY + 32 : TINY + 64, 0:128] = parts[2].astype(BF)

    pump(2)
    take_halo(halo, 2, b2, b1)
    pump(0)

    def neighbours(y, carry):
        rows = chunk(y, line)
        up = links[8:16, 0:256] * pltpu.roll(three(pair(b1, rows)), frames - 1, 1)
        down = links[0:8, 0:256] * pltpu.roll(three(pair(b2, rows)), 1, 1)
        cs[rows, 0:256] = up.reshape(line, 256).astype(BF)
        cs[rows, 256:512] = down.reshape(line, 256).astype(BF)
        return carry

    loop(side, neighbours)

    for side_lanes, low_row in ((0, REDUCE_0), (256, REDUCE_2)):
        h_t[...] = cs[:, side_lanes : side_lanes + 256].T
        for block in range(4):
            cols = slice(256 * block, 256 * (block + 1))
            rows = slice(low_row + 256 * block, low_row + 256 * (block + 1))
            gbuf[rows, :] = dot(h_t[...], xs[:, cols]).astype(BF)
        if side_lanes == 0:
            gbuf[LATERAL_0 : LATERAL_0 + 256, :] = dot(h_t[...], fp[:, 256:512]).astype(BF)
            launch(REDUCE_2)
            pump(1, 2)
    launch(gbuf.shape[0])
    pump(3)

    def input_grad(number, carry):
        rows = chunk(number, 2 * line)
        total = dot_nt(cs[rows, 0:256], wr[0])
        total = total + dot_nt(cs[rows, 256:512], wr[2])
        ds[rows, :] = (ds[rows, :].astype(F32) + total).astype(BF)
        return carry

    def input_grad_fast(number, carry):
        size = 2 * line
        rows = chunk(number, size)
        total = dot(dzf[rows, 0:256], bt[...])
        mid = dot_nt(cs[rows, 512:768], wl[256:640, :])
        up = dot_nt(cs[rows, 0:256], wl[0:256, :])
        total = total + jnp.concatenate([mid, zeros(size, 128)], axis=1)
        total = total + jnp.concatenate([zeros(size, 256), up], axis=1)
        unpacked(df, number, size, total, True)
        return carry

    parts_ = side // 2
    lax.fori_loop(0, parts_ // 2, input_grad_fast, 0)
    pump(4, 2)
    lax.fori_loop(parts_ // 2, parts_, input_grad_fast, 0)
    save_df = pltpu.make_async_copy(df, fast_grad, store.at[3])
    save_df.start()
    pump(1)
    lax.fori_loop(0, parts_ // 2, input_grad, 0)
    pump(3, 4, 2, 1)
    lax.fori_loop(parts_ // 2, parts_, input_grad, 0)
    save_ds = pltpu.make_async_copy(ds, slow_grad, store.at[4])
    save_ds.start()
    pump(3, 4, 1, 2, 0)

    while any(live.values()):
        pump(3, 4, 1, 2, 0)
    for each in norm_made:
        each.wait()
    total = n_in[0]
    for slot in range(1, n_dp):
        total = total + n_in[slot]
    norm_out[...] = total
    for each in saves:
        each.wait()
    save_fast.wait()
    save_df.wait()
    save_ds.wait()


def spatial_stage(ref, tap):
    if tap == 8:
        return ref.at[0:256, 768:1024]
    top = 1024 + 256 * (tap // 4)
    return ref.at[top : top + 256, 256 * (tap % 4) : 256 * (tap % 4) + 256]


def lateral_stage(ref, tap):
    return ref.at[256 + 128 * tap : 384 + 128 * tap, 768:1024]


def block_call(mesh, frames, side, rows, operands):
    n_dp, n_group = mesh.shape["dp"], mesh.shape["group"]
    pixels = side * side
    n = pixels * frames
    line = side * frames
    dma = pltpu.SemaphoreType.DMA
    vmem = pltpu.VMEM
    shape = jax.ShapeDtypeStruct
    peers = n_group - 1
    pieces, depth = pieces_of(n_dp), n_dp // 2
    sums_scratch = []
    for place, (_, size) in enumerate(pieces):
        sizes = stage_sizes(place, size, depth)
        sums_scratch += [vmem((2, count, each, 256), BF) for each, count in sizes]
        sums_scratch += [dma((2 * depth,)), dma((2 + 4 * sum(count for _, count in sizes),))]
    return pl.pallas_call(
        partial(block_kernel, n_dp, n_group, frames, side, pieces),
        out_shape=(
            shape((n, 1024), BF),
            shape((4 * n, 128), BF),
            shape((n, 1024), BF),
            shape((4 * n, 128), F32),
            shape((rows, 256), BF),
            shape((16, 256), F32),
        ),
        in_specs=[ANYWHERE] * 4 + [SCALARS] * 2 + [ANYWHERE] * 4 + [WHOLE] * 4,
        out_specs=(ANYWHERE,) * 5 + (WHOLE,),
        scratch_shapes=[
            vmem((n, 1024), BF),
            vmem((n, 1024), BF),
            vmem((4 * n, 128), BF),
            vmem((4 * n, 128), BF),
            vmem((n, 512), BF),
            vmem((4 * n, 128), F32),
            vmem((4 * n, 128), F32),
            vmem((n, 1024), BF),
            vmem((n, 1024), F32),
            vmem((n, 256), F32),
            vmem((n, 256), F32),
            vmem((2, n, 128), F32),
            vmem((2, n, 128), F32),
            vmem((side + 2, line, 768), BF),
            vmem((side + 2, line, 384), BF),
            vmem((n, 256), BF),
            vmem((n, 128), BF),
            vmem((n, 128), F32),
            vmem((n, 128), F32),
            vmem((n, 128), F32),
            vmem((n, 512), BF),
            vmem((256, n), BF),
            vmem((3, 1024, 256), BF),
            vmem((9 * 256, 256), BF),
            vmem((256, 1024), BF),
            vmem((640, 256), BF),
            vmem((256, 512), BF),
            vmem((9, 128, 128), BF),
            vmem((3, 384, 128), BF),
            vmem((128, 512), BF),
            vmem((rows, 256), BF),
            vmem((8, 1024), F32),
            vmem((16, 256), F32),
            vmem((32, 128), F32),
            vmem((4, 2, -(-pixels // 16) * 16, 128), BF),
            vmem((4, 2, -(-pixels // 16) * 16, 128), BF),
            vmem((4, -(-pixels // 64) * 16, 128), BF),
            vmem((4, -(-pixels // 64) * 16, 128), BF),
            vmem((4, n_group, 8, 256), F32),
            vmem((2, n_group, 8, 1024), F32),
            vmem((6, n_group, 8, 128), F32),
            dma((LOADS,)),
            dma((5,)),
            dma((2, 4)),
            dma((2, 4)),
            dma((peers,)),
            dma((4, peers)),
            dma((2, peers)),
            dma((peers,)),
            dma((6, peers)),
            vmem((rows, 256), BF),
            vmem((16, 256), F32),
            vmem((n_dp, 16, 256), F32),
            dma((n_dp - 1,)),
            dma((n_dp - 1,)),
            dma((len(pieces),)),
        ]
        + sums_scratch,
        compiler_params=pltpu.CompilerParams(
            collective_id=0, has_side_effects=True, vmem_limit_bytes=VMEM_LIMIT
        ),
        name="bottleneck",
    )(*operands)


def body(mesh, slow_in, fast_in, slow_cotangent, fast_cotangent, clip_start, clip_end, *rest):
    weights, moments_old, norms = rest[:7], rest[7:14], rest[14:]
    frames, side, slow_width = slow_in.shape[1], slow_in.shape[2], slow_in.shape[4]
    fast_frames, fast_width = fast_in.shape[1], fast_in.shape[4]
    rows = rows_total(mesh.shape["dp"])

    def flat(array):
        return jnp.transpose(array[0], (1, 2, 0, 3)).reshape(-1, array.shape[4])

    def unflat(array, count):
        grid = array.reshape(side, side, count, array.shape[1])
        return jnp.transpose(grid, (2, 0, 1, 3))[None]

    def turn(arrays):
        return arrays[:4] + (jnp.swapaxes(arrays[4], 1, 2),) + arrays[5:]

    def wide(array):
        return jnp.pad(array, ((0, 0), (0, 2048 - array.shape[1]))).reshape(16, 256)

    turned = turn(weights)
    *kept, grads, norm_grad = block_call(
        mesh,
        frames,
        side,
        rows,
        (
            flat(slow_in),
            flat(fast_in),
            flat(slow_cotangent),
            flat(fast_cotangent),
            clip_start,
            clip_end,
            *turned,
            wide(norms[0]),
        ),
    )
    norm_grad = norm_grad.reshape(2, 2048)[:, : norms[0].shape[1]]
    weights_new, moments_new, kept = muon(grads, turned, turn(moments_old), kept)
    slow_out, fast_out, slow_grad, fast_grad = kept
    weights_new, moments_new = turn(tuple(weights_new)), turn(tuple(moments_new))
    params_new, first_new, second_new = adam_step(*norms, norm_grad)
    return (
        unflat(slow_out, frames),
        unflat(fast_out, fast_frames),
        unflat(slow_grad, frames),
        unflat(fast_grad, fast_frames),
        *weights_new,
        *moments_new,
        first_new,
        second_new,
        params_new,
    )


def solution(mesh):
    sharded = P("group", "dp", None, None, None)
    return jax.shard_map(
        partial(body, mesh),
        mesh=mesh,
        in_specs=(sharded,) * 4 + (P("group", None),) * 2 + (P(),) * 17,
        out_specs=(sharded,) * 4 + (P(),) * 17,
        check_vma=False,
    )
```

```python
from functools import partial
import math

import jax
import jax.numpy as jnp
from jax import lax
from jax.experimental import pallas as pl
from jax.experimental.pallas import tpu as pltpu
from jax.sharding import PartitionSpec as P

NS_STEPS = 5
STEP = 10


EPS = 1e-05
MU = 0.95
LR = 0.3
BETA_ONE = 0.9
BETA_TWO = 0.95
LR_NORM = 0.2
ADAM_EPS = 1e-08
NS_A = 3.4445
NS_B = -4.775
NS_C = 2.0315
F32 = jnp.float32
BF = jnp.bfloat16
MESH = pl.DeviceIdType.MESH
REDUCE_1 = 3328
LATERAL_2 = 4352
TINY = 4736
REDUCE_0 = 4864
LATERAL_0 = 5888
REDUCE_2 = 6144
ROWS = 7168
CUTS = (1024, 3072, 4096, 6144)
LOADS = 25
PUMPS = {
    "a": (0,),
    "b": (1, 0),
    "c": (0,),
    "e": (1,),
    "f": (2,),
    "g": (0,),
    "h": (3, 1),
    "i": (4, 2),
    "j": (1,),
    "l": (3, 2, 4),
    "m": (1,),
    "n": (3, 4, 2, 1, 0),
    "z": (3, 4, 1, 2, 0),
}
VMEM_LIMIT = 62 * 2**20
WHOLE = pl.BlockSpec(memory_space=pltpu.VMEM)
ANYWHERE = pl.BlockSpec(memory_space=pl.ANY)
SCALARS = pl.BlockSpec(memory_space=pltpu.SMEM)


def adam_step(params, first, second, grad):
    first_new = BETA_ONE * first + (1.0 - BETA_ONE) * grad
    second_new = BETA_TWO * second + (1.0 - BETA_TWO) * grad * grad
    corrected = first_new / (1.0 - BETA_ONE**STEP)
    params_new = params - LR_NORM * corrected / (
        jnp.sqrt(second_new / (1.0 - BETA_TWO**STEP)) + ADAM_EPS
    )
    return (params_new, first_new, second_new)


def rows_total(n_dp):
    unit = 256 * (n_dp // 2)
    return -(-ROWS // unit) * unit


def pieces_of(n_dp):
    unit = 256 * (n_dp // 2)
    cuts = [0] + [cut // unit * unit for cut in CUTS] + [rows_total(n_dp)]
    cuts = sorted(set(cuts))
    return [(low, high - low) for low, high in zip(cuts[:-1], cuts[1:])]


def orders_of(place):
    return (("x", "y", "z"), ("y", "x", "z"))


def stage_sizes(place, size, depth):
    rows, result = size // 4, []
    for axis in orders_of(place)[0]:
        rows = rows // depth if axis == "z" else rows // 2
        result.append((rows, depth - 1 if axis == "z" else 1))
    return result


def dot(left, right):
    return jnp.dot(left, right, preferred_element_type=F32)


def dot_nt(left, right):
    return lax.dot_general(left, right, (((1,), (1,)), ((), ())), preferred_element_type=F32)


def dot_tn(left, right):
    return lax.dot_general(left, right, (((0,), (0,)), ((), ())), preferred_element_type=F32)


def split(value):
    high = value.astype(BF)
    return high, (value - high.astype(F32)).astype(BF)


def dot_split(left, right):
    return dot(
        jnp.concatenate([left[0], left[0], left[1]], axis=1),
        jnp.concatenate([right[0], right[1], right[0]], axis=0),
    )


def gram_tn(value):
    low = value.astype(BF)
    return dot_tn(low, low)


def gram_nt(value):
    low = value.astype(BF)
    return dot_nt(low, low)


def eye(size, kept=None):
    row = lax.broadcasted_iota(jnp.int32, (size, size), 0)
    col = lax.broadcasted_iota(jnp.int32, (size, size), 1)
    return jnp.where(row == col, 1.0, 0.0).astype(F32)


def square_split(value):
    high, low = value
    cross = dot(high, low)
    return dot(high, high) + cross + cross.T


def newton_poly(a, square):
    return NS_A * eye(a.shape[0]) + NS_B * a + NS_C * square


def newton_first(chains):
    newton_middle(chains, True)


def newton_middle(chains, first=False):
    values = [a_ref[...] for a_ref, _ in chains]
    splits = [split(a) for a in values]
    squares = [square_split(each) for each in splits]
    polys = [newton_poly(a, square) for a, square in zip(values, squares)]
    fine = [a.shape[0] < 256 for a in values]
    polys = [split(poly) if each else poly.astype(BF) for poly, each in zip(polys, fine)]
    if first:
        products = [
            poly[0].astype(F32) + poly[1].astype(F32) if each else poly.astype(F32)
            for poly, each in zip(polys, fine)
        ]
    else:
        products = [
            dot(p_ref[...].astype(BF), poly[0] if each else poly)
            for (_, p_ref), poly, each in zip(chains, polys, fine)
        ]
    once = [
        dot_split(a, poly) if each else dot(a[0], poly) + dot(a[1], poly)
        for a, poly, each in zip(splits, polys, fine)
    ]
    once = [split(each) for each in once]
    twice = [
        dot_split(a, poly) if each else dot(poly, a[0]) + dot(poly, a[1])
        for a, poly, each in zip(once, polys, fine)
    ]
    for (a_ref, p_ref), a, product in zip(chains, twice, products):
        a_ref[...] = a
        p_ref[...] = product


def newton_last(chains):
    values = [a_ref[...] for a_ref, _ in chains]
    lows = [a.astype(BF) for a in values]
    squares = [dot(low, low) for low in lows]
    polys = [
        (NS_A * eye(a.shape[0]) + NS_B * a + NS_C * square).astype(BF)
        for a, square in zip(values, squares)
    ]
    products = [dot(p_ref[...].astype(BF), poly) for (_, p_ref), poly in zip(chains, polys)]
    for (_, p_ref), product in zip(chains, products):
        p_ref[...] = product


def newton_steps():
    return [newton_first] + [newton_middle] * (NS_STEPS - 2) + [newton_last]


def norm_of(gram, size):
    trace = jnp.sum(gram * eye(size))
    return 1.0 / (jnp.sqrt(trace) + 1e-07)


def muon_kernel(*refs):
    grads, norm_grad, norms = refs[0], refs[1], refs[2:5]
    weight_in, moment_in, kept = refs[5:12], refs[12:19], refs[19:23]
    weight_out, moment_out, kept_out = refs[23:30], refs[30:37], refs[37:41]
    norms_out, g_buf = refs[41:44], refs[44]
    weight, moment, keep = refs[45:52], refs[52:59], refs[59:63]
    chain_a, chain_p, small_a, small_p, low_buf, wide_keep = refs[63:69]
    sem, g_sem, tap_sem, out_sem, keep_in, keep_out = refs[69:75]

    g_cuts = (0, 1024, REDUCE_1, LATERAL_2, TINY, REDUCE_0, LATERAL_0, REDUCE_2, ROWS)
    loads = {}
    for place, (low, high) in enumerate(zip(g_cuts[:-1], g_cuts[1:])):
        span = pl.ds(low, high - low)
        loads[low] = pltpu.make_async_copy(grads.at[span], g_buf.at[span], g_sem.at[place])
    loads_m = [None] + [
        pltpu.make_async_copy(moment_in[i], moment[i], sem.at[0, i]) for i in range(1, 7)
    ]
    loads_w = [pltpu.make_async_copy(weight_in[i], weight[i], sem.at[1, i]) for i in range(7)]
    taps_m = [
        pltpu.make_async_copy(moment_in[0].at[tap], moment[0].at[tap], tap_sem.at[tap])
        for tap in range(3)
    ]
    loads[0].start()
    loads_m[2].start()
    for tap, low in ((1, REDUCE_1), (0, REDUCE_0), (2, REDUCE_2)):
        loads[low].start()
        taps_m[tap].start()
    stores, moving = [], []
    for place, (source, target) in enumerate(zip(kept, keep)):
        rows = source.shape[0] // 2
        for part in range(2):
            span = pl.ds(rows * part, rows)
            made = pltpu.make_async_copy(
                source.at[span], target.at[span], keep_in.at[place, part]
            )
            moving.append((place, part, span, made))
    later = [loads[1024], loads_m[1], loads_m[3]]
    later += [loads[low] for low in (LATERAL_2, LATERAL_0, TINY)] + loads_m[4:7]
    later += [each[3] for each in moving] + [loads_w[i] for i in (2, 0, 1, 3, 4, 5, 6)]

    def start_next(count):
        for _ in range(min(count, len(later))):
            later.pop(0).start()

    def move(count):
        for _ in range(min(count, len(moving))):
            place, part, span, made = moving.pop(0)
            made.wait()
            source = keep[place]
            if source.dtype != kept_out[place].dtype:
                source = wide_keep
                size = keep[place].shape[0] // 14

                def widen(number, carry, place=place):
                    rows = pl.ds(pl.multiple_of(number * size, 16), size)
                    wide_keep[rows, :] = keep[place][rows, :].astype(F32)
                    return carry

                lax.fori_loop(7 * part, 7 * part + 7, widen, 0)
            stores.append(
                pltpu.make_async_copy(
                    source.at[span], kept_out[place].at[span], keep_out.at[place, part]
                )
            )
            stores[-1].start()

    def send(source, target, number, i):
        made = pltpu.make_async_copy(source, target, out_sem.at[number, i])
        made.start()
        stores.append(made)

    scales = []

    def close(i, number, gram):
        send(moment[i], moment_out[i], 0, i)
        inverse = norm_of(gram, 256)
        scales.append(inverse)
        chain_a[number] = gram * (inverse * inverse)

    loads[0].wait()
    loads_m[2].wait()
    gram = jnp.zeros((256, 256), F32)
    for block in range(4):
        cols, rows = (slice(256 * block, 256 * (block + 1)) for _ in range(2))
        new = MU * moment[2][:, cols] + g_buf[rows, :].astype(F32)
        moment[2][:, cols] = new
        low = new.astype(BF)
        low_buf[rows, :] = low
        gram = gram + dot_nt(low, low)
    close(2, 0, gram)
    start_next(9)

    gram = jnp.zeros((256, 256), F32)
    for tap, low_row in ((1, REDUCE_1), (0, REDUCE_0), (2, REDUCE_2)):
        loads[low_row].wait()
        taps_m[tap].wait()
        if tap == 0:
            start_next(4)
        if tap == 2:
            start_next(len(later))
        for part in range(4):
            rows = slice(256 * part, 256 * (part + 1))
            span = slice(low_row + 256 * part, low_row + 256 * (part + 1))
            new = MU * moment[0][tap, rows, :] + g_buf[span, :].T.astype(F32)
            moment[0][tap, rows, :] = new
            low_buf[span, :] = new.astype(BF)
        low = low_buf[low_row : low_row + 1024, :]
        gram = gram + dot_tn(low, low)
    close(0, 1, gram)
    move(1)

    loads[1024].wait()
    loads_m[1].wait()

    def renew_spatial(number, carry):
        taps = pl.ds(3 * number, 3)
        span = pl.ds(pl.multiple_of(1024 + 768 * number, 16), 768)
        new = MU * moment[1][taps].reshape(768, 256) + g_buf[span, :].astype(F32)
        moment[1][taps] = new.reshape(3, 256, 256)
        low = new.astype(BF)
        low_buf[span, :] = low
        chain_a[2] += dot_tn(low, low)
        return carry

    chain_a[2] = jnp.zeros((256, 256), F32)
    lax.fori_loop(0, 3, renew_spatial, 0)
    close(1, 2, chain_a[2])
    move(1)

    loads_m[3].wait()
    loads[LATERAL_2].wait()
    loads[LATERAL_0].wait()
    first = g_buf[LATERAL_0 : LATERAL_0 + 256, :].T
    second = g_buf[LATERAL_2 : LATERAL_2 + 256, :].T
    third = g_buf[LATERAL_2 + 256 : LATERAL_2 + 384, :]
    third = jnp.concatenate([third[:, :128], third[:, 128:]], axis=0).T
    turned = jnp.concatenate([first, second, third], axis=0).astype(F32)
    new = MU * moment[3][...].reshape(640, 256) + turned
    moment[3][...] = new.reshape(5, 128, 256)
    lateral_low = new.astype(BF)
    close(3, 3, dot_tn(lateral_low, lateral_low))
    move(1)

    for kind in range(2):
        for part in range(7):
            lanes = slice(256 * part, min(256 * (part + 1), norms[0].shape[1]))
            row, width = slice(kind, kind + 1), lanes.stop - lanes.start
            grad = norm_grad[8 * kind + part : 8 * kind + part + 1, :width]
            news = adam_step(*(each[row, lanes] for each in norms), grad)
            for target, new in zip(norms_out, news):
                target[row, lanes] = new

    loads[TINY].wait()
    for i in (4, 5, 6):
        loads_m[i].wait()
    tiny = g_buf[TINY : TINY + 128, :].astype(F32)
    reduce_new = []
    for tap in range(3):
        rows, cols = 32 * (tap // 2), 128 * (tap % 2)
        new = MU * moment[4][tap] + tiny[rows : rows + 32, cols : cols + 128]
        moment[4][tap] = new
        reduce_new.append(new)
    expand_new = MU * moment[6][...] + tiny[32:64, 128:256]
    moment[6][...] = expand_new
    spatial_new = []
    for tap in range(9):
        block = tiny[64 + 32 * (tap // 8) : 96 + 32 * (tap // 8), 128 * (tap % 8 // 4) :][:, :128]
        if tap % 4:
            block = pltpu.roll(block, 128 - 32 * (tap % 4), 1)
        new = MU * moment[5][tap] + block[:, :32]
        moment[5][tap] = new
        spatial_new.append(new)
    for i in (4, 5, 6):
        send(moment[i], moment_out[i], 0, i)
    grams = (
        sum(gram_tn(new) for new in spatial_new),
        sum(gram_nt(new) for new in reduce_new),
        gram_nt(expand_new),
    )
    tiny_scales = [norm_of(gram, 32) for gram in grams]
    blocks = []
    for place, (gram, inverse) in enumerate(zip(grams, tiny_scales)):
        wide = jnp.concatenate([gram * (inverse * inverse), jnp.zeros((32, 96), F32)], axis=1)
        blocks.append(pltpu.roll(wide, 32 * place, 1) if place else wide)
    blocks.append(jnp.zeros((32, 128), F32))
    small_a[...] = jnp.concatenate(blocks, axis=0)
    move(1)

    chains = [(chain_a.at[n], chain_p.at[n]) for n in range(4)] + [(small_a, small_p)]
    for step in newton_steps():
        step(chains)
        move(1)

    loads_w[2].wait()
    poly = (chain_p[0] * (2.0 * LR * scales[0])).astype(BF)
    for block in range(4):
        cols, rows = (slice(256 * block, 256 * (block + 1)) for _ in range(2))
        weight[2][:, cols] = weight[2][:, cols] - dot(poly, low_buf[rows, :])
    send(weight[2], weight_out[2], 1, 2)

    loads_w[0].wait()
    poly = (chain_p[1] * (LR * scales[1])).astype(BF)
    for tap, low_row in enumerate((REDUCE_0, REDUCE_1, REDUCE_2)):
        low = low_buf[low_row : low_row + 1024, :]
        weight[0][tap] = weight[0][tap] - dot(low, poly)
    send(weight[0], weight_out[0], 1, 0)

    loads_w[1].wait()
    poly = (chain_p[2] * (LR * scales[2])).astype(BF)

    def apply_spatial(number, carry):
        taps = pl.ds(3 * number, 3)
        span = pl.ds(pl.multiple_of(1024 + 768 * number, 16), 768)
        change = dot(low_buf[span, :], poly).reshape(3, 256, 256)
        weight[1][taps] = weight[1][taps] - change
        return carry

    lax.fori_loop(0, 3, apply_spatial, 0)
    send(weight[1], weight_out[1], 1, 1)

    loads_w[3].wait()
    poly = (chain_p[3] * (LR * scales[3])).astype(BF)
    weight[3][...] = weight[3][...] - dot(lateral_low, poly).reshape(5, 128, 256)
    send(weight[3], weight_out[3], 1, 3)
    for i in (4, 5, 6):
        loads_w[i].wait()
    tiny_p = small_p[...].astype(BF)
    for tap in range(9):
        change = dot(moment[5][tap].astype(BF), tiny_p[:32, :32])
        weight[5][tap] = weight[5][tap] - LR * tiny_scales[0] * change
    none = jnp.zeros((32, 128), BF)
    for tap in range(3):
        stack = jnp.concatenate([none, moment[4][tap].astype(BF), none, none], axis=0)
        weight[4][tap] = weight[4][tap] - LR * tiny_scales[1] * dot(tiny_p[32:64, :], stack)
    stack = jnp.concatenate([none, none, moment[6][...].astype(BF), none], axis=0)
    weight[6][...] = weight[6][...] - LR * 2.0 * tiny_scales[2] * dot(tiny_p[64:96, :], stack)
    for i in (4, 5, 6):
        send(weight[i], weight_out[i], 1, i)
    move(len(moving))
    for made in stores:
        made.wait()


def muon(grads, norm_grad, norms, weights, moments_old, kept):
    shapes = [jax.ShapeDtypeStruct(each.shape, F32) for each in weights]
    types = (BF, BF, F32, F32)
    same = [jax.ShapeDtypeStruct(each.shape, kind) for each, kind in zip(kept, types)]
    dma = pltpu.SemaphoreType.DMA
    out = pl.pallas_call(
        muon_kernel,
        out_shape=shapes + shapes + same + [jax.ShapeDtypeStruct(norms[0].shape, F32)] * 3,
        in_specs=[ANYWHERE] + [WHOLE] * 4 + [ANYWHERE] * 18,
        out_specs=[ANYWHERE] * 18 + [WHOLE] * 3,
        scratch_shapes=[pltpu.VMEM(grads.shape, BF)]
        + [pltpu.VMEM(each.shape, F32) for each in weights] * 2
        + [pltpu.VMEM(each.shape, each.dtype) for each in kept]
        + [
            pltpu.VMEM((4, 256, 256), F32),
            pltpu.VMEM((4, 256, 256), F32),
            pltpu.VMEM((128, 128), F32),
            pltpu.VMEM((128, 128), F32),
            pltpu.VMEM(grads.shape, BF),
            pltpu.VMEM(kept[2].shape, F32),
            dma((2, 7)),
            dma((8,)),
            dma((3,)),
            dma((2, 7)),
            dma((4, 2)),
            dma((4, 2)),
        ],
        compiler_params=pltpu.CompilerParams(vmem_limit_bytes=VMEM_LIMIT),
        name="muon",
    )(grads, norm_grad, *norms, *weights, *moments_old, *kept)
    return out[:7], out[7:14], out[14:18], out[18:]


def sigmoid(value):
    return 0.5 * jnp.tanh(0.5 * value) + 0.5


def spread(row):
    return jnp.broadcast_to(row, (8, row.shape[1]))


def tiled(value):
    value = value + pltpu.roll(value, 64, 1)
    return value + pltpu.roll(value, 32, 1)


def block_kernel(n_dp, n_group, frames, side, pieces, *refs):
    slow_in, fast_in, slow_cot, fast_cot, starts, ends = refs[:6]
    w_reduce, w_spatial, w_expand, w_lateral, f_reduce, f_spatial, f_expand, params = refs[6:14]
    slow_out, fast_out, slow_grad, fast_grad, g_out, norm_out = refs[14:20]
    (
        xs, cs, xn, cf, fp, zf, df, ds, zc, za, zb, b1, b2, sa, fa, hsb, hfb, zfa, zfb, fx,
        dzf, h_t, wr, ws, we, wl, bt, fs, fst, fe, gbuf, masks, links, fast_mask, xh_in, hs, hr, fhs, fhr, st_a, st_c, st_f,
        load, store, h_send, h_recv, s_send, a_recv, c_recv, f_send, f_recv, summed, norm_loc, n_in, n_send, n_recv,
        g_save, *sums_refs,
    ) = refs[20:]
    pixels = side * side
    n_rows = pixels * frames
    line = side * frames
    dp, group = lax.axis_index("dp"), lax.axis_index("group")
    after = (lax.rem(dp + 1, n_dp), group)
    before = (lax.rem(dp + n_dp - 1, n_dp), group)
    peers = [(dp, lax.rem(group + step, n_group)) for step in range(1, n_group)]

    dp_peers = [(lax.rem(dp + step, n_dp), group) for step in range(1, n_dp)]
    barrier = pltpu.get_barrier_semaphore()
    for other in peers + dp_peers:
        pl.semaphore_signal(barrier, inc=1, device_id=other, device_id_type=MESH)

    loads = {}

    def fetch(name, source, target):
        loads[name] = pltpu.make_async_copy(source, target, load.at[len(loads) % LOADS])
        loads[name].start()

    def ready(*names):
        for name in names:
            loads[name].wait()

    half = n_rows // 2
    fetch("xn", fast_in, xn)
    for tap in range(5):
        fetch(("wl", tap), w_lateral.at[tap], lateral_stage(zc, tap))
    fetch("wr0", w_reduce.at[0], zc.at[0:1024, 0:256])
    fetch("xs", slow_in, xs)
    fetch("wr2", w_reduce.at[2], zc.at[0:1024, 512:768])
    fetch("wr1", w_reduce.at[1], zc.at[0:1024, 256:512])
    for tap in range(9):
        fetch(("ws", tap), w_spatial.at[tap], spatial_stage(zc, tap))
    for block in range(4):
        fetch(
            ("we", block),
            w_expand.at[:, 256 * block : 256 * (block + 1)],
            zb.at[256 * block : 256 * (block + 1)],
        )
    fetch("cs", slow_cot, cs)
    fetch("cf", fast_cot, cf)

    first = dp * frames
    row_id = lax.broadcasted_iota(jnp.int32, (frames, 128), 0)
    lane = lax.broadcasted_iota(jnp.int32, (8, 128), 1)

    def info(offset, rows):
        frame = first + offset + rows
        inside = jnp.zeros(rows.shape, jnp.int32)
        begun = jnp.zeros(rows.shape, jnp.int32)
        for slot in range(starts.shape[1]):
            open_ = frame >= starts[0, slot]
            begun = begun + jnp.where(open_, 1, 0)
            inside = jnp.where(open_ & (frame < ends[0, slot]), 1, inside)
        return inside, begun

    own, own_segment = info(0, row_id)
    valid = own.astype(F32)
    for offset, place in ((-1, 0), (1, 1)):
        near, near_segment = info(offset, row_id)
        both = jnp.where((own * near == 1) & (own_segment == near_segment), 1.0, 0.0)
        links[8 * place : 8 * place + 8, 0:128] = both.astype(F32)
        links[8 * place : 8 * place + 8, 128:256] = both.astype(F32)
        inner = jnp.where(row_id == (0, frames - 1)[place], 0.0, both).astype(F32)
        links[16 + 8 * place : 24 + 8 * place, 0:128] = inner
        links[16 + 8 * place : 24 + 8 * place, 128:256] = inner
    for block in range(8):
        masks[0:8, 128 * block : 128 * (block + 1)] = valid
    fast_id = lax.broadcasted_iota(jnp.int32, (4 * frames, 128), 0)
    fast_valid = info(0, fast_id >> 2)[0].astype(F32)
    fast_mask[...] = fast_valid
    count_local = jnp.sum(valid, axis=0, keepdims=True) * float(pixels)
    count_block = spread(count_local)

    def chunk(number, size):
        return pl.ds(pl.multiple_of(number * size, 16), size)

    def three(value):
        return value.reshape(-1, 8, value.shape[-1])

    def fold(value):
        return jnp.sum(three(value), axis=0)

    def pair(ref, rows):
        return jnp.concatenate([ref[0, rows, :], ref[1, rows, :]], axis=1)

    def set_pair(ref, rows, value):
        ref[0, rows, :] = value[:, :128]
        ref[1, rows, :] = value[:, 128:]

    def loop(count, body, carry=0):
        return lax.fori_loop(0, count, body, carry)

    def zeros(*shape):
        return jnp.zeros(shape, F32)

    depth = n_dp // 2
    core, side_y = lax.rem(group, 2), group // 2
    side_x, side_z = lax.rem(dp, 2), dp // 2
    pair_core = (dp, group + 1 - 2 * core)
    sides = {"x": side_x, "y": side_y}
    over = {"x": (dp + 1 - 2 * side_x, group), "y": (dp, group + 2 - 4 * side_y)}
    live = {}

    def at(ref, start, size):
        return ref.at[pl.ds(pl.multiple_of(start, 16), size)]

    def regions(place):
        start, size = pieces[place]
        base = start + core * (size // 2)
        sizes = stage_sizes(place, size, depth)
        result = []
        for way, axes in enumerate(orders_of(place)):
            offset = base + way * (size // 4)
            offsets = [offset]
            for axis, (rows, _) in zip(axes, sizes):
                offset = offset + (side_z if axis == "z" else sides[axis]) * rows
                offsets.append(offset)
            result.append(offsets)
        return base, sizes, result

    def begin(place):
        number = live[place][0]
        start, size = pieces[place]
        send, recv = sums_refs[5 * place + 3 : 5 * place + 5]
        base, sizes, offsets = regions(place)
        made = []

        def add_copy(source, target, device):
            made.append(
                pltpu.make_async_remote_copy(
                    src_ref=source,
                    dst_ref=target,
                    send_sem=send.at[0],
                    recv_sem=recv.at[number],
                    device_id=device,
                    device_id_type=MESH,
                )
            )

        if number == 0:
            other = start + (1 - core) * (size // 2)
            add_copy(at(gbuf, other, size // 2), at(summed, other, size // 2), pair_core)
        elif number == 7:
            add_copy(at(summed, base, size // 2), at(summed, base, size // 2), pair_core)
        else:
            stage = number - 1 if number < 4 else 6 - number
            rows, _ = sizes[stage]
            into = sums_refs[5 * place + stage]
            for way, axes in enumerate(orders_of(place)):
                axis, before_ = axes[stage], offsets[way][stage]
                mine = at(summed, offsets[way][stage + 1], rows)
                if axis == "z":
                    for step in range(1, depth):
                        other = lax.rem(side_z + step, depth)
                        device = (other * 2 + side_x, group)
                        if number < 4:
                            source = at(gbuf, before_ + other * rows, rows)
                            add_copy(source, into.at[way, step - 1], device)
                        else:
                            add_copy(mine, mine, device)
                elif number < 4:
                    source = at(gbuf, before_ + (1 - sides[axis]) * rows, rows)
                    add_copy(source, into.at[way, 0], over[axis])
                else:
                    add_copy(mine, mine, over[axis])
        for each in made:
            each.start()
        if 0 < number < 7:
            made = []
            add_copy(into, into, pair_core)
        live[place] = (number, made[0])

    def add_rows(start, size, target, sources):
        step_rows = math.gcd(size, 64)

        def step(number, carry):
            row = pl.multiple_of(number * step_rows, 16)
            rows = pl.ds(pl.multiple_of(start + row, 16), step_rows)
            total = gbuf[rows, :].astype(F32)
            for source in sources(row, step_rows, rows):
                total = total + source.astype(F32)
            target[rows, :] = total.astype(BF)
            return carry

        lax.fori_loop(0, size // step_rows, step, 0)

    def finish(place):
        number, made = live[place]
        start, size = pieces[place]
        base, sizes, offsets = regions(place)
        made.wait()
        if number == 0:
            add_rows(base, size // 2, gbuf, lambda row, count, rows: [summed[rows, :]])
        elif number < 4:
            rows_, messages = sizes[number - 1]
            into = sums_refs[5 * place + number - 1]
            for way in range(2):
                add_rows(
                    offsets[way][number],
                    rows_,
                    summed if number == 3 else gbuf,
                    lambda row, count, rows, way=way: [
                        into[way, message, pl.ds(row, count), :] for message in range(messages)
                    ],
                )
        elif number == 7:
            save = pltpu.make_async_copy(
                summed.at[start : start + size], g_out.at[start : start + size], g_save.at[place]
            )
            save.start()
            saves.append(save)
        live[place] = (number + 1, None) if number < 7 else None

    saves, norm_made = [], []

    def share_norms():
        n_in[dp] = norm_loc[...]
        for peer in dp_peers:
            norm_made.append(
                pltpu.make_async_remote_copy(
                    src_ref=n_in.at[dp],
                    dst_ref=n_in.at[dp],
                    send_sem=n_send.at[0],
                    recv_sem=n_recv.at[0],
                    device_id=peer,
                    device_id_type=MESH,
                )
            )
            norm_made[-1].start()

    def launch(ready_rows):
        for place, (start, size) in enumerate(pieces):
            if place not in live and start + size <= ready_rows:
                live[place] = (0, None)
                begin(place)

    def point(name):
        pump(*PUMPS.get(name, ()))

    def pump(*places):
        for place in places:
            if live.get(place):
                finish(place)
                if live[place]:
                    begin(place)


    row8 = lax.broadcasted_iota(jnp.int32, (8, 1), 0)

    def share(store_ref, sends, recvs, place, sums, squares, extra=None):
        top = jnp.sum(sums, axis=0, keepdims=True)
        second = jnp.sum(squares, axis=0, keepdims=True)
        block = jnp.where(row8 == 0, top, jnp.where(row8 == 1, second, 0.0))
        if extra is not None:
            block = jnp.where(row8 == 2, extra, block)
        store_ref[place, group] = block
        made = []
        for peer in peers:
            made.append(
                pltpu.make_async_remote_copy(
                    src_ref=store_ref.at[place, group],
                    dst_ref=store_ref.at[place, group],
                    send_sem=sends.at[0],
                    recv_sem=recvs.at[place],
                    device_id=peer,
                    device_id_type=MESH,
                )
            )
            made[-1].start()

        part = store_ref.at[place, 0 : n_group - 1]
        arrived = pltpu.make_async_remote_copy(
            src_ref=part,
            dst_ref=part,
            send_sem=sends.at[0],
            recv_sem=recvs.at[place],
            device_id=peers[0],
            device_id_type=MESH,
        )

        def receive():
            arrived.wait()
            total = store_ref[place, 0]
            for slot in range(1, n_group):
                total = total + store_ref[place, slot]
            return [spread(total[i : i + 1, :]) for i in range(3)]

        return receive

    def share_a(place, sums, squares):
        return share(st_a, s_send, a_recv, place, sums, squares)

    def share_c(place, sums, squares):
        return share(st_c, s_send, c_recv, place, sums, squares)

    def share_f(place, sums, squares, extra=None):
        return share(st_f, f_send, f_recv, place, sums, squares, extra)

    def coefs(total, squares, count, gain, bias):
        mean = total / count
        inverse = lax.rsqrt(squares / count - mean * mean + EPS)
        slope_a = gain * inverse
        return mean, inverse, slope_a, bias - mean * slope_a

    def back_coefs(total, cross, count, mean, inverse, slope_a):
        c3 = slope_a * inverse * cross / count
        return slope_a * total / count - mean * c3, c3

    def param(kind, place):
        row = slice(kind, kind + 1)
        if place < 2:
            return spread(params[row, 256 * place : 256 * place + 256])
        if place == 2:
            return spread(params[row, 512:1536])
        low = spread(params[row, 1536:1664])
        rest = params[row, 1664:]
        none = zeros(1, 128 - rest.shape[1])
        high = spread(jnp.concatenate([rest, none], axis=1))
        if place == 3:
            return tiled(jnp.where(lane < 32, low, 0.0))
        if place == 4:
            return tiled(jnp.where((lane >= 32) & (lane < 64), low, 0.0))
        return jnp.where(lane < 64, pltpu.roll(low, 64, 1), pltpu.roll(high, 64, 1))

    bt[...] = jnp.zeros(bt.shape, BF)
    for tap in range(3):
        low = f_reduce[tap].astype(BF)
        for q in range(4):
            other = q + tap - 1
            if 0 <= other < 4:
                bt[32 * q : 32 * q + 32, 128 * other : 128 * other + 128] = low
    bt[128:160, 384:512] = f_reduce[0].astype(BF)
    bt[224:256, 0:128] = f_reduce[2].astype(BF)
    fe[...] = jnp.zeros(fe.shape, BF)
    for q in range(4):
        fe[32 * q : 32 * q + 32, 128 * q : 128 * q + 128] = f_expand[...].astype(BF)
    for tap in range(9):
        wide = jnp.concatenate([f_spatial[tap], zeros(32, 96)], axis=1)
        for q in range(4):
            fs[tap, 32 * q : 32 * q + 32, :] = (
                pltpu.roll(wide, 32 * q, 1) if q else wide
            ).astype(BF)
        side_b = 128 * (tap % 3)
        fst[tap // 3, side_b : side_b + 128, :] = fs[tap].T

    if gbuf.shape[0] > ROWS:
        gbuf[ROWS:, :] = jnp.zeros((gbuf.shape[0] - ROWS, 256), BF)

    ready("xn")

    def widen(number, carry):
        rows = chunk(number, 4 * 2 * line)
        zf[rows, :] = xn[rows, :].astype(F32)
        return carry

    loop(side // 2, widen)

    def pack(source, target):
        def step(number, carry):
            size = 2 * line
            start = pl.multiple_of(number * 4 * size, 16)
            for q in range(4):
                target[chunk(number, size), 128 * q : 128 * q + 128] = source[
                    pl.ds(start + q, size, stride=4), :
                ].astype(BF)
            return carry

        loop(side // 2, step)

    pack(zf, fp)

    for tap in range(5):
        ready(("wl", tap))
        wl[128 * tap : 128 * tap + 128, :] = lateral_stage(zc, tap)[...].astype(BF)

    def lower_reduce(tap):
        ready("wr%d" % tap)

        def step(number, carry):
            rows = chunk(number, 128)
            wr[tap, rows, :] = zc[rows, 256 * tap : 256 * tap + 256].astype(BF)
            return carry

        loop(8, step)

    def edges(number, carry):
        rows = chunk(number, half)
        set_pair(b1, rows, dot(xs[rows, :], wr[0]) + dot(fp[rows, 256:512], wl[0:256, :]))
        set_pair(b2, rows, dot(xs[rows, :], wr[2]))
        return carry

    def fast_first(number, carry):
        rows = chunk(number, half)
        both = dot_nt(fp[rows, :], bt[...])
        zfa[rows, :] = (three(both[:, :128]) * masks[0:8, 0:128]).reshape(half, 128)
        fx[rows, :] = both[:, 128:]
        return carry

    ends_ = pl.ds(frames - 1, pixels, stride=frames)
    heads = pl.ds(0, pixels, stride=frames)

    def halo_copy(ref, place, way, sems):
        made = pltpu.make_async_remote_copy(
            src_ref=ref[0].at[place + way],
            dst_ref=ref[1].at[place + way],
            send_sem=h_send.at[sems, place + way],
            recv_sem=h_recv.at[sems, place + way],
            device_id=(after, before)[way],
            device_id_type=MESH,
        )
        pl.when((dp < n_dp - 1, dp > 0)[way])(made.start)
        return made

    def halo_wait(made):
        @pl.when(dp < n_dp - 1)
        def _():
            made[0].wait_send()
            made[1].wait_recv()

        @pl.when(dp > 0)
        def _():
            made[1].wait_send()
            made[0].wait_recv()

    for way, edge in enumerate((0, n_dp - 1)):

        @pl.when(dp == edge)
        def _(way=way):
            xh_in[way] = jnp.zeros(xh_in.shape[1:], BF)
            for place in (way, 2 + way):
                hr[place] = jnp.zeros(hr.shape[1:], BF)
                fhr[place] = jnp.zeros(fhr.shape[1:], BF)

    def send_halo(place, last, zero):
        for part in range(2):
            hs[place, part, 0:pixels, :] = last[part, ends_, :].astype(BF)
            hs[place + 1, part, 0:pixels, :] = zero[part, heads, :].astype(BF)
        return [halo_copy((hs, hr), place, way, 0) for way in range(2)]

    def take_halo(made, place, last, zero):
        halo_wait(made)
        for part in range(2):
            last[part, ends_, :] = hr[place, part, 0:pixels, :].astype(F32)
            zero[part, heads, :] = hr[place + 1, part, 0:pixels, :].astype(F32)

    block_rows = -(-pixels // 64) * 16
    lanes_ = lax.broadcasted_iota(jnp.int32, (block_rows, 128), 1)
    fill = zeros(4 * block_rows - pixels, 128)

    def send_fast_halo(place, ref, first_lanes):
        for way, (rows, first_lane) in enumerate(zip((ends_, heads), first_lanes)):
            value = jnp.concatenate([ref[rows, :], fill], axis=0)
            total = zeros(block_rows, 128)
            for q in range(4):
                piece = value[block_rows * q : block_rows * (q + 1)]
                turn = (32 * q - first_lane) % 128
                piece = pltpu.roll(piece, turn, 1) if turn else piece
                total = jnp.where((lanes_ >= 32 * q) & (lanes_ < 32 * q + 32), piece, total)
            fhs[place + way] = total.astype(BF)
        return [halo_copy((fhs, fhr), place, way, 1) for way in range(2)]

    def take_fast_halo(made, place, first_lanes):
        halo_wait(made)
        result = []
        for way, first_lane in enumerate(first_lanes):
            value = fhr[place + way].astype(F32)
            pieces_ = []
            for q in range(4):
                turn = (first_lane - 32 * q) % 128
                piece = pltpu.roll(value, turn, 1) if turn else value
                keep = (lanes_ >= first_lane) & (lanes_ < first_lane + 32)
                pieces_.append(jnp.where(keep, piece, 0.0))
            result.append(jnp.concatenate(pieces_, axis=0)[:pixels])
        return result

    low = lax.broadcasted_iota(jnp.int32, (pixels, 128), 1) < 64

    def silu_of(value, slope_a, shift):
        norm = value * slope_a + shift
        return norm * sigmoid(norm)

    def slope_of(norm):
        gate = sigmoid(norm)
        return gate + norm * gate * (1.0 - gate)

    def shifted(ref, y, value, flip):
        width = value.shape[1]
        edge = zeros(frames, width)
        back = jnp.concatenate([edge, value[: line - frames]], axis=0).astype(BF)
        ahead = jnp.concatenate([value[frames:], edge], axis=0).astype(BF)
        ref[y + 1, :, 0:width] = ahead if flip else back
        ref[y + 1, :, width : 2 * width] = value.astype(BF)
        ref[y + 1, :, 2 * width : 3 * width] = back if flip else ahead

    def spatial(z_ref, pad_ref, weight, width, slope_a, shift, out_ref):
        def hide(y, carry):
            value = silu_of(three(z_ref[chunk(y, line), :]), slope_a, shift)
            value = value * masks[0:8, 0:width]
            shifted(pad_ref, y, value.reshape(line, width), False)
            return carry

        loop(side, hide)
        tall = side // 2

        def step(number, carry):
            total = zeros(half, width)
            for a in range(3):
                patch = pad_ref[pl.ds(number * tall + a, tall)].reshape(half, 3 * width)
                total = total + dot(patch, weight(a))
            out_ref[chunk(number, half), :] = total
            return carry[0] + fold(total), carry[1] + fold(total * total)

        return loop(2, step, (zeros(8, width), zeros(8, width)))

    def hide_to(z_ref, target, width, slope_a, shift):
        def hide(y, carry):
            rows = chunk(y, line)
            value = silu_of(three(z_ref[rows, :]), slope_a, shift) * masks[0:8, 0:width]
            target[rows, :] = value.reshape(line, width).astype(BF)
            return carry

        loop(side, hide)

    def unpacked(ref, number, size, value, add):
        start = pl.multiple_of(number * 4 * size, 16)
        for q in range(4):
            place = pl.ds(start + q, size, stride=4)
            piece = value[:, 128 * q : 128 * q + 128]
            ref[place, :] = ref[place, :] + piece if add else piece

    def four(value):
        return value[:, 0:128] + value[:, 128:256] + value[:, 256:384] + value[:, 384:512]

    fast_line = 4 * line

    def quad(value):
        return value.reshape(-1, 4, 8, 128)

    def fold_quad(value):
        return jnp.sum(value.reshape(-1, 8, 128), axis=0)

    def through(z_ref, rows, back, slope_a, shift):
        z = three(z_ref[rows, :])
        grad = three(back) * slope_of(z * slope_a + shift)
        return grad, jnp.sum(grad, axis=0), jnp.sum(grad * z, axis=0)

    def scaled_sums(sums, mean, inverse):
        return sums[0], inverse * (sums[1] - mean * sums[0])

    def back_spatial(dy, z_ref, pad_ref, width, slope_a, c2, c3):
        def step(y, carry):
            rows = chunk(y, line)
            grad = slope_a * three(dy(rows)) - masks[0:8, 0:width] * (c2 + c3 * three(z_ref[rows, :]))
            shifted(pad_ref, y, grad.reshape(line, width), True)
            return carry

        loop(side, step)

    loop(2, fast_first)
    hs[...] = jnp.zeros(hs.shape, BF)
    pl.semaphore_wait(barrier, n_group + n_dp - 2)
    fast_halo = send_fast_halo(0, fx, (0, 96))

    lower_reduce(0)
    lower_reduce(2)
    ready("xs")
    loop(2, edges)
    halo = send_halo(0, b1, b2)

    def middle(number, carry):
        rows = chunk(number, 2 * line)
        total = dot(xs[rows, :], wr[1]) + dot(fp[rows, 0:384], wl[256:640, :])
        za[rows, :] = (three(total) * masks[0:8, 0:256]).reshape(2 * line, 256)
        return carry

    middle_parts = side // 2
    from_before, from_after = take_fast_halo(fast_halo, 0, (0, 96))
    fx[ends_, :] = jnp.where(low, from_before, fx[ends_, :])
    fx[heads, :] = jnp.where(low, fx[heads, :], from_after)

    def join_fast(number, carry):
        rows = chunk(number, line)
        cross = three(fx[rows, :])
        moved = jnp.where(
            lane < 64,
            links[0:8, 0:128] * pltpu.roll(cross, 1, 1),
            links[8:16, 0:128] * pltpu.roll(cross, frames - 1, 1),
        )
        total = three(zfa[rows, :]) + moved
        zfa[rows, :] = total.reshape(line, 128)
        return carry[0] + jnp.sum(total, axis=0), carry[1] + jnp.sum(total * total, axis=0)

    sums = loop(side, join_fast, (zeros(8, 128), zeros(8, 128)))
    got_fa = share_f(0, *sums, extra=count_block)
    lower_reduce(1)
    lax.fori_loop(0, middle_parts // 2, middle, 0)

    padded = xh_in.shape[1] // 5
    staged = gbuf.shape[0] - 10 * padded
    for way, rows in enumerate((ends_, heads)):
        for block in range(5):
            top = staged + (5 * way + block) * padded + pixels
            gbuf[top : top + padded - pixels, :] = jnp.zeros((padded - pixels, 256), BF)

    def stage(way, block, value):
        top, left = staged + (5 * way + block // 2) * padded, 128 * (block % 2)
        gbuf[top : top + pixels, left : left + 128] = value.astype(BF)

    for block in range(8):
        zfb[...] = xs[:, 128 * block : 128 * (block + 1)].astype(F32)
        stage(0, block, zfb[ends_, :])
        stage(1, block, zfb[heads, :])
    for q, way, block in ((2, 0, 8), (3, 0, 9), (0, 1, 8)):
        zfb[...] = fp[:, 128 * q : 128 * q + 128].astype(F32)
        stage(way, block, zfb[(ends_, heads)[way], :])
    stage(1, 9, zeros(pixels, 128))
    for tap in range(9):
        ready(("ws", tap))
        ws[256 * tap : 256 * tap + 256, :] = spatial_stage(zc, tap)[...].astype(BF)
    for block in range(4):
        ready(("we", block))
        we[:, 256 * block : 256 * block + 256] = zb[256 * block : 256 * block + 256, :].astype(BF)
    sa[0] = jnp.zeros((line, 768), BF)
    sa[side + 1] = jnp.zeros((line, 768), BF)
    fa[0] = jnp.zeros((line, 384), BF)
    fa[side + 1] = jnp.zeros((line, 384), BF)

    sums, squares, count = got_fa()
    fast_count = 4.0 * count
    counts = jnp.concatenate([count] * 8, axis=1)
    mean_fa, inv_fa, m_fa, s_fa = coefs(
        tiled(sums), tiled(squares), fast_count, param(0, 3), param(1, 3)
    )
    sums = spatial(
        zfa, fa, lambda a: fs[3 * a : 3 * a + 3].reshape(384, 128), 128, m_fa, s_fa, zfb
    )
    got_fb = share_f(1, *sums)

    lax.fori_loop(middle_parts // 2, middle_parts, middle, 0)
    take_halo(halo, 0, b1, b2)
    x_halo = []
    for way in range(2):
        made = pltpu.make_async_remote_copy(
            src_ref=gbuf.at[staged + 5 * padded * way : staged + 5 * padded * (way + 1)],
            dst_ref=xh_in.at[way],
            send_sem=h_send.at[2, way],
            recv_sem=h_recv.at[2, way],
            device_id=(after, before)[way],
            device_id_type=MESH,
        )
        pl.when((dp < n_dp - 1, dp > 0)[way])(made.start)
        x_halo.append(made)

    def join(number, carry):
        rows = chunk(number, line)
        total = three(za[rows, :])
        total = total + links[0:8, 0:256] * pltpu.roll(three(pair(b1, rows)), 1, 1)
        total = total + links[8:16, 0:256] * pltpu.roll(three(pair(b2, rows)), frames - 1, 1)
        za[rows, :] = total.reshape(line, 256)
        return carry[0] + jnp.sum(total, axis=0), carry[1] + jnp.sum(total * total, axis=0)

    sums = loop(side, join, (zeros(8, 256), zeros(8, 256)))
    got_sa = share_a(0, *sums)

    sums, squares, _ = got_fb()
    mean_fb, inv_fb, m_fb, s_fb = coefs(
        tiled(sums), tiled(squares), fast_count, param(0, 4), param(1, 4)
    )
    hide_to(zfb, hfb, 128, m_fb, s_fb)

    def expand_fast(number, carry):
        size = 2 * line
        total = dot(hfb[chunk(number, size), :], fe[...])
        unpacked(zf, number, size, total, False)
        return carry[0] + four(fold(total)), carry[1] + four(fold(total * total))

    sums = loop(side // 2, expand_fast, (zeros(8, 128), zeros(8, 128)))
    got_fc = share_f(2, *sums)

    sums, squares, _ = got_sa()
    mean_sa, inv_sa, m_sa, s_sa = coefs(sums, squares, counts[:, :256], param(0, 0), param(1, 0))
    sums = spatial(za, sa, lambda a: ws[768 * a : 768 * a + 768, :], 256, m_sa, s_sa, zb)
    got_sb = share_a(1, *sums)

    sums, squares, _ = got_fc()
    mean_fc, inv_fc, m_fc, s_fc = coefs(sums, squares, fast_count, param(0, 5), param(1, 5))
    ready("cf")

    def finish_fast(y, carry):
        rows = chunk(y, fast_line)
        z = quad(zf[rows, :])
        norm = z * m_fc + s_fc + quad(xn[rows, :].astype(F32))
        gate = sigmoid(norm)
        kept = gate * fast_mask[...].reshape(4, 8, 128)
        act = norm * kept
        grad = quad(cf[rows, :].astype(F32)) * (kept + act * (1.0 - gate))
        cf[rows, :] = act.reshape(fast_line, 128).astype(BF)
        df[rows, :] = grad.reshape(fast_line, 128)
        return carry[0] + fold_quad(grad), carry[1] + fold_quad(grad * z)

    sums = loop(side, finish_fast, (zeros(8, 128), zeros(8, 128)))
    back_fc = share_f(3, *scaled_sums(sums, mean_fc, inv_fc))
    save_fast = pltpu.make_async_copy(cf, fast_out, store.at[1])
    save_fast.start()

    sums, squares, _ = got_sb()
    mean_sb, inv_sb, m_sb, s_sb = coefs(sums, squares, counts[:, :256], param(0, 1), param(1, 1))
    def hide_part(part):
        rows = slice(2 * line * part, 2 * line * (part + 1))
        value = silu_of(three(zb[rows, :]), m_sb, s_sb) * masks[0:8, 0:256]
        hsb[rows, :] = value.reshape(2 * line, 256).astype(BF)

    hide_part(0)
    sums = (zeros(8, 1024), zeros(8, 1024))
    for part in range(side // 2):
        rows = slice(2 * line * part, 2 * line * (part + 1))
        total = dot(hsb[rows, :], we[...])
        if part + 1 < side // 2:
            hide_part(part + 1)
        zc[rows, :] = total
        sums = sums[0] + fold(total), sums[1] + fold(total * total)
    got_sc = share_c(0, *sums)

    norm_loc[...] = zeros(16, 256)
    total_fc, cross_fc, _ = back_fc()
    c2, c3 = back_coefs(total_fc, cross_fc, fast_count, mean_fc, inv_fc, m_fc)

    def back_fast(y, carry, c2=c2, c3=c3):
        rows = chunk(y, fast_line)
        mask = fast_mask[...].reshape(4, 8, 128)
        grad = m_fc * quad(df[rows, :]) - mask * (c2 + c3 * quad(zf[rows, :]))
        zf[rows, :] = grad.reshape(fast_line, 128)
        return carry

    loop(side, back_fast)
    pack(zf, dzf)

    def back_hidden_fast(number, carry):
        rows = chunk(number, half)
        back = dot_nt(dzf[rows, :], fe[...])
        grad, one, two = through(zfb, rows, back, m_fb, s_fb)
        fx[rows, :] = grad.reshape(half, 128)
        return carry[0] + one, carry[1] + two

    sums = loop(2, back_hidden_fast, (zeros(8, 128), zeros(8, 128)))
    back_fb = share_f(4, *scaled_sums(sums, mean_fb, inv_fb))
    wide = dot_tn(hfb[...], dzf[...])
    grad_fc = sum(wide[32 * q : 32 * q + 32, 128 * q : 128 * q + 128] for q in range(4))
    gbuf[TINY + 32 : TINY + 64, 128:256] = grad_fc.astype(BF)

    sums, squares, _ = got_sc()
    mean_sc, inv_sc, m_sc, s_sc = coefs(sums, squares, counts, param(0, 2), param(1, 2))
    ready("cs")

    def finish_slow(y, carry):
        rows = chunk(y, line)
        z = three(zc[rows, :])
        norm = z * m_sc + s_sc + three(xs[rows, :].astype(F32))
        gate = sigmoid(norm)
        kept = gate * masks[0:8, :]
        act = norm * kept
        grad = three(cs[rows, :].astype(F32)) * (kept + act * (1.0 - gate))
        cs[rows, :] = act.reshape(line, 1024).astype(BF)
        ds[rows, :] = grad.reshape(line, 1024).astype(BF)
        return carry[0] + jnp.sum(grad, axis=0), carry[1] + jnp.sum(grad * z, axis=0)

    sums = loop(side, finish_slow, (zeros(8, 1024), zeros(8, 1024)))
    back_sc = share_c(1, *scaled_sums(sums, mean_sc, inv_sc))
    save_slow = pltpu.make_async_copy(cs, slow_out, store.at[0])
    save_slow.start()

    total_fb, cross_fb, _ = back_fb()
    total_fb, cross_fb = tiled(total_fb), tiled(cross_fb)
    c2, c3 = back_coefs(total_fb, cross_fb, fast_count, mean_fb, inv_fb, m_fb)
    hfb[...] = fa[1 : side + 1, :, 128:256].reshape(n_rows, 128)
    back_spatial(lambda rows: fx[rows, :], zfb, fa, 128, m_fb, c2, c3)

    def back_first_fast(number, carry):
        rows = chunk(number, half)
        tall = side // 2
        back = zeros(half, 128)
        for a in range(3):
            patch = fa[pl.ds(number * tall + 2 - a, tall)].reshape(half, 384)
            back = back + dot(patch, fst[a])
        grad, one, two = through(zfa, rows, back, m_fa, s_fa)
        fx[rows, :] = grad.reshape(half, 128)
        return carry[0] + one, carry[1] + two

    sums = loop(2, back_first_fast, (zeros(8, 128), zeros(8, 128)))
    back_fa = share_f(5, *scaled_sums(sums, mean_fa, inv_fa))

    total, cross, _ = back_sc()
    for block in range(4):
        cols = slice(256 * block, 256 * (block + 1))
        norm_loc[2 + block : 3 + block, :] = cross[0:1, cols]
        norm_loc[10 + block : 11 + block, :] = total[0:1, cols]
    c2, c3 = back_coefs(total, cross, counts, mean_sc, inv_sc, m_sc)
    save_slow.wait()

    def back_part(part, c2=c2, c3=c3):
        for half_part in range(2):
            rows = slice(line * (2 * part + half_part), line * (2 * part + half_part + 1))
            grad = m_sc * three(ds[rows, :].astype(F32))
            grad = grad - masks[0:8, :] * (c2 + c3 * three(zc[rows, :]))
            cs[rows, :] = grad.reshape(line, 1024).astype(BF)

    back_part(0)
    sums = (zeros(8, 256), zeros(8, 256))
    for part in range(side // 2):
        rows = slice(2 * line * part, 2 * line * (part + 1))
        back = dot_nt(cs[rows, :], we[...])
        if part + 1 < side // 2:
            back_part(part + 1)
        grad, one, two = through(zb, rows, back, m_sb, s_sb)
        set_pair(b1, rows, grad.reshape(2 * line, 256))
        sums = sums[0] + one, sums[1] + two
    back_sb = share_a(2, *scaled_sums(sums, mean_sb, inv_sb))
    h_t[...] = hsb[...].T
    for block in range(4):
        cols = slice(256 * block, 256 * (block + 1))
        gbuf[cols, :] = dot(h_t[...], cs[:, cols]).astype(BF)
    launch(1024)

    total_fa, cross_fa, _ = back_fa()
    total_fa, cross_fa = tiled(total_fa), tiled(cross_fa)
    c2, c3 = back_coefs(total_fa, cross_fa, fast_count, mean_fa, inv_fa, m_fa)

    def back_one_fast(y, carry, c2=c2, c3=c3):
        rows = chunk(y, line)
        grad = m_fa * three(fx[rows, :]) - masks[0:8, 0:128] * (c2 + c3 * three(zfa[rows, :]))
        grad = grad.reshape(line, 128)
        zfb[rows, :] = grad
        dzf[rows, 0:128] = grad.astype(BF)
        return carry

    loop(side, back_one_fast)
    fast_halo = send_fast_halo(2, zfb, (96, 0))
    pump(0)

    total, cross, _ = back_sb()
    norm_loc[1:2, :] = cross[0:1, :]
    norm_loc[9:10, :] = total[0:1, :]
    c2, c3 = back_coefs(total, cross, counts[:, :256], mean_sb, inv_sb, m_sb)
    h_t[...] = sa[1 : side + 1, :, 256:512].reshape(n_rows, 256).T
    back_spatial(lambda rows: pair(b1, rows), zb, sa, 256, m_sb, c2, c3)

    def spatial_grad(tap, carry):
        for b in range(3):
            patch = sa[pl.ds(2 - tap, side), :, 256 * b : 256 * (b + 1)].reshape(n_rows, 256)
            place = pl.multiple_of(1024 + 768 * tap + 256 * b, 16)
            gbuf[pl.ds(place, 256), :] = dot(h_t[...], patch).astype(BF)
        return carry

    loop(3, spatial_grad)
    launch(REDUCE_1)
    point("a")

    def back_first(number, carry):
        rows = chunk(number, half)
        tall = side // 2
        back = zeros(half, 256)
        for a in range(3):
            for b in range(3):
                tap = 3 * a + b
                patch = sa[pl.ds(number * tall + 2 - a, tall), :, 256 * b : 256 * (b + 1)]
                back = back + dot_nt(patch.reshape(half, 256), ws[256 * tap : 256 * tap + 256, :])
        grad, one, two = through(za, rows, back, m_sa, s_sa)
        set_pair(b1, rows, grad.reshape(half, 256))
        return carry[0] + one, carry[1] + two

    sums = back_first(0, (zeros(8, 256), zeros(8, 256)))
    point("a2")
    sums = back_first(1, sums)
    back_sa = share_a(3, *scaled_sums(sums, mean_sa, inv_sa))
    point("b")

    lanes = lax.broadcasted_iota(jnp.int32, (32, 128), 1)
    tiles = [zeros(32, 128) for _ in range(3)]
    for a in range(3):
        patch = fa[2 - a : 2 - a + side].reshape(n_rows, 384)
        wide = dot_tn(hfb[...], patch)
        for b in range(3):
            tap = 3 * a + b
            for q in range(4):
                piece = wide[32 * q : 32 * q + 32, 128 * b : 128 * b + 128]
                turn = (32 * (tap % 4) - 32 * q) % 128
                piece = pltpu.roll(piece, turn, 1) if turn else piece
                inside = (lanes >= 32 * (tap % 4)) & (lanes < 32 * (tap % 4) + 32)
                tiles[tap // 4] = tiles[tap // 4] + jnp.where(inside, piece, 0.0)
    gbuf[TINY + 64 : TINY + 96, 0:128] = tiles[0].astype(BF)
    gbuf[TINY + 64 : TINY + 96, 128:256] = tiles[1].astype(BF)
    gbuf[TINY + 96 : TINY + 128, 0:128] = tiles[2].astype(BF)
    gbuf[TINY + 96 : TINY + 128, 128:256] = jnp.zeros((32, 128), BF)


    total, cross, _ = back_sa()
    norm_loc[0:1, :] = cross[0:1, :]
    norm_loc[8:9, :] = total[0:1, :]
    c2, c3 = back_coefs(total, cross, counts[:, :256], mean_sa, inv_sa, m_sa)

    def back_one(y, carry, c2=c2, c3=c3):
        rows = chunk(y, line)
        grad = m_sa * three(pair(b1, rows)) - masks[0:8, 0:256] * (c2 + c3 * three(za[rows, :]))
        grad = grad.reshape(line, 256)
        set_pair(b1, rows, grad)
        set_pair(b2, rows, grad)
        cs[rows, 512:768] = grad.astype(BF)
        return carry

    loop(side, back_one)
    point("c")
    halo = send_halo(2, b2, b1)
    point("d")
    for top, values in ((6, (cross_fa, cross_fb, cross_fc)), (14, (total_fa, total_fb, total_fc))):
        turned = pltpu.roll(values[2], 64, 1)
        left = jnp.where(lane < 32, values[0], jnp.where(lane < 64, values[1], turned))
        norm_loc[top : top + 1, 0:128] = left[0:1]
        norm_loc[top : top + 1, 128:256] = jnp.where(lane < 64, turned, 0.0)[0:1]
    share_norms()

    h_t[...] = cs[:, 512:768].T
    for block in range(4):
        cols = slice(256 * block, 256 * (block + 1))
        rows = slice(REDUCE_1 + 256 * block, REDUCE_1 + 256 * (block + 1))
        gbuf[rows, :] = dot(h_t[...], xs[:, cols]).astype(BF)
    wide = dot(h_t[...], fp[:, 0:384]).astype(BF)
    gbuf[LATERAL_2 : LATERAL_2 + 256, :] = wide[:, 0:256]
    gbuf[LATERAL_2 + 256 : LATERAL_2 + 384, 0:128] = wide[0:128, 256:384]
    gbuf[LATERAL_2 + 256 : LATERAL_2 + 384, 128:256] = wide[128:256, 256:384]
    launch(LATERAL_2 + 384)
    point("e")

    halo_wait(x_halo)

    def edge_rows(ref, rows, link):
        value = ref[rows, :] * link
        fill_rows = jnp.zeros((padded - pixels, 128), F32)
        return jnp.concatenate([value, fill_rows], axis=0).astype(BF)

    def neighbours(first_link):
        def step(y, carry):
            rows = chunk(y, line)
            back = links[first_link : first_link + 8, :]
            ahead = links[first_link + 8 : first_link + 16, :]
            up = ahead * pltpu.roll(three(pair(b1, rows)), frames - 1, 1)
            down = back * pltpu.roll(three(pair(b2, rows)), 1, 1)
            cs[rows, 0:256] = up.reshape(line, 256).astype(BF)
            cs[rows, 256:512] = down.reshape(line, 256).astype(BF)
            cross = three(zfb[rows, :])
            moved = jnp.where(
                lane < 64,
                ahead[:, :128] * pltpu.roll(cross, frames - 1, 1),
                back[:, :128] * pltpu.roll(cross, 1, 1),
            )
            moved = jnp.where((lane < 32) | (lane >= 96), moved, 0.0)
            dzf[rows, 128:256] = moved.reshape(line, 128).astype(BF)
            return carry

        loop(side, step)

    neighbours(16)
    link_back, link_ahead = links[0:1, 0:128], links[8 + frames - 1 : 8 + frames, 0:128]
    wide = dot_tn(dzf[:, 0:256], fp[...])
    parts = [zeros(32, 128) for _ in range(3)]
    for tap in range(3):
        for q in range(4):
            other = q + tap - 1
            if 0 <= other < 4:
                parts[tap] = parts[tap] + wide[
                    32 * q : 32 * q + 32, 128 * other : 128 * other + 128
                ]
    parts[0] = parts[0] + wide[128:160, 384:512]
    parts[2] = parts[2] + wide[224:256, 0:128]
    wide = dot_tn(edge_rows(zfb, heads, link_back), xh_in[0, 4 * padded :, 128:256])
    parts[0] = parts[0] + wide[0:32]
    wide = dot_tn(edge_rows(zfb, ends_, link_ahead), xh_in[1, 4 * padded :, 0:128])
    parts[2] = parts[2] + wide[96:128]
    gbuf[TINY : TINY + 32, 0:128] = parts[0].astype(BF)
    gbuf[TINY : TINY + 32, 128:256] = parts[1].astype(BF)
    gbuf[TINY + 32 : TINY + 64, 0:128] = parts[2].astype(BF)
    point("f")

    for way, (side_lanes, low_row, rows_, link) in enumerate(
        ((0, REDUCE_0, heads, link_back), (256, REDUCE_2, ends_, link_ahead))
    ):
        h_t[...] = cs[:, side_lanes : side_lanes + 256].T
        edge = [edge_rows(b1.at[part], rows_, link) for part in range(2)]
        edge = jnp.concatenate(edge, axis=1).T
        for block in range(4):
            cols = slice(256 * block, 256 * (block + 1))
            rows = slice(low_row + 256 * block, low_row + 256 * (block + 1))
            total = dot(h_t[...], xs[:, cols]) + dot(edge, xh_in[way, padded * block : padded * (block + 1), :])
            gbuf[rows, :] = total.astype(BF)
        if way == 0:
            total = dot(h_t[...], fp[:, 256:512]) + dot(edge, xh_in[0, 4 * padded :, :])
            gbuf[LATERAL_0 : LATERAL_0 + 256, :] = total.astype(BF)
            launch(REDUCE_2)
            point("g")
    launch(gbuf.shape[0])
    point("h")

    def input_grad_mid(number, carry):
        rows = chunk(number, half)
        total = ds[rows, :].astype(F32) + dot_nt(cs[rows, 512:768], wr[1])
        ds[rows, :] = total.astype(BF)
        return carry

    loop(2, input_grad_mid)
    point("i")
    take_halo(halo, 2, b2, b1)
    from_before, from_after = take_fast_halo(fast_halo, 2, (96, 0))
    zfb[ends_, :] = jnp.where(low, zfb[ends_, :], from_before)
    zfb[heads, :] = jnp.where(low, from_after, zfb[heads, :])
    neighbours(0)
    point("j")

    def input_grad(number, carry):
        rows = chunk(number, 2 * line)
        total = dot_nt(cs[rows, 0:256], wr[0])
        total = total + dot_nt(cs[rows, 256:512], wr[2])
        ds[rows, :] = (ds[rows, :].astype(F32) + total).astype(BF)
        return carry

    def input_grad_fast(number, carry):
        size = 2 * line
        rows = chunk(number, size)
        total = dot(dzf[rows, 0:256], bt[...])
        mid = dot_nt(cs[rows, 512:768], wl[256:640, :])
        up = dot_nt(cs[rows, 0:256], wl[0:256, :])
        total = total + jnp.concatenate([mid, zeros(size, 128)], axis=1)
        total = total + jnp.concatenate([zeros(size, 256), up], axis=1)
        unpacked(df, number, size, total, True)
        return carry

    parts_ = side // 2
    lax.fori_loop(0, parts_ // 2, input_grad_fast, 0)
    point("k")
    lax.fori_loop(parts_ // 2, parts_, input_grad_fast, 0)
    save_df = pltpu.make_async_copy(df, fast_grad, store.at[3])
    save_df.start()
    point("l")
    lax.fori_loop(0, parts_ // 2, input_grad, 0)
    point("m")
    lax.fori_loop(parts_ // 2, parts_, input_grad, 0)
    save_ds = pltpu.make_async_copy(ds, slow_grad, store.at[4])
    save_ds.start()
    point("n")

    while any(live.values()):
        point("z")
    part = n_in.at[0 : n_dp - 1]
    pltpu.make_async_remote_copy(
        src_ref=part,
        dst_ref=part,
        send_sem=n_send.at[0],
        recv_sem=n_recv.at[0],
        device_id=dp_peers[0],
        device_id_type=MESH,
    ).wait()
    total = n_in[0]
    for slot in range(1, n_dp):
        total = total + n_in[slot]
    norm_out[...] = total
    for each in saves:
        each.wait()
    save_fast.wait()
    save_df.wait()
    save_ds.wait()


def spatial_stage(ref, tap):
    if tap == 8:
        return ref.at[0:256, 768:1024]
    top = 1024 + 256 * (tap // 4)
    return ref.at[top : top + 256, 256 * (tap % 4) : 256 * (tap % 4) + 256]


def lateral_stage(ref, tap):
    return ref.at[256 + 128 * tap : 384 + 128 * tap, 768:1024]


def block_call(mesh, frames, side, rows, operands):
    n_dp, n_group = mesh.shape["dp"], mesh.shape["group"]
    pixels = side * side
    n = pixels * frames
    line = side * frames
    dma = pltpu.SemaphoreType.DMA
    vmem = pltpu.VMEM
    shape = jax.ShapeDtypeStruct
    peers = n_group - 1
    pieces, depth = pieces_of(n_dp), n_dp // 2
    sums_scratch = []
    for place, (_, size) in enumerate(pieces):
        sizes = stage_sizes(place, size, depth)
        sums_scratch += [vmem((2, count, each, 256), BF) for each, count in sizes]
        sums_scratch += [dma((1,)), dma((8,))]
    return pl.pallas_call(
        partial(block_kernel, n_dp, n_group, frames, side, pieces),
        out_shape=(
            shape((n, 1024), BF),
            shape((4 * n, 128), BF),
            shape((n, 1024), BF),
            shape((4 * n, 128), F32),
            shape((rows, 256), BF),
            shape((16, 256), F32),
        ),
        in_specs=[ANYWHERE] * 4 + [SCALARS] * 2 + [ANYWHERE] * 4 + [WHOLE] * 4,
        out_specs=(ANYWHERE,) * 5 + (WHOLE,),
        scratch_shapes=[
            vmem((n, 1024), BF),
            vmem((n, 1024), BF),
            vmem((4 * n, 128), BF),
            vmem((4 * n, 128), BF),
            vmem((n, 512), BF),
            vmem((4 * n, 128), F32),
            vmem((4 * n, 128), F32),
            vmem((n, 1024), BF),
            vmem((n, 1024), F32),
            vmem((n, 256), F32),
            vmem((n, 256), F32),
            vmem((2, n, 128), F32),
            vmem((2, n, 128), F32),
            vmem((side + 2, line, 768), BF),
            vmem((side + 2, line, 384), BF),
            vmem((n, 256), BF),
            vmem((n, 128), BF),
            vmem((n, 128), F32),
            vmem((n, 128), F32),
            vmem((n, 128), F32),
            vmem((n, 512), BF),
            vmem((256, n), BF),
            vmem((3, 1024, 256), BF),
            vmem((9 * 256, 256), BF),
            vmem((256, 1024), BF),
            vmem((640, 256), BF),
            vmem((256, 512), BF),
            vmem((9, 128, 128), BF),
            vmem((3, 384, 128), BF),
            vmem((128, 512), BF),
            vmem((rows, 256), BF),
            vmem((8, 1024), F32),
            vmem((32, 256), F32),
            vmem((32, 128), F32),
            vmem((2, 5 * (-(-pixels // 16) * 16), 256), BF),
            vmem((4, 2, -(-pixels // 16) * 16, 128), BF),
            vmem((4, 2, -(-pixels // 16) * 16, 128), BF),
            vmem((4, -(-pixels // 64) * 16, 128), BF),
            vmem((4, -(-pixels // 64) * 16, 128), BF),
            vmem((4, n_group, 8, 256), F32),
            vmem((2, n_group, 8, 1024), F32),
            vmem((6, n_group, 8, 128), F32),
            dma((LOADS,)),
            dma((5,)),
            dma((3, 4)),
            dma((3, 4)),
            dma((1,)),
            dma((4,)),
            dma((2,)),
            dma((1,)),
            dma((6,)),
            vmem((rows, 256), BF),
            vmem((16, 256), F32),
            vmem((n_dp, 16, 256), F32),
            dma((1,)),
            dma((1,)),
            dma((len(pieces),)),
        ]
        + sums_scratch,
        compiler_params=pltpu.CompilerParams(
            collective_id=0, has_side_effects=True, vmem_limit_bytes=VMEM_LIMIT
        ),
        name="bottleneck",
    )(*operands)


def body(mesh, slow_in, fast_in, slow_cotangent, fast_cotangent, clip_start, clip_end, *rest):
    weights, moments_old, norms = rest[:7], rest[7:14], rest[14:]
    frames, side, slow_width = slow_in.shape[1], slow_in.shape[2], slow_in.shape[4]
    fast_frames, fast_width = fast_in.shape[1], fast_in.shape[4]
    rows = rows_total(mesh.shape["dp"])

    def flat(array):
        return jnp.transpose(array[0], (1, 2, 0, 3)).reshape(-1, array.shape[4])

    def unflat(array, count):
        grid = array.reshape(side, side, count, array.shape[1])
        return jnp.transpose(grid, (2, 0, 1, 3))[None]

    def turn(arrays):
        return arrays[:4] + (jnp.swapaxes(arrays[4], 1, 2),) + arrays[5:]

    turned = turn(weights)
    *kept, grads, norm_grad = block_call(
        mesh,
        frames,
        side,
        rows,
        (
            flat(slow_in),
            flat(fast_in),
            flat(slow_cotangent),
            flat(fast_cotangent),
            clip_start,
            clip_end,
            *turned,
            norms[0],
        ),
    )
    weights_new, moments_new, kept, norms_new = muon(
        grads, norm_grad, norms, turned, turn(moments_old), kept
    )
    slow_out, fast_out, slow_grad, fast_grad = kept
    weights_new, moments_new = turn(tuple(weights_new)), turn(tuple(moments_new))
    params_new, first_new, second_new = norms_new
    return (
        unflat(slow_out, frames),
        unflat(fast_out, fast_frames),
        unflat(slow_grad, frames),
        unflat(fast_grad, fast_frames),
        *weights_new,
        *moments_new,
        first_new,
        second_new,
        params_new,
    )


def solution(mesh):
    sharded = P("group", "dp", None, None, None)
    return jax.shard_map(
        partial(body, mesh),
        mesh=mesh,
        in_specs=(sharded,) * 4 + (P("group", None),) * 2 + (P(),) * 17,
        out_specs=(sharded,) * 4 + (P(),) * 17,
        check_vma=False,
    )
```

```python
from functools import partial
import math

import jax
import jax.numpy as jnp
from jax import lax
from jax.experimental import pallas as pl
from jax.experimental.pallas import tpu as pltpu
from jax.sharding import PartitionSpec as P

NS_STEPS = 5
STEP = 10


EPS = 1e-05
MU = 0.95
LR = 0.3
BETA_ONE = 0.9
BETA_TWO = 0.95
LR_NORM = 0.2
ADAM_EPS = 1e-08
NS_A = 3.4445
NS_B = -4.775
NS_C = 2.0315
F32 = jnp.float32
BF = jnp.bfloat16
MESH = pl.DeviceIdType.MESH
REDUCE_1 = 3328
LATERAL_2 = 4352
TINY = 4736
REDUCE_0 = 4864
LATERAL_0 = 5888
REDUCE_2 = 6144
ROWS = 7168
CUTS = (1024, 3072, 4096, 6144)
LOADS = 29
PARTS = 7
PUMPS = {
    "a": (0,),
    "b": (1, 0),
    "c": (0,),
    "e": (1,),
    "f": (2,),
    "g": (0,),
    "h": (3, 1),
    "i": (4, 2),
    "j": (1,),
    "l": (3, 2, 4),
    "m": (1,),
    "n": (3, 4, 2, 1, 0),
    "z": (3, 4, 1, 2, 0),
}
VMEM_LIMIT = 62 * 2**20
WHOLE = pl.BlockSpec(memory_space=pltpu.VMEM)
ANYWHERE = pl.BlockSpec(memory_space=pl.ANY)
SCALARS = pl.BlockSpec(memory_space=pltpu.SMEM)


def adam_step(params, first, second, grad):
    first_new = BETA_ONE * first + (1.0 - BETA_ONE) * grad
    second_new = BETA_TWO * second + (1.0 - BETA_TWO) * grad * grad
    corrected = first_new / (1.0 - BETA_ONE**STEP)
    params_new = params - LR_NORM * corrected / (
        jnp.sqrt(second_new / (1.0 - BETA_TWO**STEP)) + ADAM_EPS
    )
    return (params_new, first_new, second_new)


def rows_total(n_dp):
    unit = 256 * (n_dp // 2)
    return -(-ROWS // unit) * unit


def pieces_of(n_dp):
    unit = 256 * (n_dp // 2)
    cuts = [0] + [cut // unit * unit for cut in CUTS] + [rows_total(n_dp)]
    cuts = sorted(set(cuts))
    return [(low, high - low) for low, high in zip(cuts[:-1], cuts[1:])]


def orders_of(place):
    return (("x", "y", "z"), ("y", "x", "z"))


def stage_sizes(place, size, depth):
    rows, result = size // 4, []
    for axis in orders_of(place)[0]:
        rows = rows // depth if axis == "z" else rows // 2
        result.append((rows, depth - 1 if axis == "z" else 1))
    return result


def dot(left, right):
    return jnp.dot(left, right, preferred_element_type=F32)


def dot_nt(left, right):
    return lax.dot_general(left, right, (((1,), (1,)), ((), ())), preferred_element_type=F32)


def dot_tn(left, right):
    return lax.dot_general(left, right, (((0,), (0,)), ((), ())), preferred_element_type=F32)


def split(value):
    high = value.astype(BF)
    return high, (value - high.astype(F32)).astype(BF)


def dot_split(left, right):
    return dot(
        jnp.concatenate([left[0], left[0], left[1]], axis=1),
        jnp.concatenate([right[0], right[1], right[0]], axis=0),
    )


def gram_tn(value):
    low = value.astype(BF)
    return dot_tn(low, low)


def gram_nt(value):
    low = value.astype(BF)
    return dot_nt(low, low)


def eye(size, kept=None):
    row = lax.broadcasted_iota(jnp.int32, (size, size), 0)
    col = lax.broadcasted_iota(jnp.int32, (size, size), 1)
    return jnp.where(row == col, 1.0, 0.0).astype(F32)


def square_split(value):
    high, low = value
    cross = dot(high, low)
    return dot(high, high) + cross + cross.T


def newton_poly(a, square):
    return NS_A * eye(a.shape[0]) + NS_B * a + NS_C * square


def newton_first(chains):
    newton_middle(chains, True)


def newton_middle(chains, first=False):
    values = [a_ref[...] for a_ref, _ in chains]
    splits = [split(a) for a in values]
    squares = [square_split(each) for each in splits]
    polys = [newton_poly(a, square) for a, square in zip(values, squares)]
    fine = [a.shape[0] < 256 for a in values]
    polys = [split(poly) if each else poly.astype(BF) for poly, each in zip(polys, fine)]
    if first:
        products = [
            poly[0].astype(F32) + poly[1].astype(F32) if each else poly.astype(F32)
            for poly, each in zip(polys, fine)
        ]
    else:
        products = [
            dot(p_ref[...].astype(BF), poly[0] if each else poly)
            for (_, p_ref), poly, each in zip(chains, polys, fine)
        ]
    once = [
        dot_split(a, poly) if each else dot(a[0], poly) + dot(a[1], poly)
        for a, poly, each in zip(splits, polys, fine)
    ]
    once = [split(each) for each in once]
    twice = [
        dot_split(a, poly) if each else dot(poly, a[0]) + dot(poly, a[1])
        for a, poly, each in zip(once, polys, fine)
    ]
    for (a_ref, p_ref), a, product in zip(chains, twice, products):
        a_ref[...] = a
        p_ref[...] = product


def newton_last(chains):
    values = [a_ref[...] for a_ref, _ in chains]
    lows = [a.astype(BF) for a in values]
    squares = [dot(low, low) for low in lows]
    polys = [
        (NS_A * eye(a.shape[0]) + NS_B * a + NS_C * square).astype(BF)
        for a, square in zip(values, squares)
    ]
    products = [dot(p_ref[...].astype(BF), poly) for (_, p_ref), poly in zip(chains, polys)]
    for (_, p_ref), product in zip(chains, products):
        p_ref[...] = product


def newton_steps():
    return [newton_first] + [newton_middle] * (NS_STEPS - 2) + [newton_last]


def norm_of(gram, size):
    trace = jnp.sum(gram * eye(size))
    return 1.0 / (jnp.sqrt(trace) + 1e-07)


def muon_kernel(*refs):
    grads, norm_grad, norms = refs[0], refs[1], refs[2:5]
    weight_in, moment_in, kept = refs[5:12], refs[12:19], refs[19:23]
    weight_out, moment_out, kept_out = refs[23:30], refs[30:37], refs[37:41]
    norms_out, g_buf = refs[41:44], refs[44]
    weight, moment, keep = refs[45:52], refs[52:59], refs[59:63]
    chain_a, chain_p, small_a, small_p, low_buf = refs[63:68]
    wide_keep = refs[68:70]
    sem, g_sem, tap_sem, out_sem, keep_in, keep_out, norm_sem = refs[70:77]
    norm_grad_in, norms_in, norms_target = norm_grad, norms, norms_out
    norm_grad, norms, norms_out = refs[77], refs[78:81], refs[81:84]
    loads_n = [
        pltpu.make_async_copy(source, target, norm_sem.at[place])
        for place, (source, target) in enumerate(
            zip((norm_grad_in, *norms_in), (norm_grad, *norms))
        )
    ]

    g_cuts = (0, 1024, REDUCE_1, LATERAL_2, TINY, REDUCE_0, LATERAL_0, REDUCE_2, ROWS)
    loads = {}
    for place, (low, high) in enumerate(zip(g_cuts[:-1], g_cuts[1:])):
        span = pl.ds(low, high - low)
        loads[low] = pltpu.make_async_copy(grads.at[span], g_buf.at[span], g_sem.at[place])
    loads_m, loads_w = (
        [None] * 2
        + [pltpu.make_async_copy(source[i], target[i], sem.at[kind, i]) for i in range(2, 7)]
        for kind, (source, target) in enumerate(((moment_in, moment), (weight_in, weight)))
    )
    thirds = [slice(3 * part, 3 * part + 3) for part in range(3)]

    def three_parts(source, target, spans, first):
        return [
            pltpu.make_async_copy(source.at[span], target.at[span], tap_sem.at[first + part])
            for part, span in enumerate(spans)
        ]

    taps_m = three_parts(moment_in[0], moment[0], range(3), 0)
    taps_w = three_parts(weight_in[0], weight[0], range(3), 3)
    parts_m = three_parts(moment_in[1], moment[1], thirds, 6)
    parts_w = three_parts(weight_in[1], weight[1], thirds, 9)
    loads[0].start()
    loads_m[2].start()
    for tap, low in ((1, REDUCE_1), (0, REDUCE_0), (2, REDUCE_2)):
        loads[low].start()
        taps_m[tap].start()
    stores, moving = [], []
    for place, (source, target) in enumerate(zip(kept, keep)):
        rows = source.shape[0] // PARTS
        for part in range(PARTS):
            span = pl.ds(rows * part, rows)
            made = pltpu.make_async_copy(
                source.at[span], target.at[span], keep_in.at[place, part]
            )
            moving.append((place, part, span, made))
    later = [loads[1024], *parts_m, loads_m[3]]
    later += [loads[low] for low in (LATERAL_2, LATERAL_0, TINY)] + loads_m[4:7] + loads_n
    later += [each[3] for each in moving] + [loads_w[2], *taps_w, *parts_w, *loads_w[3:7]]

    def start_next(count):
        for _ in range(min(count, len(later))):
            later.pop(0).start()

    def move(count):
        for _ in range(min(count * PARTS // 2, len(moving))):
            place, part, span, made = moving.pop(0)
            made.wait()
            source = keep[place]
            if source.dtype != kept_out[place].dtype:
                source = wide_keep[place - 2]
                size = keep[place].shape[0] // 14
                each = 14 // PARTS

                def widen(number, carry, place=place, size=size):
                    rows = pl.ds(pl.multiple_of(number * size, 16), size)
                    wide_keep[place - 2][rows, :] = keep[place][rows, :].astype(F32)
                    return carry

                lax.fori_loop(each * part, each * (part + 1), widen, 0)
            stores.append(
                pltpu.make_async_copy(
                    source.at[span], kept_out[place].at[span], keep_out.at[place, part]
                )
            )
            stores[-1].start()

    sent = []

    def send(source, target):
        sent.append(pltpu.make_async_copy(source, target, out_sem.at[len(sent)]))
        sent[-1].start()

    scales = []

    def close(number, gram):
        inverse = norm_of(gram, 256)
        scales.append(inverse)
        chain_a[number] = gram * (inverse * inverse)

    loads[0].wait()
    loads_m[2].wait()
    gram = jnp.zeros((256, 256), F32)
    for block in range(4):
        cols, rows = (slice(256 * block, 256 * (block + 1)) for _ in range(2))
        new = MU * moment[2][:, cols] + g_buf[rows, :].astype(F32)
        moment[2][:, cols] = new
        low = new.astype(BF)
        low_buf[rows, :] = low
        gram = gram + dot_nt(low, low)
    send(moment[2], moment_out[2])
    close(0, gram)
    start_next(15)

    gram = jnp.zeros((256, 256), F32)
    for tap, low_row in ((1, REDUCE_1), (0, REDUCE_0), (2, REDUCE_2)):
        loads[low_row].wait()
        taps_m[tap].wait()
        if tap == 0:
            start_next(4 * PARTS // 2)
        if tap == 2:
            start_next(len(later))
        for part in range(4):
            rows = slice(256 * part, 256 * (part + 1))
            span = slice(low_row + 256 * part, low_row + 256 * (part + 1))
            new = MU * moment[0][tap, rows, :] + g_buf[span, :].T.astype(F32)
            moment[0][tap, rows, :] = new
            low_buf[span, :] = new.astype(BF)
        send(moment[0].at[tap], moment_out[0].at[tap])
        low = low_buf[low_row : low_row + 1024, :]
        gram = gram + dot_tn(low, low)
    close(1, gram)
    move(1)

    loads[1024].wait()
    gram = jnp.zeros((256, 256), F32)
    for part, taps in enumerate(thirds):
        parts_m[part].wait()
        span = slice(1024 + 768 * part, 1792 + 768 * part)
        new = MU * moment[1][taps].reshape(768, 256) + g_buf[span, :].astype(F32)
        moment[1][taps] = new.reshape(3, 256, 256)
        send(moment[1].at[taps], moment_out[1].at[taps])
        low = new.astype(BF)
        low_buf[span, :] = low
        gram = gram + dot_tn(low, low)
    close(2, gram)
    move(1)

    loads_m[3].wait()
    loads[LATERAL_2].wait()
    loads[LATERAL_0].wait()
    first = g_buf[LATERAL_0 : LATERAL_0 + 256, :].T
    second = g_buf[LATERAL_2 : LATERAL_2 + 256, :].T
    third = g_buf[LATERAL_2 + 256 : LATERAL_2 + 384, :]
    third = jnp.concatenate([third[:, :128], third[:, 128:]], axis=0).T
    turned = jnp.concatenate([first, second, third], axis=0).astype(F32)
    new = MU * moment[3][...].reshape(640, 256) + turned
    moment[3][...] = new.reshape(5, 128, 256)
    lateral_low = new.astype(BF)
    send(moment[3], moment_out[3])
    close(3, dot_tn(lateral_low, lateral_low))
    move(1)

    for each in loads_n:
        each.wait()
    for kind in range(2):
        for part in range(7):
            lanes = slice(256 * part, min(256 * (part + 1), norms[0].shape[1]))
            row, width = slice(kind, kind + 1), lanes.stop - lanes.start
            grad = norm_grad[8 * kind + part : 8 * kind + part + 1, :width]
            news = adam_step(*(each[row, lanes] for each in norms), grad)
            for target, new in zip(norms_out, news):
                target[row, lanes] = new
    for place in range(3):
        stores.append(
            pltpu.make_async_copy(norms_out[place], norms_target[place], norm_sem.at[4 + place])
        )
        stores[-1].start()

    loads[TINY].wait()
    for i in (4, 5, 6):
        loads_m[i].wait()
    tiny = g_buf[TINY : TINY + 128, :].astype(F32)
    reduce_new = []
    for tap in range(3):
        rows, cols = 32 * (tap // 2), 128 * (tap % 2)
        new = MU * moment[4][tap] + tiny[rows : rows + 32, cols : cols + 128]
        moment[4][tap] = new
        reduce_new.append(new)
    expand_new = MU * moment[6][...] + tiny[32:64, 128:256]
    moment[6][...] = expand_new
    spatial_new = []
    for tap in range(9):
        block = tiny[64 + 32 * (tap // 8) : 96 + 32 * (tap // 8), 128 * (tap % 8 // 4) :][:, :128]
        if tap % 4:
            block = pltpu.roll(block, 128 - 32 * (tap % 4), 1)
        new = MU * moment[5][tap] + block[:, :32]
        moment[5][tap] = new
        spatial_new.append(new)
    for i in (4, 5, 6):
        send(moment[i], moment_out[i])
    grams = (
        sum(gram_tn(new) for new in spatial_new),
        sum(gram_nt(new) for new in reduce_new),
        gram_nt(expand_new),
    )
    tiny_scales = [norm_of(gram, 32) for gram in grams]
    blocks = []
    for place, (gram, inverse) in enumerate(zip(grams, tiny_scales)):
        wide = jnp.concatenate([gram * (inverse * inverse), jnp.zeros((32, 96), F32)], axis=1)
        blocks.append(pltpu.roll(wide, 32 * place, 1) if place else wide)
    blocks.append(jnp.zeros((32, 128), F32))
    small_a[...] = jnp.concatenate(blocks, axis=0)
    move(1)

    chains = [(chain_a.at[n], chain_p.at[n]) for n in range(4)] + [(small_a, small_p)]
    for step in newton_steps():
        step(chains)
        move(1)

    loads_w[2].wait()
    poly = (chain_p[0] * (2.0 * LR * scales[0])).astype(BF)
    for block in range(4):
        cols, rows = (slice(256 * block, 256 * (block + 1)) for _ in range(2))
        weight[2][:, cols] = weight[2][:, cols] - dot(poly, low_buf[rows, :])
    send(weight[2], weight_out[2])

    poly = (chain_p[1] * (LR * scales[1])).astype(BF)
    for tap, low_row in enumerate((REDUCE_0, REDUCE_1, REDUCE_2)):
        taps_w[tap].wait()
        low = low_buf[low_row : low_row + 1024, :]
        weight[0][tap] = weight[0][tap] - dot(low, poly)
        send(weight[0].at[tap], weight_out[0].at[tap])

    poly = (chain_p[2] * (LR * scales[2])).astype(BF)
    for part, taps in enumerate(thirds):
        parts_w[part].wait()
        change = dot(low_buf[1024 + 768 * part : 1792 + 768 * part, :], poly)
        weight[1][taps] = weight[1][taps] - change.reshape(3, 256, 256)
        send(weight[1].at[taps], weight_out[1].at[taps])

    loads_w[3].wait()
    poly = (chain_p[3] * (LR * scales[3])).astype(BF)
    weight[3][...] = weight[3][...] - dot(lateral_low, poly).reshape(5, 128, 256)
    send(weight[3], weight_out[3])
    for i in (4, 5, 6):
        loads_w[i].wait()
    tiny_p = small_p[...].astype(BF)
    for tap in range(9):
        change = dot(moment[5][tap].astype(BF), tiny_p[:32, :32])
        weight[5][tap] = weight[5][tap] - LR * tiny_scales[0] * change
    none = jnp.zeros((32, 128), BF)
    for tap in range(3):
        stack = jnp.concatenate([none, moment[4][tap].astype(BF), none, none], axis=0)
        weight[4][tap] = weight[4][tap] - LR * tiny_scales[1] * dot(tiny_p[32:64, :], stack)
    stack = jnp.concatenate([none, none, moment[6][...].astype(BF), none], axis=0)
    weight[6][...] = weight[6][...] - LR * 2.0 * tiny_scales[2] * dot(tiny_p[64:96, :], stack)
    for i in (4, 5, 6):
        send(weight[i], weight_out[i])
    move(len(moving))
    for made in stores + sent:
        made.wait()


def muon(grads, norm_grad, norms, weights, moments_old, kept):
    shapes = [jax.ShapeDtypeStruct(each.shape, F32) for each in weights]
    types = (BF, BF, F32, F32)
    same = [jax.ShapeDtypeStruct(each.shape, kind) for each, kind in zip(kept, types)]
    dma = pltpu.SemaphoreType.DMA
    out = pl.pallas_call(
        muon_kernel,
        out_shape=shapes + shapes + same + [jax.ShapeDtypeStruct(norms[0].shape, F32)] * 3,
        in_specs=[ANYWHERE] * 23,
        out_specs=[ANYWHERE] * 21,
        scratch_shapes=[pltpu.VMEM(grads.shape, BF)]
        + [pltpu.VMEM(each.shape, F32) for each in weights] * 2
        + [pltpu.VMEM(each.shape, each.dtype) for each in kept]
        + [
            pltpu.VMEM((4, 256, 256), F32),
            pltpu.VMEM((4, 256, 256), F32),
            pltpu.VMEM((128, 128), F32),
            pltpu.VMEM((128, 128), F32),
            pltpu.VMEM(grads.shape, BF),
            pltpu.VMEM(kept[2].shape, F32),
            pltpu.VMEM(kept[3].shape, F32),
            dma((2, 7)),
            dma((8,)),
            dma((12,)),
            dma((24,)),
            dma((4, PARTS)),
            dma((4, PARTS)),
            dma((7,)),
            pltpu.VMEM(norm_grad.shape, F32),
        ]
        + [pltpu.VMEM(norms[0].shape, F32)] * 6,
        compiler_params=pltpu.CompilerParams(vmem_limit_bytes=VMEM_LIMIT),
        name="muon",
    )(grads, norm_grad, *norms, *weights, *moments_old, *kept)
    return out[:7], out[7:14], out[14:18], out[18:]


def sigmoid(value):
    return 0.5 * jnp.tanh(0.5 * value) + 0.5


def spread(row):
    return jnp.broadcast_to(row, (8, row.shape[1]))


def tiled(value):
    value = value + pltpu.roll(value, 64, 1)
    return value + pltpu.roll(value, 32, 1)


def block_kernel(n_dp, n_group, frames, side, pieces, *refs):
    slow_in, fast_in, slow_cot, fast_cot, starts, ends = refs[:6]
    w_reduce, w_spatial, w_expand, w_lateral = refs[6:10]
    small_in = refs[10:14]
    slow_out, fast_out, slow_grad, fast_grad, g_out, norm_out = refs[14:20]
    (
        xs, cs, xn, cf, fp, zf, df, ds, zc, za, zb, b1, b2, sa, fa, hsb, hfb, zfa, zfb, fx,
        dzf, h_t, wr, ws, we, wl, bt, fs, fst, fe, gbuf, masks, links, fast_mask, xh_in, hs, hr, fhs, fhr, st_a, st_c, st_f,
        load, store, h_send, h_recv, s_send, a_recv, c_recv, f_send, f_recv, summed, norm_loc, n_in, n_send, n_recv,
        g_save, f_reduce, f_spatial, f_expand, params, *sums_refs,
    ) = refs[20:]
    pixels = side * side
    n_rows = pixels * frames
    line = side * frames
    dp, group = lax.axis_index("dp"), lax.axis_index("group")
    after = (lax.rem(dp + 1, n_dp), group)
    before = (lax.rem(dp + n_dp - 1, n_dp), group)
    peers = [(dp, lax.rem(group + step, n_group)) for step in range(1, n_group)]

    dp_peers = [(lax.rem(dp + step, n_dp), group) for step in range(1, n_dp)]
    barrier = pltpu.get_barrier_semaphore()
    for other in peers + dp_peers:
        pl.semaphore_signal(barrier, inc=1, device_id=other, device_id_type=MESH)

    loads = {}

    def fetch(name, source, target):
        loads[name] = pltpu.make_async_copy(source, target, load.at[len(loads) % LOADS])
        loads[name].start()

    def ready(*names):
        for name in names:
            loads[name].wait()

    half = n_rows // 2
    fetch("xn", fast_in, xn)
    for place, target in enumerate((f_reduce, f_spatial, f_expand, params)):
        fetch(("small", place), small_in[place], target)
    for tap in range(5):
        fetch(("wl", tap), w_lateral.at[tap], lateral_stage(zc, tap))
    fetch("wr0", w_reduce.at[0], zc.at[0:1024, 0:256])
    fetch("xs", slow_in, xs)
    fetch("wr2", w_reduce.at[2], zc.at[0:1024, 512:768])
    fetch("wr1", w_reduce.at[1], zc.at[0:1024, 256:512])
    for tap in range(9):
        fetch(("ws", tap), w_spatial.at[tap], spatial_stage(zc, tap))
    for block in range(4):
        fetch(
            ("we", block),
            w_expand.at[:, 256 * block : 256 * (block + 1)],
            zb.at[256 * block : 256 * (block + 1)],
        )
    fetch("cs", slow_cot, cs)
    fetch("cf", fast_cot, cf)

    first = dp * frames
    row_id = lax.broadcasted_iota(jnp.int32, (frames, 128), 0)
    lane = lax.broadcasted_iota(jnp.int32, (8, 128), 1)

    def info(offset, rows):
        frame = first + offset + rows
        inside = jnp.zeros(rows.shape, jnp.int32)
        begun = jnp.zeros(rows.shape, jnp.int32)
        for slot in range(starts.shape[1]):
            open_ = frame >= starts[0, slot]
            begun = begun + jnp.where(open_, 1, 0)
            inside = jnp.where(open_ & (frame < ends[0, slot]), 1, inside)
        return inside, begun

    own, own_segment = info(0, row_id)
    valid = own.astype(F32)
    for offset, place in ((-1, 0), (1, 1)):
        near, near_segment = info(offset, row_id)
        both = jnp.where((own * near == 1) & (own_segment == near_segment), 1.0, 0.0)
        links[8 * place : 8 * place + 8, 0:128] = both.astype(F32)
        links[8 * place : 8 * place + 8, 128:256] = both.astype(F32)
        inner = jnp.where(row_id == (0, frames - 1)[place], 0.0, both).astype(F32)
        links[16 + 8 * place : 24 + 8 * place, 0:128] = inner
        links[16 + 8 * place : 24 + 8 * place, 128:256] = inner
    for block in range(8):
        masks[0:8, 128 * block : 128 * (block + 1)] = valid
    fast_id = lax.broadcasted_iota(jnp.int32, (4 * frames, 128), 0)
    fast_valid = info(0, fast_id >> 2)[0].astype(F32)
    fast_mask[...] = fast_valid
    count_local = jnp.sum(valid, axis=0, keepdims=True) * float(pixels)
    count_block = spread(count_local)

    def chunk(number, size):
        return pl.ds(pl.multiple_of(number * size, 16), size)

    def three(value):
        return value.reshape(-1, 8, value.shape[-1])

    def fold(value):
        return jnp.sum(three(value), axis=0)

    def pair(ref, rows):
        return jnp.concatenate([ref[0, rows, :], ref[1, rows, :]], axis=1)

    def set_pair(ref, rows, value):
        ref[0, rows, :] = value[:, :128]
        ref[1, rows, :] = value[:, 128:]

    def loop(count, body, carry=0):
        return lax.fori_loop(0, count, body, carry)

    def zeros(*shape):
        return jnp.zeros(shape, F32)

    depth = n_dp // 2
    core, side_y = lax.rem(group, 2), group // 2
    side_x, side_z = lax.rem(dp, 2), dp // 2
    pair_core = (dp, group + 1 - 2 * core)
    sides = {"x": side_x, "y": side_y}
    over = {"x": (dp + 1 - 2 * side_x, group), "y": (dp, group + 2 - 4 * side_y)}
    live = {}

    def at(ref, start, size):
        return ref.at[pl.ds(pl.multiple_of(start, 16), size)]

    def regions(place):
        start, size = pieces[place]
        base = start + core * (size // 2)
        sizes = stage_sizes(place, size, depth)
        result = []
        for way, axes in enumerate(orders_of(place)):
            offset = base + way * (size // 4)
            offsets = [offset]
            for axis, (rows, _) in zip(axes, sizes):
                offset = offset + (side_z if axis == "z" else sides[axis]) * rows
                offsets.append(offset)
            result.append(offsets)
        return base, sizes, result

    def begin(place):
        number = live[place][0]
        start, size = pieces[place]
        send, recv = sums_refs[5 * place + 3 : 5 * place + 5]
        base, sizes, offsets = regions(place)
        made = []

        def add_copy(source, target, device):
            made.append(
                pltpu.make_async_remote_copy(
                    src_ref=source,
                    dst_ref=target,
                    send_sem=send.at[0],
                    recv_sem=recv.at[number],
                    device_id=device,
                    device_id_type=MESH,
                )
            )

        if number == 0:
            other = start + (1 - core) * (size // 2)
            add_copy(at(gbuf, other, size // 2), at(summed, other, size // 2), pair_core)
        elif number == 7:
            add_copy(at(summed, base, size // 2), at(summed, base, size // 2), pair_core)
        else:
            stage = number - 1 if number < 4 else 6 - number
            rows, _ = sizes[stage]
            into = sums_refs[5 * place + stage]
            for way, axes in enumerate(orders_of(place)):
                axis, before_ = axes[stage], offsets[way][stage]
                mine = at(summed, offsets[way][stage + 1], rows)
                if axis == "z":
                    for step in range(1, depth):
                        other = lax.rem(side_z + step, depth)
                        device = (other * 2 + side_x, group)
                        if number < 4:
                            source = at(gbuf, before_ + other * rows, rows)
                            add_copy(source, into.at[way, step - 1], device)
                        else:
                            add_copy(mine, mine, device)
                elif number < 4:
                    source = at(gbuf, before_ + (1 - sides[axis]) * rows, rows)
                    add_copy(source, into.at[way, 0], over[axis])
                else:
                    add_copy(mine, mine, over[axis])
        for each in made:
            each.start()
        if 0 < number < 7:
            made = []
            add_copy(into, into, pair_core)
        live[place] = (number, made[0])

    def add_rows(start, size, target, sources):
        step_rows = math.gcd(size, 64)

        def step(number, carry):
            row = pl.multiple_of(number * step_rows, 16)
            rows = pl.ds(pl.multiple_of(start + row, 16), step_rows)
            total = gbuf[rows, :].astype(F32)
            for source in sources(row, step_rows, rows):
                total = total + source.astype(F32)
            target[rows, :] = total.astype(BF)
            return carry

        lax.fori_loop(0, size // step_rows, step, 0)

    def finish(place):
        number, made = live[place]
        start, size = pieces[place]
        base, sizes, offsets = regions(place)
        made.wait()
        if number == 0:
            add_rows(base, size // 2, gbuf, lambda row, count, rows: [summed[rows, :]])
        elif number < 4:
            rows_, messages = sizes[number - 1]
            into = sums_refs[5 * place + number - 1]
            for way in range(2):
                add_rows(
                    offsets[way][number],
                    rows_,
                    summed if number == 3 else gbuf,
                    lambda row, count, rows, way=way: [
                        into[way, message, pl.ds(row, count), :] for message in range(messages)
                    ],
                )
        elif number == 7:
            save = pltpu.make_async_copy(
                summed.at[start : start + size], g_out.at[start : start + size], g_save.at[place]
            )
            save.start()
            saves.append(save)
        live[place] = (number + 1, None) if number < 7 else None

    saves, norm_made = [], []

    def share_norms():
        n_in[dp] = norm_loc[...]
        for peer in dp_peers:
            norm_made.append(
                pltpu.make_async_remote_copy(
                    src_ref=n_in.at[dp],
                    dst_ref=n_in.at[dp],
                    send_sem=n_send.at[0],
                    recv_sem=n_recv.at[0],
                    device_id=peer,
                    device_id_type=MESH,
                )
            )
            norm_made[-1].start()

    def launch(ready_rows):
        for place, (start, size) in enumerate(pieces):
            if place not in live and start + size <= ready_rows:
                live[place] = (0, None)
                begin(place)

    def point(name):
        pump(*PUMPS.get(name, ()))

    def pump(*places):
        for place in places:
            if live.get(place):
                finish(place)
                if live[place]:
                    begin(place)


    row8 = lax.broadcasted_iota(jnp.int32, (8, 1), 0)

    def share(store_ref, sends, recvs, place, sums, squares, extra=None):
        top = jnp.sum(sums, axis=0, keepdims=True)
        second = jnp.sum(squares, axis=0, keepdims=True)
        block = jnp.where(row8 == 0, top, jnp.where(row8 == 1, second, 0.0))
        if extra is not None:
            block = jnp.where(row8 == 2, extra, block)
        store_ref[place, group] = block
        made = []
        for peer in peers:
            made.append(
                pltpu.make_async_remote_copy(
                    src_ref=store_ref.at[place, group],
                    dst_ref=store_ref.at[place, group],
                    send_sem=sends.at[0],
                    recv_sem=recvs.at[place],
                    device_id=peer,
                    device_id_type=MESH,
                )
            )
            made[-1].start()

        part = store_ref.at[place, 0 : n_group - 1]
        arrived = pltpu.make_async_remote_copy(
            src_ref=part,
            dst_ref=part,
            send_sem=sends.at[0],
            recv_sem=recvs.at[place],
            device_id=peers[0],
            device_id_type=MESH,
        )

        def receive():
            arrived.wait()
            total = store_ref[place, 0]
            for slot in range(1, n_group):
                total = total + store_ref[place, slot]
            return [spread(total[i : i + 1, :]) for i in range(3)]

        return receive

    def share_a(place, sums, squares):
        return share(st_a, s_send, a_recv, place, sums, squares)

    def share_c(place, sums, squares):
        return share(st_c, s_send, c_recv, place, sums, squares)

    def share_f(place, sums, squares, extra=None):
        return share(st_f, f_send, f_recv, place, sums, squares, extra)

    def coefs(total, squares, count, gain, bias):
        mean = total / count
        inverse = lax.rsqrt(squares / count - mean * mean + EPS)
        slope_a = gain * inverse
        return mean, inverse, slope_a, bias - mean * slope_a

    def back_coefs(total, cross, count, mean, inverse, slope_a):
        c3 = slope_a * inverse * cross / count
        return slope_a * total / count - mean * c3, c3

    def param(kind, place):
        row = slice(kind, kind + 1)
        if place < 2:
            return spread(params[row, 256 * place : 256 * place + 256])
        if place == 2:
            return spread(params[row, 512:1536])
        low = spread(params[row, 1536:1664])
        rest = params[row, 1664:]
        none = zeros(1, 128 - rest.shape[1])
        high = spread(jnp.concatenate([rest, none], axis=1))
        if place == 3:
            return tiled(jnp.where(lane < 32, low, 0.0))
        if place == 4:
            return tiled(jnp.where((lane >= 32) & (lane < 64), low, 0.0))
        return jnp.where(lane < 64, pltpu.roll(low, 64, 1), pltpu.roll(high, 64, 1))

    if gbuf.shape[0] > ROWS:
        gbuf[ROWS:, :] = jnp.zeros((gbuf.shape[0] - ROWS, 256), BF)

    ready("xn")

    def widen(number, carry):
        rows = chunk(number, 4 * 2 * line)
        zf[rows, :] = xn[rows, :].astype(F32)
        return carry

    loop(side // 2, widen)

    def pack(source, target):
        def step(number, carry):
            size = 2 * line
            start = pl.multiple_of(number * 4 * size, 16)
            for q in range(4):
                target[chunk(number, size), 128 * q : 128 * q + 128] = source[
                    pl.ds(start + q, size, stride=4), :
                ].astype(BF)
            return carry

        loop(side // 2, step)

    pack(zf, fp)

    for place in range(4):
        ready(("small", place))
    bt[...] = jnp.zeros(bt.shape, BF)
    for tap in range(3):
        low = f_reduce[tap].astype(BF)
        for q in range(4):
            other = q + tap - 1
            if 0 <= other < 4:
                bt[32 * q : 32 * q + 32, 128 * other : 128 * other + 128] = low
    bt[128:160, 384:512] = f_reduce[0].astype(BF)
    bt[224:256, 0:128] = f_reduce[2].astype(BF)
    fe[...] = jnp.zeros(fe.shape, BF)
    for q in range(4):
        fe[32 * q : 32 * q + 32, 128 * q : 128 * q + 128] = f_expand[...].astype(BF)
    for tap in range(9):
        wide = jnp.concatenate([f_spatial[tap], zeros(32, 96)], axis=1)
        for q in range(4):
            fs[tap, 32 * q : 32 * q + 32, :] = (
                pltpu.roll(wide, 32 * q, 1) if q else wide
            ).astype(BF)
        side_b = 128 * (tap % 3)
        fst[tap // 3, side_b : side_b + 128, :] = fs[tap].T

    for tap in range(5):
        ready(("wl", tap))
        wl[128 * tap : 128 * tap + 128, :] = lateral_stage(zc, tap)[...].astype(BF)

    def lower_reduce(tap):
        ready("wr%d" % tap)

        def step(number, carry):
            rows = chunk(number, 128)
            wr[tap, rows, :] = zc[rows, 256 * tap : 256 * tap + 256].astype(BF)
            return carry

        loop(8, step)

    def edges(number, carry):
        rows = chunk(number, half)
        set_pair(b1, rows, dot(xs[rows, :], wr[0]) + dot(fp[rows, 256:512], wl[0:256, :]))
        set_pair(b2, rows, dot(xs[rows, :], wr[2]))
        return carry

    def fast_first(number, carry):
        rows = chunk(number, half)
        both = dot_nt(fp[rows, :], bt[...])
        zfa[rows, :] = (three(both[:, :128]) * masks[0:8, 0:128]).reshape(half, 128)
        fx[rows, :] = both[:, 128:]
        return carry

    ends_ = pl.ds(frames - 1, pixels, stride=frames)
    heads = pl.ds(0, pixels, stride=frames)

    def halo_copy(ref, place, way, sems):
        made = pltpu.make_async_remote_copy(
            src_ref=ref[0].at[place + way],
            dst_ref=ref[1].at[place + way],
            send_sem=h_send.at[sems, place + way],
            recv_sem=h_recv.at[sems, place + way],
            device_id=(after, before)[way],
            device_id_type=MESH,
        )
        pl.when((dp < n_dp - 1, dp > 0)[way])(made.start)
        return made

    def halo_wait(made):
        @pl.when(dp < n_dp - 1)
        def _():
            made[0].wait_send()
            made[1].wait_recv()

        @pl.when(dp > 0)
        def _():
            made[1].wait_send()
            made[0].wait_recv()

    for way, edge in enumerate((0, n_dp - 1)):

        @pl.when(dp == edge)
        def _(way=way):
            xh_in[way] = jnp.zeros(xh_in.shape[1:], BF)
            for place in (way, 2 + way):
                hr[place] = jnp.zeros(hr.shape[1:], BF)
                fhr[place] = jnp.zeros(fhr.shape[1:], BF)

    def send_halo(place, last, zero):
        for part in range(2):
            hs[place, part, 0:pixels, :] = last[part, ends_, :].astype(BF)
            hs[place + 1, part, 0:pixels, :] = zero[part, heads, :].astype(BF)
        return [halo_copy((hs, hr), place, way, 0) for way in range(2)]

    def take_halo(made, place, last, zero):
        halo_wait(made)
        for part in range(2):
            last[part, ends_, :] = hr[place, part, 0:pixels, :].astype(F32)
            zero[part, heads, :] = hr[place + 1, part, 0:pixels, :].astype(F32)

    block_rows = -(-pixels // 64) * 16
    lanes_ = lax.broadcasted_iota(jnp.int32, (block_rows, 128), 1)
    fill = zeros(4 * block_rows - pixels, 128)

    def send_fast_halo(place, ref, first_lanes):
        for way, (rows, first_lane) in enumerate(zip((ends_, heads), first_lanes)):
            value = jnp.concatenate([ref[rows, :], fill], axis=0)
            total = zeros(block_rows, 128)
            for q in range(4):
                piece = value[block_rows * q : block_rows * (q + 1)]
                turn = (32 * q - first_lane) % 128
                piece = pltpu.roll(piece, turn, 1) if turn else piece
                total = jnp.where((lanes_ >= 32 * q) & (lanes_ < 32 * q + 32), piece, total)
            fhs[place + way] = total.astype(BF)
        return [halo_copy((fhs, fhr), place, way, 1) for way in range(2)]

    def take_fast_halo(made, place, first_lanes):
        halo_wait(made)
        result = []
        for way, first_lane in enumerate(first_lanes):
            value = fhr[place + way].astype(F32)
            pieces_ = []
            for q in range(4):
                turn = (first_lane - 32 * q) % 128
                piece = pltpu.roll(value, turn, 1) if turn else value
                keep = (lanes_ >= first_lane) & (lanes_ < first_lane + 32)
                pieces_.append(jnp.where(keep, piece, 0.0))
            result.append(jnp.concatenate(pieces_, axis=0)[:pixels])
        return result

    low = lax.broadcasted_iota(jnp.int32, (pixels, 128), 1) < 64

    def silu_of(value, slope_a, shift):
        norm = value * slope_a + shift
        return norm * sigmoid(norm)

    def slope_of(norm):
        gate = sigmoid(norm)
        return gate + norm * gate * (1.0 - gate)

    def shifted(ref, y, value, flip):
        width = value.shape[1]
        edge = zeros(frames, width)
        back = jnp.concatenate([edge, value[: line - frames]], axis=0).astype(BF)
        ahead = jnp.concatenate([value[frames:], edge], axis=0).astype(BF)
        ref[y + 1, :, 0:width] = ahead if flip else back
        ref[y + 1, :, width : 2 * width] = value.astype(BF)
        ref[y + 1, :, 2 * width : 3 * width] = back if flip else ahead

    def spatial(z_ref, pad_ref, weight, width, slope_a, shift, out_ref):
        def hide(y, carry):
            value = silu_of(three(z_ref[chunk(y, line), :]), slope_a, shift)
            value = value * masks[0:8, 0:width]
            shifted(pad_ref, y, value.reshape(line, width), False)
            return carry

        loop(side, hide)
        tall = side // 2

        def step(number, carry):
            total = zeros(half, width)
            for a in range(3):
                patch = pad_ref[pl.ds(number * tall + a, tall)].reshape(half, 3 * width)
                total = total + dot(patch, weight(a))
            out_ref[chunk(number, half), :] = total
            return carry[0] + fold(total), carry[1] + fold(total * total)

        return loop(2, step, (zeros(8, width), zeros(8, width)))

    def hide_to(z_ref, target, width, slope_a, shift):
        def hide(y, carry):
            rows = chunk(y, line)
            value = silu_of(three(z_ref[rows, :]), slope_a, shift) * masks[0:8, 0:width]
            target[rows, :] = value.reshape(line, width).astype(BF)
            return carry

        loop(side, hide)

    def unpacked(ref, number, size, value, add):
        start = pl.multiple_of(number * 4 * size, 16)
        for q in range(4):
            place = pl.ds(start + q, size, stride=4)
            piece = value[:, 128 * q : 128 * q + 128]
            ref[place, :] = ref[place, :] + piece if add else piece

    def four(value):
        return value[:, 0:128] + value[:, 128:256] + value[:, 256:384] + value[:, 384:512]

    fast_line = 4 * line

    def quad(value):
        return value.reshape(-1, 4, 8, 128)

    def fold_quad(value):
        return jnp.sum(value.reshape(-1, 8, 128), axis=0)

    def through(z_ref, rows, back, slope_a, shift):
        z = three(z_ref[rows, :])
        grad = three(back) * slope_of(z * slope_a + shift)
        return grad, jnp.sum(grad, axis=0), jnp.sum(grad * z, axis=0)

    def scaled_sums(sums, mean, inverse):
        return sums[0], inverse * (sums[1] - mean * sums[0])

    def back_spatial(dy, z_ref, pad_ref, width, slope_a, c2, c3):
        def step(y, carry):
            rows = chunk(y, line)
            grad = slope_a * three(dy(rows)) - masks[0:8, 0:width] * (c2 + c3 * three(z_ref[rows, :]))
            shifted(pad_ref, y, grad.reshape(line, width), True)
            return carry

        loop(side, step)

    loop(2, fast_first)
    hs[...] = jnp.zeros(hs.shape, BF)
    pl.semaphore_wait(barrier, n_group + n_dp - 2)
    fast_halo = send_fast_halo(0, fx, (0, 96))

    lower_reduce(0)
    lower_reduce(2)
    ready("xs")
    loop(2, edges)
    halo = send_halo(0, b1, b2)

    def middle(number, carry):
        rows = chunk(number, 2 * line)
        total = dot(xs[rows, :], wr[1]) + dot(fp[rows, 0:384], wl[256:640, :])
        za[rows, :] = (three(total) * masks[0:8, 0:256]).reshape(2 * line, 256)
        return carry

    middle_parts = side // 2
    from_before, from_after = take_fast_halo(fast_halo, 0, (0, 96))
    fx[ends_, :] = jnp.where(low, from_before, fx[ends_, :])
    fx[heads, :] = jnp.where(low, fx[heads, :], from_after)

    def join_fast(number, carry):
        rows = chunk(number, line)
        cross = three(fx[rows, :])
        moved = jnp.where(
            lane < 64,
            links[0:8, 0:128] * pltpu.roll(cross, 1, 1),
            links[8:16, 0:128] * pltpu.roll(cross, frames - 1, 1),
        )
        total = three(zfa[rows, :]) + moved
        zfa[rows, :] = total.reshape(line, 128)
        return carry[0] + jnp.sum(total, axis=0), carry[1] + jnp.sum(total * total, axis=0)

    sums = loop(side, join_fast, (zeros(8, 128), zeros(8, 128)))
    got_fa = share_f(0, *sums, extra=count_block)
    lower_reduce(1)
    lax.fori_loop(0, middle_parts // 2, middle, 0)

    padded = xh_in.shape[1] // 5
    staged = gbuf.shape[0] - 10 * padded
    for way, rows in enumerate((ends_, heads)):
        for block in range(5):
            top = staged + (5 * way + block) * padded + pixels
            gbuf[top : top + padded - pixels, :] = jnp.zeros((padded - pixels, 256), BF)

    def stage(way, block, value):
        top, left = staged + (5 * way + block // 2) * padded, 128 * (block % 2)
        gbuf[top : top + pixels, left : left + 128] = value.astype(BF)

    for block in range(8):
        zfb[...] = xs[:, 128 * block : 128 * (block + 1)].astype(F32)
        stage(0, block, zfb[ends_, :])
        stage(1, block, zfb[heads, :])
    for q, way, block in ((2, 0, 8), (3, 0, 9), (0, 1, 8)):
        zfb[...] = fp[:, 128 * q : 128 * q + 128].astype(F32)
        stage(way, block, zfb[(ends_, heads)[way], :])
    stage(1, 9, zeros(pixels, 128))
    for tap in range(9):
        ready(("ws", tap))
        ws[256 * tap : 256 * tap + 256, :] = spatial_stage(zc, tap)[...].astype(BF)
    for block in range(4):
        ready(("we", block))
        we[:, 256 * block : 256 * block + 256] = zb[256 * block : 256 * block + 256, :].astype(BF)
    sa[0] = jnp.zeros((line, 768), BF)
    sa[side + 1] = jnp.zeros((line, 768), BF)
    fa[0] = jnp.zeros((line, 384), BF)
    fa[side + 1] = jnp.zeros((line, 384), BF)

    sums, squares, count = got_fa()
    fast_count = 4.0 * count
    counts = jnp.concatenate([count] * 8, axis=1)
    mean_fa, inv_fa, m_fa, s_fa = coefs(
        tiled(sums), tiled(squares), fast_count, param(0, 3), param(1, 3)
    )
    sums = spatial(
        zfa, fa, lambda a: fs[3 * a : 3 * a + 3].reshape(384, 128), 128, m_fa, s_fa, zfb
    )
    got_fb = share_f(1, *sums)

    lax.fori_loop(middle_parts // 2, middle_parts, middle, 0)
    take_halo(halo, 0, b1, b2)
    x_halo = []
    for way in range(2):
        made = pltpu.make_async_remote_copy(
            src_ref=gbuf.at[staged + 5 * padded * way : staged + 5 * padded * (way + 1)],
            dst_ref=xh_in.at[way],
            send_sem=h_send.at[2, way],
            recv_sem=h_recv.at[2, way],
            device_id=(after, before)[way],
            device_id_type=MESH,
        )
        pl.when((dp < n_dp - 1, dp > 0)[way])(made.start)
        x_halo.append(made)

    def join(number, carry):
        rows = chunk(number, line)
        total = three(za[rows, :])
        total = total + links[0:8, 0:256] * pltpu.roll(three(pair(b1, rows)), 1, 1)
        total = total + links[8:16, 0:256] * pltpu.roll(three(pair(b2, rows)), frames - 1, 1)
        za[rows, :] = total.reshape(line, 256)
        return carry[0] + jnp.sum(total, axis=0), carry[1] + jnp.sum(total * total, axis=0)

    sums = loop(side, join, (zeros(8, 256), zeros(8, 256)))
    got_sa = share_a(0, *sums)

    sums, squares, _ = got_fb()
    mean_fb, inv_fb, m_fb, s_fb = coefs(
        tiled(sums), tiled(squares), fast_count, param(0, 4), param(1, 4)
    )
    hide_to(zfb, hfb, 128, m_fb, s_fb)

    def expand_fast(number, carry):
        size = 2 * line
        total = dot(hfb[chunk(number, size), :], fe[...])
        unpacked(zf, number, size, total, False)
        return carry[0] + four(fold(total)), carry[1] + four(fold(total * total))

    sums = loop(side // 2, expand_fast, (zeros(8, 128), zeros(8, 128)))
    got_fc = share_f(2, *sums)

    sums, squares, _ = got_sa()
    mean_sa, inv_sa, m_sa, s_sa = coefs(sums, squares, counts[:, :256], param(0, 0), param(1, 0))
    sums = spatial(za, sa, lambda a: ws[768 * a : 768 * a + 768, :], 256, m_sa, s_sa, zb)
    got_sb = share_a(1, *sums)

    sums, squares, _ = got_fc()
    mean_fc, inv_fc, m_fc, s_fc = coefs(sums, squares, fast_count, param(0, 5), param(1, 5))
    ready("cf")

    def finish_fast(y, carry):
        rows = chunk(y, fast_line)
        z = quad(zf[rows, :])
        norm = z * m_fc + s_fc + quad(xn[rows, :].astype(F32))
        gate = sigmoid(norm)
        kept = gate * fast_mask[...].reshape(4, 8, 128)
        act = norm * kept
        grad = quad(cf[rows, :].astype(F32)) * (kept + act * (1.0 - gate))
        cf[rows, :] = act.reshape(fast_line, 128).astype(BF)
        df[rows, :] = grad.reshape(fast_line, 128)
        return carry[0] + fold_quad(grad), carry[1] + fold_quad(grad * z)

    sums = loop(side, finish_fast, (zeros(8, 128), zeros(8, 128)))
    back_fc = share_f(3, *scaled_sums(sums, mean_fc, inv_fc))
    save_fast = pltpu.make_async_copy(cf, fast_out, store.at[1])
    save_fast.start()

    sums, squares, _ = got_sb()
    mean_sb, inv_sb, m_sb, s_sb = coefs(sums, squares, counts[:, :256], param(0, 1), param(1, 1))
    def hide_part(part):
        rows = slice(2 * line * part, 2 * line * (part + 1))
        value = silu_of(three(zb[rows, :]), m_sb, s_sb) * masks[0:8, 0:256]
        hsb[rows, :] = value.reshape(2 * line, 256).astype(BF)

    hide_part(0)
    sums = (zeros(8, 1024), zeros(8, 1024))
    for part in range(side // 2):
        rows = slice(2 * line * part, 2 * line * (part + 1))
        total = dot(hsb[rows, :], we[...])
        if part + 1 < side // 2:
            hide_part(part + 1)
        zc[rows, :] = total
        sums = sums[0] + fold(total), sums[1] + fold(total * total)
    got_sc = share_c(0, *sums)

    norm_loc[...] = zeros(16, 256)
    total_fc, cross_fc, _ = back_fc()
    c2, c3 = back_coefs(total_fc, cross_fc, fast_count, mean_fc, inv_fc, m_fc)

    def back_fast(y, carry, c2=c2, c3=c3):
        rows = chunk(y, fast_line)
        mask = fast_mask[...].reshape(4, 8, 128)
        grad = m_fc * quad(df[rows, :]) - mask * (c2 + c3 * quad(zf[rows, :]))
        zf[rows, :] = grad.reshape(fast_line, 128)
        return carry

    loop(side, back_fast)
    pack(zf, dzf)

    def back_hidden_fast(number, carry):
        rows = chunk(number, half)
        back = dot_nt(dzf[rows, :], fe[...])
        grad, one, two = through(zfb, rows, back, m_fb, s_fb)
        fx[rows, :] = grad.reshape(half, 128)
        return carry[0] + one, carry[1] + two

    sums = loop(2, back_hidden_fast, (zeros(8, 128), zeros(8, 128)))
    back_fb = share_f(4, *scaled_sums(sums, mean_fb, inv_fb))
    wide = dot_tn(hfb[...], dzf[...])
    grad_fc = sum(wide[32 * q : 32 * q + 32, 128 * q : 128 * q + 128] for q in range(4))
    gbuf[TINY + 32 : TINY + 64, 128:256] = grad_fc.astype(BF)

    sums, squares, _ = got_sc()
    mean_sc, inv_sc, m_sc, s_sc = coefs(sums, squares, counts, param(0, 2), param(1, 2))
    ready("cs")

    def finish_slow(y, carry):
        rows = chunk(y, line)
        z = three(zc[rows, :])
        norm = z * m_sc + s_sc + three(xs[rows, :].astype(F32))
        gate = sigmoid(norm)
        kept = gate * masks[0:8, :]
        act = norm * kept
        grad = three(cs[rows, :].astype(F32)) * (kept + act * (1.0 - gate))
        cs[rows, :] = act.reshape(line, 1024).astype(BF)
        ds[rows, :] = grad.reshape(line, 1024).astype(BF)
        return carry[0] + jnp.sum(grad, axis=0), carry[1] + jnp.sum(grad * z, axis=0)

    sums = loop(side, finish_slow, (zeros(8, 1024), zeros(8, 1024)))
    back_sc = share_c(1, *scaled_sums(sums, mean_sc, inv_sc))
    save_slow = pltpu.make_async_copy(cs, slow_out, store.at[0])
    save_slow.start()

    total_fb, cross_fb, _ = back_fb()
    total_fb, cross_fb = tiled(total_fb), tiled(cross_fb)
    c2, c3 = back_coefs(total_fb, cross_fb, fast_count, mean_fb, inv_fb, m_fb)
    hfb[...] = fa[1 : side + 1, :, 128:256].reshape(n_rows, 128)
    back_spatial(lambda rows: fx[rows, :], zfb, fa, 128, m_fb, c2, c3)

    def back_first_fast(number, carry):
        rows = chunk(number, half)
        tall = side // 2
        back = zeros(half, 128)
        for a in range(3):
            patch = fa[pl.ds(number * tall + 2 - a, tall)].reshape(half, 384)
            back = back + dot(patch, fst[a])
        grad, one, two = through(zfa, rows, back, m_fa, s_fa)
        fx[rows, :] = grad.reshape(half, 128)
        return carry[0] + one, carry[1] + two

    sums = loop(2, back_first_fast, (zeros(8, 128), zeros(8, 128)))
    back_fa = share_f(5, *scaled_sums(sums, mean_fa, inv_fa))

    total, cross, _ = back_sc()
    for block in range(4):
        cols = slice(256 * block, 256 * (block + 1))
        norm_loc[2 + block : 3 + block, :] = cross[0:1, cols]
        norm_loc[10 + block : 11 + block, :] = total[0:1, cols]
    c2, c3 = back_coefs(total, cross, counts, mean_sc, inv_sc, m_sc)
    save_slow.wait()

    def back_part(part, c2=c2, c3=c3):
        for half_part in range(2):
            rows = slice(line * (2 * part + half_part), line * (2 * part + half_part + 1))
            grad = m_sc * three(ds[rows, :].astype(F32))
            grad = grad - masks[0:8, :] * (c2 + c3 * three(zc[rows, :]))
            cs[rows, :] = grad.reshape(line, 1024).astype(BF)

    back_part(0)
    sums = (zeros(8, 256), zeros(8, 256))
    for part in range(side // 2):
        rows = slice(2 * line * part, 2 * line * (part + 1))
        back = dot_nt(cs[rows, :], we[...])
        if part + 1 < side // 2:
            back_part(part + 1)
        grad, one, two = through(zb, rows, back, m_sb, s_sb)
        set_pair(b1, rows, grad.reshape(2 * line, 256))
        sums = sums[0] + one, sums[1] + two
    back_sb = share_a(2, *scaled_sums(sums, mean_sb, inv_sb))
    h_t[...] = hsb[...].T
    for block in range(4):
        cols = slice(256 * block, 256 * (block + 1))
        gbuf[cols, :] = dot(h_t[...], cs[:, cols]).astype(BF)
    launch(1024)

    total_fa, cross_fa, _ = back_fa()
    total_fa, cross_fa = tiled(total_fa), tiled(cross_fa)
    c2, c3 = back_coefs(total_fa, cross_fa, fast_count, mean_fa, inv_fa, m_fa)

    def back_one_fast(y, carry, c2=c2, c3=c3):
        rows = chunk(y, line)
        grad = m_fa * three(fx[rows, :]) - masks[0:8, 0:128] * (c2 + c3 * three(zfa[rows, :]))
        grad = grad.reshape(line, 128)
        zfb[rows, :] = grad
        dzf[rows, 0:128] = grad.astype(BF)
        return carry

    loop(side, back_one_fast)
    fast_halo = send_fast_halo(2, zfb, (96, 0))
    pump(0)

    total, cross, _ = back_sb()
    norm_loc[1:2, :] = cross[0:1, :]
    norm_loc[9:10, :] = total[0:1, :]
    c2, c3 = back_coefs(total, cross, counts[:, :256], mean_sb, inv_sb, m_sb)
    h_t[...] = sa[1 : side + 1, :, 256:512].reshape(n_rows, 256).T
    back_spatial(lambda rows: pair(b1, rows), zb, sa, 256, m_sb, c2, c3)

    def spatial_grad(tap, carry):
        for b in range(3):
            patch = sa[pl.ds(2 - tap, side), :, 256 * b : 256 * (b + 1)].reshape(n_rows, 256)
            place = pl.multiple_of(1024 + 768 * tap + 256 * b, 16)
            gbuf[pl.ds(place, 256), :] = dot(h_t[...], patch).astype(BF)
        return carry

    loop(3, spatial_grad)
    launch(REDUCE_1)
    point("a")

    def back_first(number, carry):
        rows = chunk(number, half)
        tall = side // 2
        back = zeros(half, 256)
        for a in range(3):
            for b in range(3):
                tap = 3 * a + b
                patch = sa[pl.ds(number * tall + 2 - a, tall), :, 256 * b : 256 * (b + 1)]
                back = back + dot_nt(patch.reshape(half, 256), ws[256 * tap : 256 * tap + 256, :])
        grad, one, two = through(za, rows, back, m_sa, s_sa)
        set_pair(b1, rows, grad.reshape(half, 256))
        return carry[0] + one, carry[1] + two

    sums = back_first(0, (zeros(8, 256), zeros(8, 256)))
    point("a2")
    sums = back_first(1, sums)
    back_sa = share_a(3, *scaled_sums(sums, mean_sa, inv_sa))
    point("b")

    lanes = lax.broadcasted_iota(jnp.int32, (32, 128), 1)
    tiles = [zeros(32, 128) for _ in range(3)]
    for a in range(3):
        patch = fa[2 - a : 2 - a + side].reshape(n_rows, 384)
        wide = dot_tn(hfb[...], patch)
        for b in range(3):
            tap = 3 * a + b
            for q in range(4):
                piece = wide[32 * q : 32 * q + 32, 128 * b : 128 * b + 128]
                turn = (32 * (tap % 4) - 32 * q) % 128
                piece = pltpu.roll(piece, turn, 1) if turn else piece
                inside = (lanes >= 32 * (tap % 4)) & (lanes < 32 * (tap % 4) + 32)
                tiles[tap // 4] = tiles[tap // 4] + jnp.where(inside, piece, 0.0)
    gbuf[TINY + 64 : TINY + 96, 0:128] = tiles[0].astype(BF)
    gbuf[TINY + 64 : TINY + 96, 128:256] = tiles[1].astype(BF)
    gbuf[TINY + 96 : TINY + 128, 0:128] = tiles[2].astype(BF)
    gbuf[TINY + 96 : TINY + 128, 128:256] = jnp.zeros((32, 128), BF)


    total, cross, _ = back_sa()
    norm_loc[0:1, :] = cross[0:1, :]
    norm_loc[8:9, :] = total[0:1, :]
    c2, c3 = back_coefs(total, cross, counts[:, :256], mean_sa, inv_sa, m_sa)

    def back_one(y, carry, c2=c2, c3=c3):
        rows = chunk(y, line)
        grad = m_sa * three(pair(b1, rows)) - masks[0:8, 0:256] * (c2 + c3 * three(za[rows, :]))
        grad = grad.reshape(line, 256)
        set_pair(b1, rows, grad)
        set_pair(b2, rows, grad)
        cs[rows, 512:768] = grad.astype(BF)
        return carry

    loop(side, back_one)
    point("c")
    halo = send_halo(2, b2, b1)
    point("d")
    for top, values in ((6, (cross_fa, cross_fb, cross_fc)), (14, (total_fa, total_fb, total_fc))):
        turned = pltpu.roll(values[2], 64, 1)
        left = jnp.where(lane < 32, values[0], jnp.where(lane < 64, values[1], turned))
        norm_loc[top : top + 1, 0:128] = left[0:1]
        norm_loc[top : top + 1, 128:256] = jnp.where(lane < 64, turned, 0.0)[0:1]
    share_norms()

    h_t[...] = cs[:, 512:768].T
    for block in range(4):
        cols = slice(256 * block, 256 * (block + 1))
        rows = slice(REDUCE_1 + 256 * block, REDUCE_1 + 256 * (block + 1))
        gbuf[rows, :] = dot(h_t[...], xs[:, cols]).astype(BF)
    wide = dot(h_t[...], fp[:, 0:384]).astype(BF)
    gbuf[LATERAL_2 : LATERAL_2 + 256, :] = wide[:, 0:256]
    gbuf[LATERAL_2 + 256 : LATERAL_2 + 384, 0:128] = wide[0:128, 256:384]
    gbuf[LATERAL_2 + 256 : LATERAL_2 + 384, 128:256] = wide[128:256, 256:384]
    launch(LATERAL_2 + 384)
    point("e")

    halo_wait(x_halo)

    def edge_rows(ref, rows, link):
        value = ref[rows, :] * link
        fill_rows = jnp.zeros((padded - pixels, 128), F32)
        return jnp.concatenate([value, fill_rows], axis=0).astype(BF)

    def neighbours(first_link):
        def step(y, carry):
            rows = chunk(y, line)
            back = links[first_link : first_link + 8, :]
            ahead = links[first_link + 8 : first_link + 16, :]
            up = ahead * pltpu.roll(three(pair(b1, rows)), frames - 1, 1)
            down = back * pltpu.roll(three(pair(b2, rows)), 1, 1)
            cs[rows, 0:256] = up.reshape(line, 256).astype(BF)
            cs[rows, 256:512] = down.reshape(line, 256).astype(BF)
            cross = three(zfb[rows, :])
            moved = jnp.where(
                lane < 64,
                ahead[:, :128] * pltpu.roll(cross, frames - 1, 1),
                back[:, :128] * pltpu.roll(cross, 1, 1),
            )
            moved = jnp.where((lane < 32) | (lane >= 96), moved, 0.0)
            dzf[rows, 128:256] = moved.reshape(line, 128).astype(BF)
            return carry

        loop(side, step)

    neighbours(16)
    link_back, link_ahead = links[0:1, 0:128], links[8 + frames - 1 : 8 + frames, 0:128]
    wide = dot_tn(dzf[:, 0:256], fp[...])
    parts = [zeros(32, 128) for _ in range(3)]
    for tap in range(3):
        for q in range(4):
            other = q + tap - 1
            if 0 <= other < 4:
                parts[tap] = parts[tap] + wide[
                    32 * q : 32 * q + 32, 128 * other : 128 * other + 128
                ]
    parts[0] = parts[0] + wide[128:160, 384:512]
    parts[2] = parts[2] + wide[224:256, 0:128]
    wide = dot_tn(edge_rows(zfb, heads, link_back), xh_in[0, 4 * padded :, 128:256])
    parts[0] = parts[0] + wide[0:32]
    wide = dot_tn(edge_rows(zfb, ends_, link_ahead), xh_in[1, 4 * padded :, 0:128])
    parts[2] = parts[2] + wide[96:128]
    gbuf[TINY : TINY + 32, 0:128] = parts[0].astype(BF)
    gbuf[TINY : TINY + 32, 128:256] = parts[1].astype(BF)
    gbuf[TINY + 32 : TINY + 64, 0:128] = parts[2].astype(BF)
    point("f")

    for way, (side_lanes, low_row, rows_, link) in enumerate(
        ((0, REDUCE_0, heads, link_back), (256, REDUCE_2, ends_, link_ahead))
    ):
        h_t[...] = cs[:, side_lanes : side_lanes + 256].T
        edge = [edge_rows(b1.at[part], rows_, link) for part in range(2)]
        edge = jnp.concatenate(edge, axis=1).T
        for block in range(4):
            cols = slice(256 * block, 256 * (block + 1))
            rows = slice(low_row + 256 * block, low_row + 256 * (block + 1))
            total = dot(h_t[...], xs[:, cols]) + dot(edge, xh_in[way, padded * block : padded * (block + 1), :])
            gbuf[rows, :] = total.astype(BF)
        if way == 0:
            total = dot(h_t[...], fp[:, 256:512]) + dot(edge, xh_in[0, 4 * padded :, :])
            gbuf[LATERAL_0 : LATERAL_0 + 256, :] = total.astype(BF)
            launch(REDUCE_2)
            point("g")
    launch(gbuf.shape[0])
    point("h")

    def input_grad_mid(number, carry):
        rows = chunk(number, half)
        total = ds[rows, :].astype(F32) + dot_nt(cs[rows, 512:768], wr[1])
        ds[rows, :] = total.astype(BF)
        return carry

    loop(2, input_grad_mid)
    point("i")
    take_halo(halo, 2, b2, b1)
    from_before, from_after = take_fast_halo(fast_halo, 2, (96, 0))
    zfb[ends_, :] = jnp.where(low, zfb[ends_, :], from_before)
    zfb[heads, :] = jnp.where(low, from_after, zfb[heads, :])
    neighbours(0)
    point("j")

    def input_grad(number, carry):
        rows = chunk(number, 2 * line)
        total = dot_nt(cs[rows, 0:256], wr[0])
        total = total + dot_nt(cs[rows, 256:512], wr[2])
        ds[rows, :] = (ds[rows, :].astype(F32) + total).astype(BF)
        return carry

    def input_grad_fast(number, carry):
        size = 2 * line
        rows = chunk(number, size)
        total = dot(dzf[rows, 0:256], bt[...])
        mid = dot_nt(cs[rows, 512:768], wl[256:640, :])
        up = dot_nt(cs[rows, 0:256], wl[0:256, :])
        total = total + jnp.concatenate([mid, zeros(size, 128)], axis=1)
        total = total + jnp.concatenate([zeros(size, 256), up], axis=1)
        unpacked(df, number, size, total, True)
        return carry

    parts_ = side // 2
    lax.fori_loop(0, parts_ // 2, input_grad_fast, 0)
    point("k")
    lax.fori_loop(parts_ // 2, parts_, input_grad_fast, 0)
    save_fast.wait()

    def narrow(y, carry):
        rows = chunk(y, fast_line)
        cf[rows, :] = df[rows, :].astype(BF)
        return carry

    loop(side, narrow)
    save_df = pltpu.make_async_copy(cf, fast_grad, store.at[3])
    save_df.start()
    point("l")
    lax.fori_loop(0, parts_ // 2, input_grad, 0)
    point("m")
    lax.fori_loop(parts_ // 2, parts_, input_grad, 0)
    save_ds = pltpu.make_async_copy(ds, slow_grad, store.at[4])
    save_ds.start()
    point("n")

    part = n_in.at[0 : n_dp - 1]
    pltpu.make_async_remote_copy(
        src_ref=part,
        dst_ref=part,
        send_sem=n_send.at[0],
        recv_sem=n_recv.at[0],
        device_id=dp_peers[0],
        device_id_type=MESH,
    ).wait()
    total = n_in[0]
    for slot in range(1, n_dp):
        total = total + n_in[slot]
    norm_loc[...] = total
    save_norm = pltpu.make_async_copy(norm_loc, norm_out, store.at[5])
    save_norm.start()
    while any(live.values()):
        point("z")
    save_norm.wait()
    for each in saves:
        each.wait()
    save_df.wait()
    save_ds.wait()


def spatial_stage(ref, tap):
    if tap == 8:
        return ref.at[0:256, 768:1024]
    top = 1024 + 256 * (tap // 4)
    return ref.at[top : top + 256, 256 * (tap % 4) : 256 * (tap % 4) + 256]


def lateral_stage(ref, tap):
    return ref.at[256 + 128 * tap : 384 + 128 * tap, 768:1024]


def block_call(mesh, frames, side, rows, operands):
    n_dp, n_group = mesh.shape["dp"], mesh.shape["group"]
    pixels = side * side
    n = pixels * frames
    line = side * frames
    dma = pltpu.SemaphoreType.DMA
    vmem = pltpu.VMEM
    shape = jax.ShapeDtypeStruct
    peers = n_group - 1
    pieces, depth = pieces_of(n_dp), n_dp // 2
    sums_scratch = []
    for place, (_, size) in enumerate(pieces):
        sizes = stage_sizes(place, size, depth)
        sums_scratch += [vmem((2, count, each, 256), BF) for each, count in sizes]
        sums_scratch += [dma((1,)), dma((8,))]
    return pl.pallas_call(
        partial(block_kernel, n_dp, n_group, frames, side, pieces),
        out_shape=(
            shape((n, 1024), BF),
            shape((4 * n, 128), BF),
            shape((n, 1024), BF),
            shape((4 * n, 128), BF),
            shape((rows, 256), BF),
            shape((16, 256), F32),
        ),
        in_specs=[ANYWHERE] * 4 + [SCALARS] * 2 + [ANYWHERE] * 8,
        out_specs=(ANYWHERE,) * 6,
        scratch_shapes=[
            vmem((n, 1024), BF),
            vmem((n, 1024), BF),
            vmem((4 * n, 128), BF),
            vmem((4 * n, 128), BF),
            vmem((n, 512), BF),
            vmem((4 * n, 128), F32),
            vmem((4 * n, 128), F32),
            vmem((n, 1024), BF),
            vmem((n, 1024), F32),
            vmem((n, 256), F32),
            vmem((n, 256), F32),
            vmem((2, n, 128), F32),
            vmem((2, n, 128), F32),
            vmem((side + 2, line, 768), BF),
            vmem((side + 2, line, 384), BF),
            vmem((n, 256), BF),
            vmem((n, 128), BF),
            vmem((n, 128), F32),
            vmem((n, 128), F32),
            vmem((n, 128), F32),
            vmem((n, 512), BF),
            vmem((256, n), BF),
            vmem((3, 1024, 256), BF),
            vmem((9 * 256, 256), BF),
            vmem((256, 1024), BF),
            vmem((640, 256), BF),
            vmem((256, 512), BF),
            vmem((9, 128, 128), BF),
            vmem((3, 384, 128), BF),
            vmem((128, 512), BF),
            vmem((rows, 256), BF),
            vmem((8, 1024), F32),
            vmem((32, 256), F32),
            vmem((32, 128), F32),
            vmem((2, 5 * (-(-pixels // 16) * 16), 256), BF),
            vmem((4, 2, -(-pixels // 16) * 16, 128), BF),
            vmem((4, 2, -(-pixels // 16) * 16, 128), BF),
            vmem((4, -(-pixels // 64) * 16, 128), BF),
            vmem((4, -(-pixels // 64) * 16, 128), BF),
            vmem((4, n_group, 8, 256), F32),
            vmem((2, n_group, 8, 1024), F32),
            vmem((6, n_group, 8, 128), F32),
            dma((LOADS,)),
            dma((6,)),
            dma((3, 4)),
            dma((3, 4)),
            dma((1,)),
            dma((4,)),
            dma((2,)),
            dma((1,)),
            dma((6,)),
            vmem((rows, 256), BF),
            vmem((16, 256), F32),
            vmem((n_dp, 16, 256), F32),
            dma((1,)),
            dma((1,)),
            dma((len(pieces),)),
        ]
        + [vmem(each.shape, F32) for each in operands[10:14]]
        + sums_scratch,
        compiler_params=pltpu.CompilerParams(
            collective_id=0, has_side_effects=True, vmem_limit_bytes=VMEM_LIMIT
        ),
        name="bottleneck",
    )(*operands)


def body(mesh, slow_in, fast_in, slow_cotangent, fast_cotangent, clip_start, clip_end, *rest):
    weights, moments_old, norms = rest[:7], rest[7:14], rest[14:]
    frames, side, slow_width = slow_in.shape[1], slow_in.shape[2], slow_in.shape[4]
    fast_frames, fast_width = fast_in.shape[1], fast_in.shape[4]
    rows = rows_total(mesh.shape["dp"])

    def flat(array):
        return jnp.transpose(array[0], (1, 2, 0, 3)).reshape(-1, array.shape[4])

    def unflat(array, count):
        grid = array.reshape(side, side, count, array.shape[1])
        return jnp.transpose(grid, (2, 0, 1, 3))[None]

    def turn(arrays):
        return arrays[:4] + (jnp.swapaxes(arrays[4], 1, 2),) + arrays[5:]

    turned = turn(weights)
    *kept, grads, norm_grad = block_call(
        mesh,
        frames,
        side,
        rows,
        (
            flat(slow_in),
            flat(fast_in),
            flat(slow_cotangent),
            flat(fast_cotangent),
            clip_start,
            clip_end,
            *turned,
            norms[0],
        ),
    )
    weights_new, moments_new, kept, norms_new = muon(
        grads, norm_grad, norms, turned, turn(moments_old), kept
    )
    slow_out, fast_out, slow_grad, fast_grad = kept
    weights_new, moments_new = turn(tuple(weights_new)), turn(tuple(moments_new))
    params_new, first_new, second_new = norms_new
    return (
        unflat(slow_out, frames),
        unflat(fast_out, fast_frames),
        unflat(slow_grad, frames),
        unflat(fast_grad, fast_frames),
        *weights_new,
        *moments_new,
        first_new,
        second_new,
        params_new,
    )


def solution(mesh):
    sharded = P("group", "dp", None, None, None)
    return jax.shard_map(
        partial(body, mesh),
        mesh=mesh,
        in_specs=(sharded,) * 4 + (P("group", None),) * 2 + (P(),) * 17,
        out_specs=(sharded,) * 4 + (P(),) * 17,
        check_vma=False,
    )
```

```python
from functools import partial
import math

import jax
import jax.numpy as jnp
from jax import lax
from jax.experimental import pallas as pl
from jax.experimental.pallas import tpu as pltpu
from jax.sharding import PartitionSpec as P

NS_STEPS = 5
STEP = 10


EPS = 1e-05
MU = 0.95
LR = 0.3
BETA_ONE = 0.9
BETA_TWO = 0.95
LR_NORM = 0.2
ADAM_EPS = 1e-08
NS_A = 3.4445
NS_B = -4.775
NS_C = 2.0315
F32 = jnp.float32
BF = jnp.bfloat16
MESH = pl.DeviceIdType.MESH
REDUCE_1 = 3328
LATERAL_2 = 4352
TINY = 4736
REDUCE_0 = 4864
LATERAL_0 = 5888
REDUCE_2 = 6144
ROWS = 7168
CUTS = (1024, 3072, 4096, 6144)
LOADS = 53
PARTS = 7
PUMPS = {
    "a": (0,),
    "b": (1, 0),
    "c": (0,),
    "e": (1,),
    "f": (2,),
    "g": (0,),
    "h": (3, 1),
    "i": (4, 2),
    "j": (1,),
    "l": (3, 2, 4),
    "m": (1,),
    "n": (3, 4, 2, 1, 0),
    "z": (3, 4, 1, 2, 0),
}
VMEM_LIMIT = 62 * 2**20
WHOLE = pl.BlockSpec(memory_space=pltpu.VMEM)
ANYWHERE = pl.BlockSpec(memory_space=pl.ANY)
SCALARS = pl.BlockSpec(memory_space=pltpu.SMEM)


def adam_step(params, first, second, grad):
    first_new = BETA_ONE * first + (1.0 - BETA_ONE) * grad
    second_new = BETA_TWO * second + (1.0 - BETA_TWO) * grad * grad
    corrected = first_new / (1.0 - BETA_ONE**STEP)
    params_new = params - LR_NORM * corrected / (
        jnp.sqrt(second_new / (1.0 - BETA_TWO**STEP)) + ADAM_EPS
    )
    return (params_new, first_new, second_new)


def rows_total(n_dp):
    unit = 256 * (n_dp // 2)
    return -(-ROWS // unit) * unit


def pieces_of(n_dp):
    unit = 256 * (n_dp // 2)
    cuts = [0] + [cut // unit * unit for cut in CUTS] + [rows_total(n_dp)]
    cuts = sorted(set(cuts))
    return [(low, high - low) for low, high in zip(cuts[:-1], cuts[1:])]


def orders_of(place):
    return (("x", "y", "z"), ("y", "x", "z"))


def stage_sizes(place, size, depth):
    rows, result = size // 4, []
    for axis in orders_of(place)[0]:
        rows = rows // depth if axis == "z" else rows // 2
        result.append((rows, depth - 1 if axis == "z" else 1))
    return result


def dot(left, right):
    return jnp.dot(left, right, preferred_element_type=F32)


def dot_nt(left, right):
    return lax.dot_general(left, right, (((1,), (1,)), ((), ())), preferred_element_type=F32)


def dot_tn(left, right):
    return lax.dot_general(left, right, (((0,), (0,)), ((), ())), preferred_element_type=F32)


def split(value):
    high = value.astype(BF)
    return high, (value - high.astype(F32)).astype(BF)


def dot_split(left, right):
    return dot(
        jnp.concatenate([left[0], left[0], left[1]], axis=1),
        jnp.concatenate([right[0], right[1], right[0]], axis=0),
    )


def gram_tn(value):
    low = value.astype(BF)
    return dot_tn(low, low)


def gram_nt(value):
    low = value.astype(BF)
    return dot_nt(low, low)


def eye(size, kept=None):
    row = lax.broadcasted_iota(jnp.int32, (size, size), 0)
    col = lax.broadcasted_iota(jnp.int32, (size, size), 1)
    return jnp.where(row == col, 1.0, 0.0).astype(F32)


def square_split(value):
    high, low = value
    cross = dot(high, low)
    return dot(high, high) + cross + cross.T


def newton_poly(a, square):
    return NS_A * eye(a.shape[0]) + NS_B * a + NS_C * square


def newton_first(chains):
    newton_middle(chains, True)


def newton_middle(chains, first=False):
    values = [a_ref[...] for a_ref, _ in chains]
    splits = [split(a) for a in values]
    squares = [square_split(each) for each in splits]
    polys = [newton_poly(a, square) for a, square in zip(values, squares)]
    fine = [a.shape[0] < 256 for a in values]
    polys = [split(poly) if each else poly.astype(BF) for poly, each in zip(polys, fine)]
    if first:
        products = [
            poly[0].astype(F32) + poly[1].astype(F32) if each else poly.astype(F32)
            for poly, each in zip(polys, fine)
        ]
    else:
        products = [
            dot(p_ref[...].astype(BF), poly[0] if each else poly)
            for (_, p_ref), poly, each in zip(chains, polys, fine)
        ]
    once = [
        dot_split(a, poly) if each else dot(a[0], poly) + dot(a[1], poly)
        for a, poly, each in zip(splits, polys, fine)
    ]
    once = [split(each) for each in once]
    twice = [
        dot_split(a, poly) if each else dot(poly, a[0]) + dot(poly, a[1])
        for a, poly, each in zip(once, polys, fine)
    ]
    for (a_ref, p_ref), a, product in zip(chains, twice, products):
        a_ref[...] = a
        p_ref[...] = product


def newton_last(chains):
    values = [a_ref[...] for a_ref, _ in chains]
    lows = [a.astype(BF) for a in values]
    squares = [dot(low, low) for low in lows]
    polys = [
        (NS_A * eye(a.shape[0]) + NS_B * a + NS_C * square).astype(BF)
        for a, square in zip(values, squares)
    ]
    products = [dot(p_ref[...].astype(BF), poly) for (_, p_ref), poly in zip(chains, polys)]
    for (_, p_ref), product in zip(chains, products):
        p_ref[...] = product


def newton_steps():
    return [newton_first] + [newton_middle] * (NS_STEPS - 2) + [newton_last]


def norm_of(gram, size):
    trace = jnp.sum(gram * eye(size))
    return 1.0 / (jnp.sqrt(trace) + 1e-07)


def muon_kernel(*refs):
    grads, norm_grad, norms = refs[0], refs[1], refs[2:5]
    weight_in, moment_in, kept = refs[5:12], refs[12:19], refs[19:23]
    weight_out, moment_out, kept_out = refs[23:30], refs[30:37], refs[37:41]
    norms_out, g_buf = refs[41:44], refs[44]
    weight, moment, keep = refs[45:52], refs[52:59], refs[59:63]
    chain_a, chain_p, small_a, small_p, low_buf = refs[63:68]
    wide_keep = refs[68:70]
    sem, g_sem, tap_sem, out_sem, keep_in, keep_out, norm_sem = refs[70:77]
    norm_grad_in, norms_in, norms_target = norm_grad, norms, norms_out
    norm_grad, norms, norms_out = refs[77], refs[78:81], refs[81:84]
    loads_n = [
        pltpu.make_async_copy(source, target, norm_sem.at[place])
        for place, (source, target) in enumerate(
            zip((norm_grad_in, *norms_in), (norm_grad, *norms))
        )
    ]

    g_cuts = (0, 1024, REDUCE_1, LATERAL_2, TINY, REDUCE_0, LATERAL_0, REDUCE_2, ROWS)
    loads = {}
    for place, (low, high) in enumerate(zip(g_cuts[:-1], g_cuts[1:])):
        span = pl.ds(low, high - low)
        loads[low] = pltpu.make_async_copy(grads.at[span], g_buf.at[span], g_sem.at[place])
    loads_m, loads_w = (
        [None] * 2
        + [pltpu.make_async_copy(source[i], target[i], sem.at[kind, i]) for i in range(2, 7)]
        for kind, (source, target) in enumerate(((moment_in, moment), (weight_in, weight)))
    )
    thirds = [slice(3 * part, 3 * part + 3) for part in range(3)]

    def three_parts(source, target, spans, first):
        return [
            pltpu.make_async_copy(source.at[span], target.at[span], tap_sem.at[first + part])
            for part, span in enumerate(spans)
        ]

    taps_m = three_parts(moment_in[0], moment[0], range(3), 0)
    taps_w = three_parts(weight_in[0], weight[0], range(3), 3)
    parts_m = three_parts(moment_in[1], moment[1], thirds, 6)
    parts_w = three_parts(weight_in[1], weight[1], thirds, 9)
    loads[0].start()
    loads_m[2].start()
    for tap, low in ((1, REDUCE_1), (0, REDUCE_0), (2, REDUCE_2)):
        loads[low].start()
        taps_m[tap].start()
    stores, moving = [], []
    for place, (source, target) in enumerate(zip(kept, keep)):
        rows = source.shape[0] // PARTS
        for part in range(PARTS):
            span = pl.ds(rows * part, rows)
            made = pltpu.make_async_copy(
                source.at[span], target.at[span], keep_in.at[place, part]
            )
            moving.append((place, part, span, made))
    later = [loads[1024], *parts_m, loads_m[3]]
    later += [loads[low] for low in (LATERAL_2, LATERAL_0, TINY)] + loads_m[4:7] + loads_n
    later += [each[3] for each in moving] + [loads_w[2], *taps_w, *parts_w, *loads_w[3:7]]

    def start_next(count):
        for _ in range(min(count, len(later))):
            later.pop(0).start()

    def move(count):
        for _ in range(min(count * PARTS // 2, len(moving))):
            place, part, span, made = moving.pop(0)
            made.wait()
            source = keep[place]
            if source.dtype != kept_out[place].dtype:
                source = wide_keep[place - 2]
                size = keep[place].shape[0] // 14
                each = 14 // PARTS

                def widen(number, carry, place=place, size=size):
                    rows = pl.ds(pl.multiple_of(number * size, 16), size)
                    wide_keep[place - 2][rows, :] = keep[place][rows, :].astype(F32)
                    return carry

                lax.fori_loop(each * part, each * (part + 1), widen, 0)
            stores.append(
                pltpu.make_async_copy(
                    source.at[span], kept_out[place].at[span], keep_out.at[place, part]
                )
            )
            stores[-1].start()

    sent = []

    def send(source, target):
        sent.append(pltpu.make_async_copy(source, target, out_sem.at[len(sent)]))
        sent[-1].start()

    scales = []

    def close(number, gram):
        inverse = norm_of(gram, 256)
        scales.append(inverse)
        chain_a[number] = gram * (inverse * inverse)

    start_next(15)
    loads[0].wait()
    loads_m[2].wait()
    gram = jnp.zeros((256, 256), F32)
    for block in range(4):
        cols, rows = (slice(256 * block, 256 * (block + 1)) for _ in range(2))
        new = MU * moment[2][:, cols] + g_buf[rows, :].astype(F32)
        moment[2][:, cols] = new
        low = new.astype(BF)
        low_buf[rows, :] = low
        gram = gram + dot_nt(low, low)
    send(moment[2], moment_out[2])
    close(0, gram)

    gram = jnp.zeros((256, 256), F32)
    for tap, low_row in ((1, REDUCE_1), (0, REDUCE_0), (2, REDUCE_2)):
        loads[low_row].wait()
        taps_m[tap].wait()
        if tap == 0:
            start_next(4 * PARTS // 2)
        if tap == 2:
            start_next(len(later))
        for part in range(4):
            rows = slice(256 * part, 256 * (part + 1))
            span = slice(low_row + 256 * part, low_row + 256 * (part + 1))
            new = MU * moment[0][tap, rows, :] + g_buf[span, :].T.astype(F32)
            moment[0][tap, rows, :] = new
            low_buf[span, :] = new.astype(BF)
        send(moment[0].at[tap], moment_out[0].at[tap])
        low = low_buf[low_row : low_row + 1024, :]
        gram = gram + dot_tn(low, low)
    close(1, gram)
    move(1)

    loads[1024].wait()
    gram = jnp.zeros((256, 256), F32)
    for part, taps in enumerate(thirds):
        parts_m[part].wait()
        span = slice(1024 + 768 * part, 1792 + 768 * part)
        new = MU * moment[1][taps].reshape(768, 256) + g_buf[span, :].astype(F32)
        moment[1][taps] = new.reshape(3, 256, 256)
        send(moment[1].at[taps], moment_out[1].at[taps])
        low = new.astype(BF)
        low_buf[span, :] = low
        gram = gram + dot_tn(low, low)
    close(2, gram)
    move(1)

    loads_m[3].wait()
    loads[LATERAL_2].wait()
    loads[LATERAL_0].wait()
    first = g_buf[LATERAL_0 : LATERAL_0 + 256, :].T
    second = g_buf[LATERAL_2 : LATERAL_2 + 256, :].T
    third = g_buf[LATERAL_2 + 256 : LATERAL_2 + 384, :]
    third = jnp.concatenate([third[:, :128], third[:, 128:]], axis=0).T
    turned = jnp.concatenate([first, second, third], axis=0).astype(F32)
    new = MU * moment[3][...].reshape(640, 256) + turned
    moment[3][...] = new.reshape(5, 128, 256)
    lateral_low = new.astype(BF)
    send(moment[3], moment_out[3])
    close(3, dot_tn(lateral_low, lateral_low))
    move(1)

    for each in loads_n:
        each.wait()
    for kind in range(2):
        for part in range(7):
            lanes = slice(256 * part, min(256 * (part + 1), norms[0].shape[1]))
            row, width = slice(kind, kind + 1), lanes.stop - lanes.start
            grad = norm_grad[8 * kind + part : 8 * kind + part + 1, :width]
            news = adam_step(*(each[row, lanes] for each in norms), grad)
            for target, new in zip(norms_out, news):
                target[row, lanes] = new
    for place in range(3):
        stores.append(
            pltpu.make_async_copy(norms_out[place], norms_target[place], norm_sem.at[4 + place])
        )
        stores[-1].start()

    loads[TINY].wait()
    for i in (4, 5, 6):
        loads_m[i].wait()
    tiny = g_buf[TINY : TINY + 128, :].astype(F32)
    reduce_new = []
    for tap in range(3):
        rows, cols = 32 * (tap // 2), 128 * (tap % 2)
        new = MU * moment[4][tap] + tiny[rows : rows + 32, cols : cols + 128]
        moment[4][tap] = new
        reduce_new.append(new)
    expand_new = MU * moment[6][...] + tiny[32:64, 128:256]
    moment[6][...] = expand_new
    spatial_new = []
    for tap in range(9):
        block = tiny[64 + 32 * (tap // 8) : 96 + 32 * (tap // 8), 128 * (tap % 8 // 4) :][:, :128]
        if tap % 4:
            block = pltpu.roll(block, 128 - 32 * (tap % 4), 1)
        new = MU * moment[5][tap] + block[:, :32]
        moment[5][tap] = new
        spatial_new.append(new)
    for i in (4, 5, 6):
        send(moment[i], moment_out[i])
    grams = (
        sum(gram_tn(new) for new in spatial_new),
        sum(gram_nt(new) for new in reduce_new),
        gram_nt(expand_new),
    )
    tiny_scales = [norm_of(gram, 32) for gram in grams]
    blocks = []
    for place, (gram, inverse) in enumerate(zip(grams, tiny_scales)):
        wide = jnp.concatenate([gram * (inverse * inverse), jnp.zeros((32, 96), F32)], axis=1)
        blocks.append(pltpu.roll(wide, 32 * place, 1) if place else wide)
    blocks.append(jnp.zeros((32, 128), F32))
    small_a[...] = jnp.concatenate(blocks, axis=0)
    move(1)

    chains = [(chain_a.at[n], chain_p.at[n]) for n in range(4)] + [(small_a, small_p)]
    for step in newton_steps():
        step(chains)
        move(1)

    loads_w[2].wait()
    poly = (chain_p[0] * (2.0 * LR * scales[0])).astype(BF)
    for block in range(4):
        cols, rows = (slice(256 * block, 256 * (block + 1)) for _ in range(2))
        weight[2][:, cols] = weight[2][:, cols] - dot(poly, low_buf[rows, :])
    send(weight[2], weight_out[2])

    poly = (chain_p[1] * (LR * scales[1])).astype(BF)
    for tap, low_row in enumerate((REDUCE_0, REDUCE_1, REDUCE_2)):
        taps_w[tap].wait()
        low = low_buf[low_row : low_row + 1024, :]
        weight[0][tap] = weight[0][tap] - dot(low, poly)
        send(weight[0].at[tap], weight_out[0].at[tap])

    poly = (chain_p[2] * (LR * scales[2])).astype(BF)
    for part, taps in enumerate(thirds):
        parts_w[part].wait()
        change = dot(low_buf[1024 + 768 * part : 1792 + 768 * part, :], poly)
        weight[1][taps] = weight[1][taps] - change.reshape(3, 256, 256)
        send(weight[1].at[taps], weight_out[1].at[taps])

    loads_w[3].wait()
    poly = (chain_p[3] * (LR * scales[3])).astype(BF)
    weight[3][...] = weight[3][...] - dot(lateral_low, poly).reshape(5, 128, 256)
    send(weight[3], weight_out[3])
    for i in (4, 5, 6):
        loads_w[i].wait()
    tiny_p = small_p[...].astype(BF)
    for tap in range(9):
        change = dot(moment[5][tap].astype(BF), tiny_p[:32, :32])
        weight[5][tap] = weight[5][tap] - LR * tiny_scales[0] * change
    none = jnp.zeros((32, 128), BF)
    for tap in range(3):
        stack = jnp.concatenate([none, moment[4][tap].astype(BF), none, none], axis=0)
        weight[4][tap] = weight[4][tap] - LR * tiny_scales[1] * dot(tiny_p[32:64, :], stack)
    stack = jnp.concatenate([none, none, moment[6][...].astype(BF), none], axis=0)
    weight[6][...] = weight[6][...] - LR * 2.0 * tiny_scales[2] * dot(tiny_p[64:96, :], stack)
    for i in (4, 5, 6):
        send(weight[i], weight_out[i])
    move(len(moving))
    for made in stores + sent:
        made.wait()


def muon(grads, norm_grad, norms, weights, moments_old, kept):
    shapes = [jax.ShapeDtypeStruct(each.shape, F32) for each in weights]
    types = (BF, BF, F32, F32)
    same = [jax.ShapeDtypeStruct(each.shape, kind) for each, kind in zip(kept, types)]
    dma = pltpu.SemaphoreType.DMA
    out = pl.pallas_call(
        muon_kernel,
        out_shape=shapes + shapes + same + [jax.ShapeDtypeStruct(norms[0].shape, F32)] * 3,
        in_specs=[ANYWHERE] * 23,
        out_specs=[ANYWHERE] * 21,
        scratch_shapes=[pltpu.VMEM(grads.shape, BF)]
        + [pltpu.VMEM(each.shape, F32) for each in weights] * 2
        + [pltpu.VMEM(each.shape, each.dtype) for each in kept]
        + [
            pltpu.VMEM((4, 256, 256), F32),
            pltpu.VMEM((4, 256, 256), F32),
            pltpu.VMEM((128, 128), F32),
            pltpu.VMEM((128, 128), F32),
            pltpu.VMEM(grads.shape, BF),
            pltpu.VMEM(kept[2].shape, F32),
            pltpu.VMEM(kept[3].shape, F32),
            dma((2, 7)),
            dma((8,)),
            dma((12,)),
            dma((24,)),
            dma((4, PARTS)),
            dma((4, PARTS)),
            dma((7,)),
            pltpu.VMEM(norm_grad.shape, F32),
        ]
        + [pltpu.VMEM(norms[0].shape, F32)] * 6,
        compiler_params=pltpu.CompilerParams(vmem_limit_bytes=VMEM_LIMIT),
        name="muon",
    )(grads, norm_grad, *norms, *weights, *moments_old, *kept)
    return out[:7], out[7:14], out[14:18], out[18:]


def sigmoid(value):
    return 0.5 * jnp.tanh(0.5 * value) + 0.5


def spread(row):
    return jnp.broadcast_to(row, (8, row.shape[1]))


def tiled(value):
    value = value + pltpu.roll(value, 64, 1)
    return value + pltpu.roll(value, 32, 1)


def block_kernel(n_dp, n_group, frames, side, pieces, *refs):
    slow_in, fast_in, slow_cot, fast_cot, starts, ends = refs[:6]
    w_reduce, w_spatial, w_expand, w_lateral = refs[6:10]
    small_in = refs[10:14]
    slow_out, fast_out, slow_grad, fast_grad, g_out, norm_out = refs[14:20]
    (
        xs, cs, xn, cf, fp, zf, df, ds, zc, za, zb, b1, b2, sa, fa, hsb, hfb, zfa, zfb, fx,
        dzf, h_t, wr, ws, we, wl, bt, fs, fst, fe, gbuf, masks, links, fast_mask, xh_in, hs, hr, fhs, fhr, st_a, st_c, st_f,
        load, store, h_send, h_recv, s_send, a_recv, c_recv, f_send, f_recv, summed, norm_loc, n_in, n_send, n_recv,
        g_save, f_reduce, f_spatial, f_expand, params, *sums_refs,
    ) = refs[20:]
    pixels = side * side
    n_rows = pixels * frames
    line = side * frames
    dp, group = lax.axis_index("dp"), lax.axis_index("group")
    after = (lax.rem(dp + 1, n_dp), group)
    before = (lax.rem(dp + n_dp - 1, n_dp), group)
    peers = [(dp, lax.rem(group + step, n_group)) for step in range(1, n_group)]

    dp_peers = [(lax.rem(dp + step, n_dp), group) for step in range(1, n_dp)]
    barrier = pltpu.get_barrier_semaphore()
    for other in peers + dp_peers:
        pl.semaphore_signal(barrier, inc=1, device_id=other, device_id_type=MESH)

    loads = {}

    def fetch(name, source, target):
        loads[name] = pltpu.make_async_copy(source, target, load.at[len(loads) % LOADS])
        loads[name].start()

    def ready(*names):
        for name in names:
            loads[name].wait()

    half = n_rows // 2
    parts_in = side // 2

    def fetch_parts(name, source, target):
        size = target.shape[0] // parts_in
        for part in range(parts_in):
            span = pl.ds(size * part, size)
            fetch((name, part), source.at[span], target.at[span])

    def ready_parts(name):
        ready(*((name, part) for part in range(parts_in)))

    fetch_parts("xn", fast_in, xn)
    for place, target in enumerate((f_reduce, f_spatial, f_expand, params)):
        fetch(("small", place), small_in[place], target)
    for tap in range(5):
        fetch(("wl", tap), w_lateral.at[tap], lateral_stage(zc, tap))
    fetch("wr0", w_reduce.at[0], zc.at[0:1024, 0:256])
    fetch_parts("xs", slow_in, xs)
    fetch("wr2", w_reduce.at[2], zc.at[0:1024, 512:768])
    fetch("wr1", w_reduce.at[1], zc.at[0:1024, 256:512])
    for tap in range(9):
        fetch(("ws", tap), w_spatial.at[tap], spatial_stage(zc, tap))
    for block in range(4):
        fetch(
            ("we", block),
            w_expand.at[:, 256 * block : 256 * (block + 1)],
            zb.at[256 * block : 256 * (block + 1)],
        )
    fetch_parts("cs", slow_cot, cs)
    fetch_parts("cf", fast_cot, cf)

    first = dp * frames
    row_id = lax.broadcasted_iota(jnp.int32, (frames, 128), 0)
    lane = lax.broadcasted_iota(jnp.int32, (8, 128), 1)

    def info(offset, rows):
        frame = first + offset + rows
        inside = jnp.zeros(rows.shape, jnp.int32)
        begun = jnp.zeros(rows.shape, jnp.int32)
        for slot in range(starts.shape[1]):
            open_ = frame >= starts[0, slot]
            begun = begun + jnp.where(open_, 1, 0)
            inside = jnp.where(open_ & (frame < ends[0, slot]), 1, inside)
        return inside, begun

    own, own_segment = info(0, row_id)
    valid = own.astype(F32)
    for offset, place in ((-1, 0), (1, 1)):
        near, near_segment = info(offset, row_id)
        both = jnp.where((own * near == 1) & (own_segment == near_segment), 1.0, 0.0)
        links[8 * place : 8 * place + 8, 0:128] = both.astype(F32)
        links[8 * place : 8 * place + 8, 128:256] = both.astype(F32)
        inner = jnp.where(row_id == (0, frames - 1)[place], 0.0, both).astype(F32)
        links[16 + 8 * place : 24 + 8 * place, 0:128] = inner
        links[16 + 8 * place : 24 + 8 * place, 128:256] = inner
    for block in range(8):
        masks[0:8, 128 * block : 128 * (block + 1)] = valid
    fast_id = lax.broadcasted_iota(jnp.int32, (4 * frames, 128), 0)
    fast_valid = info(0, fast_id >> 2)[0].astype(F32)
    fast_mask[...] = fast_valid
    count_local = jnp.sum(valid, axis=0, keepdims=True) * float(pixels)
    count_block = spread(count_local)

    def chunk(number, size):
        return pl.ds(pl.multiple_of(number * size, 16), size)

    def three(value):
        return value.reshape(-1, 8, value.shape[-1])

    def fold(value):
        return jnp.sum(three(value), axis=0)

    def pair(ref, rows):
        return jnp.concatenate([ref[0, rows, :], ref[1, rows, :]], axis=1)

    def set_pair(ref, rows, value):
        ref[0, rows, :] = value[:, :128]
        ref[1, rows, :] = value[:, 128:]

    def loop(count, body, carry=0):
        return lax.fori_loop(0, count, body, carry)

    def zeros(*shape):
        return jnp.zeros(shape, F32)

    depth = n_dp // 2
    core, side_y = lax.rem(group, 2), group // 2
    side_x, side_z = lax.rem(dp, 2), dp // 2
    pair_core = (dp, group + 1 - 2 * core)
    sides = {"x": side_x, "y": side_y}
    over = {"x": (dp + 1 - 2 * side_x, group), "y": (dp, group + 2 - 4 * side_y)}
    live = {}

    def at(ref, start, size):
        return ref.at[pl.ds(pl.multiple_of(start, 16), size)]

    def regions(place):
        start, size = pieces[place]
        base = start + core * (size // 2)
        sizes = stage_sizes(place, size, depth)
        result = []
        for way, axes in enumerate(orders_of(place)):
            offset = base + way * (size // 4)
            offsets = [offset]
            for axis, (rows, _) in zip(axes, sizes):
                offset = offset + (side_z if axis == "z" else sides[axis]) * rows
                offsets.append(offset)
            result.append(offsets)
        return base, sizes, result

    def begin(place):
        number = live[place][0]
        start, size = pieces[place]
        send, recv = sums_refs[5 * place + 3 : 5 * place + 5]
        base, sizes, offsets = regions(place)
        made = []

        def add_copy(source, target, device):
            made.append(
                pltpu.make_async_remote_copy(
                    src_ref=source,
                    dst_ref=target,
                    send_sem=send.at[0],
                    recv_sem=recv.at[number],
                    device_id=device,
                    device_id_type=MESH,
                )
            )

        if number == 0:
            other = start + (1 - core) * (size // 2)
            add_copy(at(gbuf, other, size // 2), at(summed, other, size // 2), pair_core)
        elif number == 7:
            add_copy(at(summed, base, size // 2), at(summed, base, size // 2), pair_core)
        else:
            stage = number - 1 if number < 4 else 6 - number
            rows, _ = sizes[stage]
            into = sums_refs[5 * place + stage]
            for way, axes in enumerate(orders_of(place)):
                axis, before_ = axes[stage], offsets[way][stage]
                mine = at(summed, offsets[way][stage + 1], rows)
                if axis == "z":
                    for step in range(1, depth):
                        other = lax.rem(side_z + step, depth)
                        device = (other * 2 + side_x, group)
                        if number < 4:
                            source = at(gbuf, before_ + other * rows, rows)
                            add_copy(source, into.at[way, step - 1], device)
                        else:
                            add_copy(mine, mine, device)
                elif number < 4:
                    source = at(gbuf, before_ + (1 - sides[axis]) * rows, rows)
                    add_copy(source, into.at[way, 0], over[axis])
                else:
                    add_copy(mine, mine, over[axis])
        for each in made:
            each.start()
        if 0 < number < 7:
            made = []
            add_copy(into, into, pair_core)
        live[place] = (number, made[0])

    def add_rows(start, size, target, sources):
        step_rows = math.gcd(size, 64)

        def step(number, carry):
            row = pl.multiple_of(number * step_rows, 16)
            rows = pl.ds(pl.multiple_of(start + row, 16), step_rows)
            total = gbuf[rows, :].astype(F32)
            for source in sources(row, step_rows, rows):
                total = total + source.astype(F32)
            target[rows, :] = total.astype(BF)
            return carry

        lax.fori_loop(0, size // step_rows, step, 0)

    def finish(place):
        number, made = live[place]
        start, size = pieces[place]
        base, sizes, offsets = regions(place)
        made.wait()
        if number == 0:
            add_rows(base, size // 2, gbuf, lambda row, count, rows: [summed[rows, :]])
        elif number < 4:
            rows_, messages = sizes[number - 1]
            into = sums_refs[5 * place + number - 1]
            for way in range(2):
                add_rows(
                    offsets[way][number],
                    rows_,
                    summed if number == 3 else gbuf,
                    lambda row, count, rows, way=way: [
                        into[way, message, pl.ds(row, count), :] for message in range(messages)
                    ],
                )
        elif number == 7:
            save = pltpu.make_async_copy(
                summed.at[start : start + size], g_out.at[start : start + size], g_save.at[place]
            )
            save.start()
            saves.append(save)
        live[place] = (number + 1, None) if number < 7 else None

    saves, norm_made = [], []

    def share_norms():
        n_in[dp] = norm_loc[...]
        for peer in dp_peers:
            norm_made.append(
                pltpu.make_async_remote_copy(
                    src_ref=n_in.at[dp],
                    dst_ref=n_in.at[dp],
                    send_sem=n_send.at[0],
                    recv_sem=n_recv.at[0],
                    device_id=peer,
                    device_id_type=MESH,
                )
            )
            norm_made[-1].start()

    def launch(ready_rows):
        for place, (start, size) in enumerate(pieces):
            if place not in live and start + size <= ready_rows:
                live[place] = (0, None)
                begin(place)

    def point(name):
        pump(*PUMPS.get(name, ()))

    def pump(*places):
        for place in places:
            if live.get(place):
                finish(place)
                if live[place]:
                    begin(place)


    row8 = lax.broadcasted_iota(jnp.int32, (8, 1), 0)

    def share(store_ref, sends, recvs, place, sums, squares, extra=None):
        top = jnp.sum(sums, axis=0, keepdims=True)
        second = jnp.sum(squares, axis=0, keepdims=True)
        block = jnp.where(row8 == 0, top, jnp.where(row8 == 1, second, 0.0))
        if extra is not None:
            block = jnp.where(row8 == 2, extra, block)
        store_ref[place, group] = block
        made = []
        for peer in peers:
            made.append(
                pltpu.make_async_remote_copy(
                    src_ref=store_ref.at[place, group],
                    dst_ref=store_ref.at[place, group],
                    send_sem=sends.at[0],
                    recv_sem=recvs.at[place],
                    device_id=peer,
                    device_id_type=MESH,
                )
            )
            made[-1].start()

        part = store_ref.at[place, 0 : n_group - 1]
        arrived = pltpu.make_async_remote_copy(
            src_ref=part,
            dst_ref=part,
            send_sem=sends.at[0],
            recv_sem=recvs.at[place],
            device_id=peers[0],
            device_id_type=MESH,
        )

        def receive():
            arrived.wait()
            total = store_ref[place, 0]
            for slot in range(1, n_group):
                total = total + store_ref[place, slot]
            return [spread(total[i : i + 1, :]) for i in range(3)]

        return receive

    def share_a(place, sums, squares):
        return share(st_a, s_send, a_recv, place, sums, squares)

    def share_c(place, sums, squares):
        return share(st_c, s_send, c_recv, place, sums, squares)

    def share_f(place, sums, squares, extra=None):
        return share(st_f, f_send, f_recv, place, sums, squares, extra)

    def coefs(total, squares, count, gain, bias):
        mean = total / count
        inverse = lax.rsqrt(squares / count - mean * mean + EPS)
        slope_a = gain * inverse
        return mean, inverse, slope_a, bias - mean * slope_a

    def back_coefs(total, cross, count, mean, inverse, slope_a):
        c3 = slope_a * inverse * cross / count
        return slope_a * total / count - mean * c3, c3

    def param(kind, place):
        row = slice(kind, kind + 1)
        if place < 2:
            return spread(params[row, 256 * place : 256 * place + 256])
        if place == 2:
            return spread(params[row, 512:1536])
        low = spread(params[row, 1536:1664])
        rest = params[row, 1664:]
        none = zeros(1, 128 - rest.shape[1])
        high = spread(jnp.concatenate([rest, none], axis=1))
        if place == 3:
            return tiled(jnp.where(lane < 32, low, 0.0))
        if place == 4:
            return tiled(jnp.where((lane >= 32) & (lane < 64), low, 0.0))
        return jnp.where(lane < 64, pltpu.roll(low, 64, 1), pltpu.roll(high, 64, 1))

    if gbuf.shape[0] > ROWS:
        gbuf[ROWS:, :] = jnp.zeros((gbuf.shape[0] - ROWS, 256), BF)


    def widen(number, carry):
        rows = chunk(number, 4 * 2 * line)
        zf[rows, :] = xn[rows, :].astype(F32)
        return carry

    for part in range(parts_in):
        ready(("xn", part))
        widen(part, 0)

    def pack(source, target):
        def step(number, carry):
            size = 2 * line
            start = pl.multiple_of(number * 4 * size, 16)
            for q in range(4):
                target[chunk(number, size), 128 * q : 128 * q + 128] = source[
                    pl.ds(start + q, size, stride=4), :
                ].astype(BF)
            return carry

        loop(side // 2, step)

    pack(zf, fp)

    for place in range(4):
        ready(("small", place))
    bt[...] = jnp.zeros(bt.shape, BF)
    for tap in range(3):
        low = f_reduce[tap].astype(BF)
        for q in range(4):
            other = q + tap - 1
            if 0 <= other < 4:
                bt[32 * q : 32 * q + 32, 128 * other : 128 * other + 128] = low
    bt[128:160, 384:512] = f_reduce[0].astype(BF)
    bt[224:256, 0:128] = f_reduce[2].astype(BF)
    fe[...] = jnp.zeros(fe.shape, BF)
    for q in range(4):
        fe[32 * q : 32 * q + 32, 128 * q : 128 * q + 128] = f_expand[...].astype(BF)
    for tap in range(9):
        wide = jnp.concatenate([f_spatial[tap], zeros(32, 96)], axis=1)
        for q in range(4):
            fs[tap, 32 * q : 32 * q + 32, :] = (
                pltpu.roll(wide, 32 * q, 1) if q else wide
            ).astype(BF)
        side_b = 128 * (tap % 3)
        fst[tap // 3, side_b : side_b + 128, :] = fs[tap].T

    for tap in range(5):
        ready(("wl", tap))
        wl[128 * tap : 128 * tap + 128, :] = lateral_stage(zc, tap)[...].astype(BF)

    def lower_reduce(tap):
        ready("wr%d" % tap)

        def step(number, carry):
            rows = chunk(number, 128)
            wr[tap, rows, :] = zc[rows, 256 * tap : 256 * tap + 256].astype(BF)
            return carry

        loop(8, step)

    def edges(number, carry):
        rows = chunk(number, half)
        set_pair(b1, rows, dot(xs[rows, :], wr[0]) + dot(fp[rows, 256:512], wl[0:256, :]))
        set_pair(b2, rows, dot(xs[rows, :], wr[2]))
        return carry

    def fast_first(number, carry):
        rows = chunk(number, half)
        both = dot_nt(fp[rows, :], bt[...])
        zfa[rows, :] = (three(both[:, :128]) * masks[0:8, 0:128]).reshape(half, 128)
        fx[rows, :] = both[:, 128:]
        return carry

    ends_ = pl.ds(frames - 1, pixels, stride=frames)
    heads = pl.ds(0, pixels, stride=frames)

    def halo_copy(ref, place, way, sems):
        made = pltpu.make_async_remote_copy(
            src_ref=ref[0].at[place + way],
            dst_ref=ref[1].at[place + way],
            send_sem=h_send.at[sems, place + way],
            recv_sem=h_recv.at[sems, place + way],
            device_id=(after, before)[way],
            device_id_type=MESH,
        )
        pl.when((dp < n_dp - 1, dp > 0)[way])(made.start)
        return made

    def halo_wait(made):
        @pl.when(dp < n_dp - 1)
        def _():
            made[0].wait_send()
            made[1].wait_recv()

        @pl.when(dp > 0)
        def _():
            made[1].wait_send()
            made[0].wait_recv()

    for way, edge in enumerate((0, n_dp - 1)):

        @pl.when(dp == edge)
        def _(way=way):
            xh_in[way] = jnp.zeros(xh_in.shape[1:], BF)
            for place in (way, 2 + way):
                hr[place] = jnp.zeros(hr.shape[1:], BF)
                fhr[place] = jnp.zeros(fhr.shape[1:], BF)

    def send_halo(place, last, zero):
        for part in range(2):
            hs[place, part, 0:pixels, :] = last[part, ends_, :].astype(BF)
            hs[place + 1, part, 0:pixels, :] = zero[part, heads, :].astype(BF)
        return [halo_copy((hs, hr), place, way, 0) for way in range(2)]

    def take_halo(made, place, last, zero):
        halo_wait(made)
        for part in range(2):
            last[part, ends_, :] = hr[place, part, 0:pixels, :].astype(F32)
            zero[part, heads, :] = hr[place + 1, part, 0:pixels, :].astype(F32)

    block_rows = -(-pixels // 64) * 16
    lanes_ = lax.broadcasted_iota(jnp.int32, (block_rows, 128), 1)
    fill = zeros(4 * block_rows - pixels, 128)

    def send_fast_halo(place, ref, first_lanes):
        for way, (rows, first_lane) in enumerate(zip((ends_, heads), first_lanes)):
            value = jnp.concatenate([ref[rows, :], fill], axis=0)
            total = zeros(block_rows, 128)
            for q in range(4):
                piece = value[block_rows * q : block_rows * (q + 1)]
                turn = (32 * q - first_lane) % 128
                piece = pltpu.roll(piece, turn, 1) if turn else piece
                total = jnp.where((lanes_ >= 32 * q) & (lanes_ < 32 * q + 32), piece, total)
            fhs[place + way] = total.astype(BF)
        return [halo_copy((fhs, fhr), place, way, 1) for way in range(2)]

    def take_fast_halo(made, place, first_lanes):
        halo_wait(made)
        result = []
        for way, first_lane in enumerate(first_lanes):
            value = fhr[place + way].astype(F32)
            pieces_ = []
            for q in range(4):
                turn = (first_lane - 32 * q) % 128
                piece = pltpu.roll(value, turn, 1) if turn else value
                keep = (lanes_ >= first_lane) & (lanes_ < first_lane + 32)
                pieces_.append(jnp.where(keep, piece, 0.0))
            result.append(jnp.concatenate(pieces_, axis=0)[:pixels])
        return result

    low = lax.broadcasted_iota(jnp.int32, (pixels, 128), 1) < 64

    def silu_of(value, slope_a, shift):
        norm = value * slope_a + shift
        return norm * sigmoid(norm)

    def slope_of(norm):
        gate = sigmoid(norm)
        return gate + norm * gate * (1.0 - gate)

    def shifted(ref, y, value, flip):
        width = value.shape[1]
        edge = zeros(frames, width)
        back = jnp.concatenate([edge, value[: line - frames]], axis=0).astype(BF)
        ahead = jnp.concatenate([value[frames:], edge], axis=0).astype(BF)
        ref[y + 1, :, 0:width] = ahead if flip else back
        ref[y + 1, :, width : 2 * width] = value.astype(BF)
        ref[y + 1, :, 2 * width : 3 * width] = back if flip else ahead

    def spatial(z_ref, pad_ref, weight, width, slope_a, shift, out_ref):
        def hide(y, carry):
            value = silu_of(three(z_ref[chunk(y, line), :]), slope_a, shift)
            value = value * masks[0:8, 0:width]
            shifted(pad_ref, y, value.reshape(line, width), False)
            return carry

        loop(side, hide)
        tall = side // 2

        def step(number, carry):
            total = zeros(half, width)
            for a in range(3):
                patch = pad_ref[pl.ds(number * tall + a, tall)].reshape(half, 3 * width)
                total = total + dot(patch, weight(a))
            out_ref[chunk(number, half), :] = total
            return carry[0] + fold(total), carry[1] + fold(total * total)

        return loop(2, step, (zeros(8, width), zeros(8, width)))

    def hide_to(z_ref, target, width, slope_a, shift):
        def hide(y, carry):
            rows = chunk(y, line)
            value = silu_of(three(z_ref[rows, :]), slope_a, shift) * masks[0:8, 0:width]
            target[rows, :] = value.reshape(line, width).astype(BF)
            return carry

        loop(side, hide)

    def unpacked(ref, number, size, value, add):
        start = pl.multiple_of(number * 4 * size, 16)
        for q in range(4):
            place = pl.ds(start + q, size, stride=4)
            piece = value[:, 128 * q : 128 * q + 128]
            ref[place, :] = ref[place, :] + piece if add else piece

    def four(value):
        return value[:, 0:128] + value[:, 128:256] + value[:, 256:384] + value[:, 384:512]

    fast_line = 4 * line

    def quad(value):
        return value.reshape(-1, 4, 8, 128)

    def fold_quad(value):
        return jnp.sum(value.reshape(-1, 8, 128), axis=0)

    def through(z_ref, rows, back, slope_a, shift):
        z = three(z_ref[rows, :])
        grad = three(back) * slope_of(z * slope_a + shift)
        return grad, jnp.sum(grad, axis=0), jnp.sum(grad * z, axis=0)

    def scaled_sums(sums, mean, inverse):
        return sums[0], inverse * (sums[1] - mean * sums[0])

    def back_spatial(dy, z_ref, pad_ref, width, slope_a, c2, c3):
        def step(y, carry):
            rows = chunk(y, line)
            grad = slope_a * three(dy(rows)) - masks[0:8, 0:width] * (c2 + c3 * three(z_ref[rows, :]))
            shifted(pad_ref, y, grad.reshape(line, width), True)
            return carry

        loop(side, step)

    loop(2, fast_first)
    hs[...] = jnp.zeros(hs.shape, BF)
    pl.semaphore_wait(barrier, n_group + n_dp - 2)
    fast_halo = send_fast_halo(0, fx, (0, 96))

    lower_reduce(0)
    lower_reduce(2)
    ready_parts("xs")
    loop(2, edges)
    halo = send_halo(0, b1, b2)

    def middle(number, carry):
        rows = chunk(number, half)
        total = dot(xs[rows, :], wr[1]) + dot(fp[rows, 0:384], wl[256:640, :])
        za[rows, :] = (three(total) * masks[0:8, 0:256]).reshape(half, 256)
        return carry

    middle_parts = 2
    from_before, from_after = take_fast_halo(fast_halo, 0, (0, 96))
    fx[ends_, :] = jnp.where(low, from_before, fx[ends_, :])
    fx[heads, :] = jnp.where(low, fx[heads, :], from_after)

    def join_fast(number, carry):
        rows = chunk(number, line)
        cross = three(fx[rows, :])
        moved = jnp.where(
            lane < 64,
            links[0:8, 0:128] * pltpu.roll(cross, 1, 1),
            links[8:16, 0:128] * pltpu.roll(cross, frames - 1, 1),
        )
        total = three(zfa[rows, :]) + moved
        zfa[rows, :] = total.reshape(line, 128)
        return carry[0] + jnp.sum(total, axis=0), carry[1] + jnp.sum(total * total, axis=0)

    sums = loop(side, join_fast, (zeros(8, 128), zeros(8, 128)))
    got_fa = share_f(0, *sums, extra=count_block)
    lower_reduce(1)
    lax.fori_loop(0, middle_parts // 2, middle, 0)

    padded = xh_in.shape[1] // 5
    staged = gbuf.shape[0] - 10 * padded
    for way, rows in enumerate((ends_, heads)):
        for block in range(5):
            top = staged + (5 * way + block) * padded + pixels
            gbuf[top : top + padded - pixels, :] = jnp.zeros((padded - pixels, 256), BF)

    def stage(way, block, value):
        top, left = staged + (5 * way + block // 2) * padded, 128 * (block % 2)
        gbuf[top : top + pixels, left : left + 128] = value.astype(BF)

    for block in range(8):
        zfb[...] = xs[:, 128 * block : 128 * (block + 1)].astype(F32)
        stage(0, block, zfb[ends_, :])
        stage(1, block, zfb[heads, :])
    for q, way, block in ((2, 0, 8), (3, 0, 9), (0, 1, 8)):
        zfb[...] = fp[:, 128 * q : 128 * q + 128].astype(F32)
        stage(way, block, zfb[(ends_, heads)[way], :])
    stage(1, 9, zeros(pixels, 128))
    for tap in range(9):
        ready(("ws", tap))
        ws[256 * tap : 256 * tap + 256, :] = spatial_stage(zc, tap)[...].astype(BF)
    for block in range(4):
        ready(("we", block))
        we[:, 256 * block : 256 * block + 256] = zb[256 * block : 256 * block + 256, :].astype(BF)
    sa[0] = jnp.zeros((line, 768), BF)
    sa[side + 1] = jnp.zeros((line, 768), BF)
    fa[0] = jnp.zeros((line, 384), BF)
    fa[side + 1] = jnp.zeros((line, 384), BF)

    sums, squares, count = got_fa()
    fast_count = 4.0 * count
    counts = jnp.concatenate([count] * 8, axis=1)
    mean_fa, inv_fa, m_fa, s_fa = coefs(
        tiled(sums), tiled(squares), fast_count, param(0, 3), param(1, 3)
    )
    sums = spatial(
        zfa, fa, lambda a: fs[3 * a : 3 * a + 3].reshape(384, 128), 128, m_fa, s_fa, zfb
    )
    got_fb = share_f(1, *sums)

    lax.fori_loop(middle_parts // 2, middle_parts, middle, 0)
    take_halo(halo, 0, b1, b2)
    x_halo = []
    for way in range(2):
        made = pltpu.make_async_remote_copy(
            src_ref=gbuf.at[staged + 5 * padded * way : staged + 5 * padded * (way + 1)],
            dst_ref=xh_in.at[way],
            send_sem=h_send.at[2, way],
            recv_sem=h_recv.at[2, way],
            device_id=(after, before)[way],
            device_id_type=MESH,
        )
        pl.when((dp < n_dp - 1, dp > 0)[way])(made.start)
        x_halo.append(made)

    def join(number, carry):
        rows = chunk(number, line)
        total = three(za[rows, :])
        total = total + links[0:8, 0:256] * pltpu.roll(three(pair(b1, rows)), 1, 1)
        total = total + links[8:16, 0:256] * pltpu.roll(three(pair(b2, rows)), frames - 1, 1)
        za[rows, :] = total.reshape(line, 256)
        return carry[0] + jnp.sum(total, axis=0), carry[1] + jnp.sum(total * total, axis=0)

    sums = loop(side, join, (zeros(8, 256), zeros(8, 256)))
    got_sa = share_a(0, *sums)

    sums, squares, _ = got_fb()
    mean_fb, inv_fb, m_fb, s_fb = coefs(
        tiled(sums), tiled(squares), fast_count, param(0, 4), param(1, 4)
    )
    hide_to(zfb, hfb, 128, m_fb, s_fb)

    def expand_fast(number, carry):
        size = 2 * line
        total = dot(hfb[chunk(number, size), :], fe[...])
        unpacked(zf, number, size, total, False)
        return carry[0] + four(fold(total)), carry[1] + four(fold(total * total))

    sums = loop(side // 2, expand_fast, (zeros(8, 128), zeros(8, 128)))
    got_fc = share_f(2, *sums)

    sums, squares, _ = got_sa()
    mean_sa, inv_sa, m_sa, s_sa = coefs(sums, squares, counts[:, :256], param(0, 0), param(1, 0))
    sums = spatial(za, sa, lambda a: ws[768 * a : 768 * a + 768, :], 256, m_sa, s_sa, zb)
    got_sb = share_a(1, *sums)

    sums, squares, _ = got_fc()
    mean_fc, inv_fc, m_fc, s_fc = coefs(sums, squares, fast_count, param(0, 5), param(1, 5))
    ready_parts("cf")

    def finish_fast(y, carry):
        rows = chunk(y, fast_line)
        z = quad(zf[rows, :])
        norm = z * m_fc + s_fc + quad(xn[rows, :].astype(F32))
        gate = sigmoid(norm)
        kept = gate * fast_mask[...].reshape(4, 8, 128)
        act = norm * kept
        grad = quad(cf[rows, :].astype(F32)) * (kept + act * (1.0 - gate))
        cf[rows, :] = act.reshape(fast_line, 128).astype(BF)
        df[rows, :] = grad.reshape(fast_line, 128)
        return carry[0] + fold_quad(grad), carry[1] + fold_quad(grad * z)

    sums = loop(side, finish_fast, (zeros(8, 128), zeros(8, 128)))
    back_fc = share_f(3, *scaled_sums(sums, mean_fc, inv_fc))
    save_fast = pltpu.make_async_copy(cf, fast_out, store.at[1])
    save_fast.start()

    sums, squares, _ = got_sb()
    mean_sb, inv_sb, m_sb, s_sb = coefs(sums, squares, counts[:, :256], param(0, 1), param(1, 1))
    def hide_part(part):
        rows = slice(2 * line * part, 2 * line * (part + 1))
        value = silu_of(three(zb[rows, :]), m_sb, s_sb) * masks[0:8, 0:256]
        hsb[rows, :] = value.reshape(2 * line, 256).astype(BF)

    hide_part(0)
    sums = (zeros(8, 1024), zeros(8, 1024))
    for part in range(side // 2):
        rows = slice(2 * line * part, 2 * line * (part + 1))
        total = dot(hsb[rows, :], we[...])
        if part + 1 < side // 2:
            hide_part(part + 1)
        zc[rows, :] = total
        sums = sums[0] + fold(total), sums[1] + fold(total * total)
    got_sc = share_c(0, *sums)

    norm_loc[...] = zeros(16, 256)
    total_fc, cross_fc, _ = back_fc()
    c2, c3 = back_coefs(total_fc, cross_fc, fast_count, mean_fc, inv_fc, m_fc)

    def back_fast(y, carry, c2=c2, c3=c3):
        rows = chunk(y, fast_line)
        mask = fast_mask[...].reshape(4, 8, 128)
        grad = m_fc * quad(df[rows, :]) - mask * (c2 + c3 * quad(zf[rows, :]))
        zf[rows, :] = grad.reshape(fast_line, 128)
        return carry

    loop(side, back_fast)
    pack(zf, dzf)

    def back_hidden_fast(number, carry):
        rows = chunk(number, half)
        back = dot_nt(dzf[rows, :], fe[...])
        grad, one, two = through(zfb, rows, back, m_fb, s_fb)
        fx[rows, :] = grad.reshape(half, 128)
        return carry[0] + one, carry[1] + two

    sums = loop(2, back_hidden_fast, (zeros(8, 128), zeros(8, 128)))
    back_fb = share_f(4, *scaled_sums(sums, mean_fb, inv_fb))
    wide = dot_tn(hfb[...], dzf[...])
    grad_fc = sum(wide[32 * q : 32 * q + 32, 128 * q : 128 * q + 128] for q in range(4))
    gbuf[TINY + 32 : TINY + 64, 128:256] = grad_fc.astype(BF)

    sums, squares, _ = got_sc()
    mean_sc, inv_sc, m_sc, s_sc = coefs(sums, squares, counts, param(0, 2), param(1, 2))
    ready_parts("cs")

    def finish_slow(y, carry):
        rows = chunk(y, line)
        z = three(zc[rows, :])
        norm = z * m_sc + s_sc + three(xs[rows, :].astype(F32))
        gate = sigmoid(norm)
        kept = gate * masks[0:8, :]
        act = norm * kept
        grad = three(cs[rows, :].astype(F32)) * (kept + act * (1.0 - gate))
        cs[rows, :] = act.reshape(line, 1024).astype(BF)
        ds[rows, :] = grad.reshape(line, 1024).astype(BF)
        return carry[0] + jnp.sum(grad, axis=0), carry[1] + jnp.sum(grad * z, axis=0)

    sums = loop(side, finish_slow, (zeros(8, 1024), zeros(8, 1024)))
    back_sc = share_c(1, *scaled_sums(sums, mean_sc, inv_sc))
    save_slow = pltpu.make_async_copy(cs, slow_out, store.at[0])
    save_slow.start()

    total_fb, cross_fb, _ = back_fb()
    total_fb, cross_fb = tiled(total_fb), tiled(cross_fb)
    c2, c3 = back_coefs(total_fb, cross_fb, fast_count, mean_fb, inv_fb, m_fb)
    hfb[...] = fa[1 : side + 1, :, 128:256].reshape(n_rows, 128)
    back_spatial(lambda rows: fx[rows, :], zfb, fa, 128, m_fb, c2, c3)

    def back_first_fast(number, carry):
        rows = chunk(number, half)
        tall = side // 2
        back = zeros(half, 128)
        for a in range(3):
            patch = fa[pl.ds(number * tall + 2 - a, tall)].reshape(half, 384)
            back = back + dot(patch, fst[a])
        grad, one, two = through(zfa, rows, back, m_fa, s_fa)
        fx[rows, :] = grad.reshape(half, 128)
        return carry[0] + one, carry[1] + two

    sums = loop(2, back_first_fast, (zeros(8, 128), zeros(8, 128)))
    back_fa = share_f(5, *scaled_sums(sums, mean_fa, inv_fa))

    total, cross, _ = back_sc()
    for block in range(4):
        cols = slice(256 * block, 256 * (block + 1))
        norm_loc[2 + block : 3 + block, :] = cross[0:1, cols]
        norm_loc[10 + block : 11 + block, :] = total[0:1, cols]
    c2, c3 = back_coefs(total, cross, counts, mean_sc, inv_sc, m_sc)
    save_slow.wait()

    def back_part(part, c2=c2, c3=c3):
        for half_part in range(2):
            rows = slice(line * (2 * part + half_part), line * (2 * part + half_part + 1))
            grad = m_sc * three(ds[rows, :].astype(F32))
            grad = grad - masks[0:8, :] * (c2 + c3 * three(zc[rows, :]))
            cs[rows, :] = grad.reshape(line, 1024).astype(BF)

    back_part(0)
    sums = (zeros(8, 256), zeros(8, 256))
    for part in range(side // 2):
        rows = slice(2 * line * part, 2 * line * (part + 1))
        back = dot_nt(cs[rows, :], we[...])
        if part + 1 < side // 2:
            back_part(part + 1)
        grad, one, two = through(zb, rows, back, m_sb, s_sb)
        set_pair(b1, rows, grad.reshape(2 * line, 256))
        sums = sums[0] + one, sums[1] + two
    back_sb = share_a(2, *scaled_sums(sums, mean_sb, inv_sb))
    h_t[...] = hsb[...].T
    for block in range(4):
        cols = slice(256 * block, 256 * (block + 1))
        gbuf[cols, :] = dot(h_t[...], cs[:, cols]).astype(BF)
    launch(1024)

    total_fa, cross_fa, _ = back_fa()
    total_fa, cross_fa = tiled(total_fa), tiled(cross_fa)
    c2, c3 = back_coefs(total_fa, cross_fa, fast_count, mean_fa, inv_fa, m_fa)

    def back_one_fast(y, carry, c2=c2, c3=c3):
        rows = chunk(y, line)
        grad = m_fa * three(fx[rows, :]) - masks[0:8, 0:128] * (c2 + c3 * three(zfa[rows, :]))
        grad = grad.reshape(line, 128)
        zfb[rows, :] = grad
        dzf[rows, 0:128] = grad.astype(BF)
        return carry

    loop(side, back_one_fast)
    fast_halo = send_fast_halo(2, zfb, (96, 0))
    pump(0)

    total, cross, _ = back_sb()
    norm_loc[1:2, :] = cross[0:1, :]
    norm_loc[9:10, :] = total[0:1, :]
    c2, c3 = back_coefs(total, cross, counts[:, :256], mean_sb, inv_sb, m_sb)
    h_t[...] = sa[1 : side + 1, :, 256:512].reshape(n_rows, 256).T
    back_spatial(lambda rows: pair(b1, rows), zb, sa, 256, m_sb, c2, c3)

    def spatial_grad(tap, carry):
        for b in range(3):
            patch = sa[pl.ds(2 - tap, side), :, 256 * b : 256 * (b + 1)].reshape(n_rows, 256)
            place = pl.multiple_of(1024 + 768 * tap + 256 * b, 16)
            gbuf[pl.ds(place, 256), :] = dot(h_t[...], patch).astype(BF)
        return carry

    loop(3, spatial_grad)
    launch(REDUCE_1)
    point("a")

    def back_first(number, carry):
        rows = chunk(number, half)
        tall = side // 2
        back = zeros(half, 256)
        for a in range(3):
            for b in range(3):
                tap = 3 * a + b
                patch = sa[pl.ds(number * tall + 2 - a, tall), :, 256 * b : 256 * (b + 1)]
                back = back + dot_nt(patch.reshape(half, 256), ws[256 * tap : 256 * tap + 256, :])
        grad, one, two = through(za, rows, back, m_sa, s_sa)
        set_pair(b1, rows, grad.reshape(half, 256))
        return carry[0] + one, carry[1] + two

    sums = back_first(0, (zeros(8, 256), zeros(8, 256)))
    point("a2")
    sums = back_first(1, sums)
    back_sa = share_a(3, *scaled_sums(sums, mean_sa, inv_sa))
    point("b")

    lanes = lax.broadcasted_iota(jnp.int32, (32, 128), 1)
    tiles = [zeros(32, 128) for _ in range(3)]
    for a in range(3):
        patch = fa[2 - a : 2 - a + side].reshape(n_rows, 384)
        wide = dot_tn(hfb[...], patch)
        for b in range(3):
            tap = 3 * a + b
            for q in range(4):
                piece = wide[32 * q : 32 * q + 32, 128 * b : 128 * b + 128]
                turn = (32 * (tap % 4) - 32 * q) % 128
                piece = pltpu.roll(piece, turn, 1) if turn else piece
                inside = (lanes >= 32 * (tap % 4)) & (lanes < 32 * (tap % 4) + 32)
                tiles[tap // 4] = tiles[tap // 4] + jnp.where(inside, piece, 0.0)
    gbuf[TINY + 64 : TINY + 96, 0:128] = tiles[0].astype(BF)
    gbuf[TINY + 64 : TINY + 96, 128:256] = tiles[1].astype(BF)
    gbuf[TINY + 96 : TINY + 128, 0:128] = tiles[2].astype(BF)
    gbuf[TINY + 96 : TINY + 128, 128:256] = jnp.zeros((32, 128), BF)


    total, cross, _ = back_sa()
    norm_loc[0:1, :] = cross[0:1, :]
    norm_loc[8:9, :] = total[0:1, :]
    c2, c3 = back_coefs(total, cross, counts[:, :256], mean_sa, inv_sa, m_sa)

    def back_one(y, carry, c2=c2, c3=c3):
        rows = chunk(y, line)
        grad = m_sa * three(pair(b1, rows)) - masks[0:8, 0:256] * (c2 + c3 * three(za[rows, :]))
        grad = grad.reshape(line, 256)
        set_pair(b1, rows, grad)
        set_pair(b2, rows, grad)
        cs[rows, 512:768] = grad.astype(BF)
        return carry

    loop(side, back_one)
    point("c")
    halo = send_halo(2, b2, b1)
    point("d")
    for top, values in ((6, (cross_fa, cross_fb, cross_fc)), (14, (total_fa, total_fb, total_fc))):
        turned = pltpu.roll(values[2], 64, 1)
        left = jnp.where(lane < 32, values[0], jnp.where(lane < 64, values[1], turned))
        norm_loc[top : top + 1, 0:128] = left[0:1]
        norm_loc[top : top + 1, 128:256] = jnp.where(lane < 64, turned, 0.0)[0:1]
    share_norms()

    h_t[...] = cs[:, 512:768].T
    for block in range(4):
        cols = slice(256 * block, 256 * (block + 1))
        rows = slice(REDUCE_1 + 256 * block, REDUCE_1 + 256 * (block + 1))
        gbuf[rows, :] = dot(h_t[...], xs[:, cols]).astype(BF)
    wide = dot(h_t[...], fp[:, 0:384]).astype(BF)
    gbuf[LATERAL_2 : LATERAL_2 + 256, :] = wide[:, 0:256]
    gbuf[LATERAL_2 + 256 : LATERAL_2 + 384, 0:128] = wide[0:128, 256:384]
    gbuf[LATERAL_2 + 256 : LATERAL_2 + 384, 128:256] = wide[128:256, 256:384]
    launch(LATERAL_2 + 384)
    point("e")

    halo_wait(x_halo)

    def edge_rows(ref, rows, link):
        value = ref[rows, :] * link
        fill_rows = jnp.zeros((padded - pixels, 128), F32)
        return jnp.concatenate([value, fill_rows], axis=0).astype(BF)

    def neighbours(first_link):
        def step(y, carry):
            rows = chunk(y, line)
            back = links[first_link : first_link + 8, :]
            ahead = links[first_link + 8 : first_link + 16, :]
            up = ahead * pltpu.roll(three(pair(b1, rows)), frames - 1, 1)
            down = back * pltpu.roll(three(pair(b2, rows)), 1, 1)
            cs[rows, 0:256] = up.reshape(line, 256).astype(BF)
            cs[rows, 256:512] = down.reshape(line, 256).astype(BF)
            cross = three(zfb[rows, :])
            moved = jnp.where(
                lane < 64,
                ahead[:, :128] * pltpu.roll(cross, frames - 1, 1),
                back[:, :128] * pltpu.roll(cross, 1, 1),
            )
            moved = jnp.where((lane < 32) | (lane >= 96), moved, 0.0)
            dzf[rows, 128:256] = moved.reshape(line, 128).astype(BF)
            return carry

        loop(side, step)

    neighbours(16)
    link_back, link_ahead = links[0:1, 0:128], links[8 + frames - 1 : 8 + frames, 0:128]
    wide = dot_tn(dzf[:, 0:256], fp[...])
    parts = [zeros(32, 128) for _ in range(3)]
    for tap in range(3):
        for q in range(4):
            other = q + tap - 1
            if 0 <= other < 4:
                parts[tap] = parts[tap] + wide[
                    32 * q : 32 * q + 32, 128 * other : 128 * other + 128
                ]
    parts[0] = parts[0] + wide[128:160, 384:512]
    parts[2] = parts[2] + wide[224:256, 0:128]
    wide = dot_tn(edge_rows(zfb, heads, link_back), xh_in[0, 4 * padded :, 128:256])
    parts[0] = parts[0] + wide[0:32]
    wide = dot_tn(edge_rows(zfb, ends_, link_ahead), xh_in[1, 4 * padded :, 0:128])
    parts[2] = parts[2] + wide[96:128]
    gbuf[TINY : TINY + 32, 0:128] = parts[0].astype(BF)
    gbuf[TINY : TINY + 32, 128:256] = parts[1].astype(BF)
    gbuf[TINY + 32 : TINY + 64, 0:128] = parts[2].astype(BF)
    point("f")

    for way, (side_lanes, low_row, rows_, link) in enumerate(
        ((0, REDUCE_0, heads, link_back), (256, REDUCE_2, ends_, link_ahead))
    ):
        h_t[...] = cs[:, side_lanes : side_lanes + 256].T
        edge = [edge_rows(b1.at[part], rows_, link) for part in range(2)]
        edge = jnp.concatenate(edge, axis=1).T
        for block in range(4):
            cols = slice(256 * block, 256 * (block + 1))
            rows = slice(low_row + 256 * block, low_row + 256 * (block + 1))
            total = dot(h_t[...], xs[:, cols]) + dot(edge, xh_in[way, padded * block : padded * (block + 1), :])
            gbuf[rows, :] = total.astype(BF)
        if way == 0:
            total = dot(h_t[...], fp[:, 256:512]) + dot(edge, xh_in[0, 4 * padded :, :])
            gbuf[LATERAL_0 : LATERAL_0 + 256, :] = total.astype(BF)
            launch(REDUCE_2)
            point("g")
    launch(gbuf.shape[0])
    point("h")

    def input_grad_mid(number, carry):
        rows = chunk(number, half)
        total = ds[rows, :].astype(F32) + dot_nt(cs[rows, 512:768], wr[1])
        ds[rows, :] = total.astype(BF)
        return carry

    loop(2, input_grad_mid)
    point("i")
    take_halo(halo, 2, b2, b1)
    from_before, from_after = take_fast_halo(fast_halo, 2, (96, 0))
    zfb[ends_, :] = jnp.where(low, zfb[ends_, :], from_before)
    zfb[heads, :] = jnp.where(low, from_after, zfb[heads, :])
    neighbours(0)
    point("j")

    def input_grad(number, carry):
        rows = chunk(number, 2 * line)
        total = dot_nt(cs[rows, 0:256], wr[0])
        total = total + dot_nt(cs[rows, 256:512], wr[2])
        ds[rows, :] = (ds[rows, :].astype(F32) + total).astype(BF)
        return carry

    def input_grad_fast(number, carry):
        size = 2 * line
        rows = chunk(number, size)
        total = dot(dzf[rows, 0:256], bt[...])
        mid = dot_nt(cs[rows, 512:768], wl[256:640, :])
        up = dot_nt(cs[rows, 0:256], wl[0:256, :])
        total = total + jnp.concatenate([mid, zeros(size, 128)], axis=1)
        total = total + jnp.concatenate([zeros(size, 256), up], axis=1)
        unpacked(df, number, size, total, True)
        return carry

    parts_ = side // 2
    lax.fori_loop(0, parts_ // 2, input_grad_fast, 0)
    point("k")
    lax.fori_loop(parts_ // 2, parts_, input_grad_fast, 0)
    save_fast.wait()

    def narrow(y, carry):
        rows = chunk(y, fast_line)
        cf[rows, :] = df[rows, :].astype(BF)
        return carry

    loop(side, narrow)
    save_df = pltpu.make_async_copy(cf, fast_grad, store.at[3])
    save_df.start()
    point("l")
    lax.fori_loop(0, parts_ // 2, input_grad, 0)
    point("m")
    lax.fori_loop(parts_ // 2, parts_, input_grad, 0)
    save_ds = pltpu.make_async_copy(ds, slow_grad, store.at[4])
    save_ds.start()
    point("n")

    part = n_in.at[0 : n_dp - 1]
    pltpu.make_async_remote_copy(
        src_ref=part,
        dst_ref=part,
        send_sem=n_send.at[0],
        recv_sem=n_recv.at[0],
        device_id=dp_peers[0],
        device_id_type=MESH,
    ).wait()
    total = n_in[0]
    for slot in range(1, n_dp):
        total = total + n_in[slot]
    norm_loc[...] = total
    save_norm = pltpu.make_async_copy(norm_loc, norm_out, store.at[5])
    save_norm.start()
    while any(live.values()):
        point("z")
    save_norm.wait()
    for each in saves:
        each.wait()
    save_df.wait()
    save_ds.wait()


def spatial_stage(ref, tap):
    if tap == 8:
        return ref.at[0:256, 768:1024]
    top = 1024 + 256 * (tap // 4)
    return ref.at[top : top + 256, 256 * (tap % 4) : 256 * (tap % 4) + 256]


def lateral_stage(ref, tap):
    return ref.at[256 + 128 * tap : 384 + 128 * tap, 768:1024]


def block_call(mesh, frames, side, rows, operands):
    n_dp, n_group = mesh.shape["dp"], mesh.shape["group"]
    pixels = side * side
    n = pixels * frames
    line = side * frames
    dma = pltpu.SemaphoreType.DMA
    vmem = pltpu.VMEM
    shape = jax.ShapeDtypeStruct
    peers = n_group - 1
    pieces, depth = pieces_of(n_dp), n_dp // 2
    sums_scratch = []
    for place, (_, size) in enumerate(pieces):
        sizes = stage_sizes(place, size, depth)
        sums_scratch += [vmem((2, count, each, 256), BF) for each, count in sizes]
        sums_scratch += [dma((1,)), dma((8,))]
    return pl.pallas_call(
        partial(block_kernel, n_dp, n_group, frames, side, pieces),
        out_shape=(
            shape((n, 1024), BF),
            shape((4 * n, 128), BF),
            shape((n, 1024), BF),
            shape((4 * n, 128), BF),
            shape((rows, 256), BF),
            shape((16, 256), F32),
        ),
        in_specs=[ANYWHERE] * 4 + [SCALARS] * 2 + [ANYWHERE] * 8,
        out_specs=(ANYWHERE,) * 6,
        scratch_shapes=[
            vmem((n, 1024), BF),
            vmem((n, 1024), BF),
            vmem((4 * n, 128), BF),
            vmem((4 * n, 128), BF),
            vmem((n, 512), BF),
            vmem((4 * n, 128), F32),
            vmem((4 * n, 128), F32),
            vmem((n, 1024), BF),
            vmem((n, 1024), F32),
            vmem((n, 256), F32),
            vmem((n, 256), F32),
            vmem((2, n, 128), F32),
            vmem((2, n, 128), F32),
            vmem((side + 2, line, 768), BF),
            vmem((side + 2, line, 384), BF),
            vmem((n, 256), BF),
            vmem((n, 128), BF),
            vmem((n, 128), F32),
            vmem((n, 128), F32),
            vmem((n, 128), F32),
            vmem((n, 512), BF),
            vmem((256, n), BF),
            vmem((3, 1024, 256), BF),
            vmem((9 * 256, 256), BF),
            vmem((256, 1024), BF),
            vmem((640, 256), BF),
            vmem((256, 512), BF),
            vmem((9, 128, 128), BF),
            vmem((3, 384, 128), BF),
            vmem((128, 512), BF),
            vmem((rows, 256), BF),
            vmem((8, 1024), F32),
            vmem((32, 256), F32),
            vmem((32, 128), F32),
            vmem((2, 5 * (-(-pixels // 16) * 16), 256), BF),
            vmem((4, 2, -(-pixels // 16) * 16, 128), BF),
            vmem((4, 2, -(-pixels // 16) * 16, 128), BF),
            vmem((4, -(-pixels // 64) * 16, 128), BF),
            vmem((4, -(-pixels // 64) * 16, 128), BF),
            vmem((4, n_group, 8, 256), F32),
            vmem((2, n_group, 8, 1024), F32),
            vmem((6, n_group, 8, 128), F32),
            dma((LOADS,)),
            dma((6,)),
            dma((3, 4)),
            dma((3, 4)),
            dma((1,)),
            dma((4,)),
            dma((2,)),
            dma((1,)),
            dma((6,)),
            vmem((rows, 256), BF),
            vmem((16, 256), F32),
            vmem((n_dp, 16, 256), F32),
            dma((1,)),
            dma((1,)),
            dma((len(pieces),)),
        ]
        + [vmem(each.shape, F32) for each in operands[10:14]]
        + sums_scratch,
        compiler_params=pltpu.CompilerParams(
            collective_id=0, has_side_effects=True, vmem_limit_bytes=VMEM_LIMIT
        ),
        name="bottleneck",
    )(*operands)


def body(mesh, slow_in, fast_in, slow_cotangent, fast_cotangent, clip_start, clip_end, *rest):
    weights, moments_old, norms = rest[:7], rest[7:14], rest[14:]
    frames, side, slow_width = slow_in.shape[1], slow_in.shape[2], slow_in.shape[4]
    fast_frames, fast_width = fast_in.shape[1], fast_in.shape[4]
    rows = rows_total(mesh.shape["dp"])

    def flat(array):
        return jnp.transpose(array[0], (1, 2, 0, 3)).reshape(-1, array.shape[4])

    def unflat(array, count):
        grid = array.reshape(side, side, count, array.shape[1])
        return jnp.transpose(grid, (2, 0, 1, 3))[None]

    def turn(arrays):
        return arrays[:4] + (jnp.swapaxes(arrays[4], 1, 2),) + arrays[5:]

    turned = turn(weights)
    *kept, grads, norm_grad = block_call(
        mesh,
        frames,
        side,
        rows,
        (
            flat(slow_in),
            flat(fast_in),
            flat(slow_cotangent),
            flat(fast_cotangent),
            clip_start,
            clip_end,
            *turned,
            norms[0],
        ),
    )
    weights_new, moments_new, kept, norms_new = muon(
        grads, norm_grad, norms, turned, turn(moments_old), kept
    )
    slow_out, fast_out, slow_grad, fast_grad = kept
    weights_new, moments_new = turn(tuple(weights_new)), turn(tuple(moments_new))
    params_new, first_new, second_new = norms_new
    return (
        unflat(slow_out, frames),
        unflat(fast_out, fast_frames),
        unflat(slow_grad, frames),
        unflat(fast_grad, fast_frames),
        *weights_new,
        *moments_new,
        first_new,
        second_new,
        params_new,
    )


def solution(mesh):
    sharded = P("group", "dp", None, None, None)
    return jax.shard_map(
        partial(body, mesh),
        mesh=mesh,
        in_specs=(sharded,) * 4 + (P("group", None),) * 2 + (P(),) * 17,
        out_specs=(sharded,) * 4 + (P(),) * 17,
        check_vma=False,
    )
```
